32 devices in a mesh: req: 4 (over y, core), exp: 8 (over z, x).
Axes of the slice: x: 2, y: 2, z: 4, core: 2. Of those that a mesh axis runs over, the one named last changes fastest.
Arguments:
- stream_in: bfloat16 [4096, 2048], P(('req', 'exp')), may hold values from -3 to 3
- queries: bfloat16 [4096, 2048], P('req', 'exp'), may hold values from -9 to 9
- keys: bfloat16 [4096, 2048], P('req', 'exp'), may hold values from -7 to 7
- values: bfloat16 [4096, 2048], P('req', 'exp'), may hold values from -6 to 6
- out_weight: bfloat16 [2048, 2048], P('exp'), may hold values from -0.29882812 to 0.29882812
- norm_gain: float32 [2048], replicated, may hold values from 0.1 to 1.9
- w_gate: bfloat16 [128, 2048, 512], P(('req', 'exp')), may hold values from -0.125 to 0.125
- w_up: bfloat16 [128, 2048, 512], P(('req', 'exp')), may hold values from -0.125 to 0.125
- w_down: bfloat16 [128, 512, 2048], P(('req', 'exp')), may hold values from -0.1875 to 0.1875
- combine: float32 [4096, 8], P(('req', 'exp')), may hold values from 0.05 to 0.6
- segment_ids: int32 [4, 1024], P('req'), may hold values from 0 to 7, never falling along the last dimension, each value on 1 to 512 neighbouring positions
- routes: int32 [4096, 8], P(('req', 'exp')), may hold values from 0 to 63, all different within a row; in each aligned block of 128 rows (0 to 127, 128 to 255, ...) at most 20 rows name the same one
- page_table: int32 [256], replicated, may hold values from 0 to 255, as said below
Outputs:
- layer_out: bfloat16 [4096, 2048], P(('req', 'exp'))
- kv_cache: bfloat16 [256, 2, 16, 2048], P('req', None, None, 'exp')
The draws below stay inside these ranges and needn't reach their ends.
Inputs may be any that keep to these rules, and one draw needn't show every extreme that they name: `segment_ids`: ids never fall along a row; every request has at most 512 tokens and one has exactly that many. `routes`: the 8 experts of a token differ; among the 128 tokens of one device each expert is named at most 20 times. `page_table`: a permutation of the pages; the 64 logical pages of each row of requests go in equal numbers to the physical pages of every row, row q holding pages q * 64 to (q + 1) * 64 - 1.
All inputs are finite; a program needn't handle non-finite values.
Results may differ from the reference program's by a relative error of at most 0.0062.
Values may be sent and summed in bfloat16 or wider, within the bound.
No kernel may reach another device: no remote copies, remote signals or barrier semaphores. Data moves between devices by JAX's collectives and lax.ppermute only.
A program may use at most 128 MiB of HBM per device.

```python
import math
import jax
import jax.numpy as jnp
import numpy as np
from jax import lax

D = 2048
H = 16
HD = 128
EXPERTS = 64
FF = 1024
TOPK = 8
TOK_DEV = 128
SEGS = 8
PAGE = 16
TOK_REQ = 1024
TOKENS = 4096
LEN_MAX = 512
MOST = 20
HALVES = 128
PAGES_REQ = 64
PAGES = 256
N_REQ = 4
N_EXP = 8


def query_key_pair(key):
    shape = (TOKENS, H * HD)
    queries_f = jnp.clip(1.2 * jax.random.normal(jax.random.fold_in(key, 11), shape, jnp.float32), -7.0, 7.0)
    keys_f = jnp.clip(1.2 * jax.random.normal(jax.random.fold_in(key, 12), shape, jnp.float32), -7.0, 7.0)
    return (queries_f, keys_f)


def draw_queries(key, part):
    return query_key_pair(key)[0].astype(jnp.bfloat16)


def draw_keys(key, part):
    return query_key_pair(key)[1].astype(jnp.bfloat16)


def draw_page_table(key, part):
    groups = PAGES // PAGES_REQ
    per_group = PAGES_REQ // groups
    source_keys = jax.random.split(jax.random.fold_in(key, 21), groups)
    target_keys = jax.random.split(jax.random.fold_in(key, 22), groups)
    source_order = jax.vmap(lambda subkey: jax.random.permutation(subkey, PAGES_REQ))(source_keys)
    target_order = jax.vmap(lambda subkey: jax.random.permutation(subkey, PAGES_REQ))(target_keys)
    target_group = source_order % groups
    within = source_order // groups
    source_index = jnp.arange(groups)[:, None]
    slot_index = target_order[target_group, source_index * per_group + within]
    return (target_group * PAGES_REQ + slot_index).reshape(-1).astype(jnp.int32)


def block_scale(own_key, extent, cuts, smallest, high):
    level = 1.0
    for dim, parts in cuts:
        heights = jax.random.uniform(jax.random.fold_in(jax.random.fold_in(own_key, 6), dim), (parts,), jnp.float32, smallest / len(cuts), high / len(cuts))
        level = level * jnp.repeat(jnp.exp(heights), extent[dim] // parts).reshape((-1,) + (1,) * (len(extent) - 1 - dim))
    return level


def split_up(amount, total, most, lean):
    weights = [(1 << 20) // math.isqrt(grade ** lean) + 1 for grade in range(2, amount + 1)]
    spare, counts = total - most - (amount - 1), [1] * (amount - 1)
    while spare > 0:
        movable = [i for i in range(amount - 1) if counts[i] < most]
        pool, left = sum([weights[i] for i in movable]), spare
        for i in movable:
            extra = min(most - counts[i], max(1, left * weights[i] // pool), spare)
            counts[i] = counts[i] + extra
            spare = spare - extra
    return np.array([most] + counts)


def uneven(key, count, total, bound, lean):
    if count == 2:
        one = jax.random.randint(key, (), max(1, total - bound), min(bound, total - 1) + 1)
        return jnp.stack([one, total - one])
    tallies = jnp.asarray(split_up(count, total, bound, lean), jnp.int32)
    twos = (count - 1) // 2
    giver, sink = tallies[1:1 + 2 * twos:2], tallies[2:2 + 2 * twos:2]
    room = jnp.minimum(giver - 1, bound - sink)
    moved = jax.random.randint(jax.random.fold_in(key, 1), (twos,), 0, 1 << 20) % (room + 1)
    tallies = tallies.at[1:1 + 2 * twos:2].set(giver - moved).at[2:2 + 2 * twos:2].set(sink + moved)
    return tallies[jax.random.permutation(jax.random.fold_in(key, 2), count)]


def shared_out(key, own, number, rows, number_of, top, bound, slope):
    order = jax.random.permutation(key, number_of)
    heavy_load, common = portions_of(number_of, rows * top, bound, slope, True), portions_of(number_of, rows * top, bound, slope, False)
    places = jnp.arange(number_of)

    def named(tallies, offset_by):
        used = int((tallies > 0).sum())
        fixed = max(1, used // 4)
        passed = fixed + (places - fixed + offset_by * (used - fixed)) % max(1, number_of - fixed)
        return jnp.zeros((number_of,), jnp.int32).at[order[jnp.where(places < fixed, places, passed)]].set(jnp.asarray(tallies, jnp.int32))

    tallies = jnp.where(number % 4 == 0, named(heavy_load, number // 4), named(common, number - number // 4 - 1))
    mixed = jax.random.permutation(jax.random.fold_in(own, 3), number_of)
    donor, receiver = mixed[0:number_of // 2 * 2:2], mixed[1:number_of // 2 * 2:2]
    margin = jnp.minimum(tallies[donor] - 1, bound - tallies[receiver]) // 2
    margin = jnp.where((donor == order[0]) | (receiver == order[0]) | (tallies[receiver] == 0), 0, jnp.maximum(margin, 0))
    passed = jax.random.randint(jax.random.fold_in(own, 4), (number_of // 2,), 0, 1 << 20) % (margin + 1)
    tallies = tallies.at[donor].add(-passed).at[receiver].add(passed)
    labels = jnp.searchsorted(jnp.cumsum(tallies), jnp.arange(rows * top), side="right").astype(jnp.int32)
    table = labels.reshape(top, rows).T
    table = table[jax.random.permutation(jax.random.fold_in(own, 1), rows)]
    offset_by = jax.random.randint(jax.random.fold_in(own, 2), (rows, 1), 0, top)
    return jnp.take_along_axis(table, (jnp.arange(top)[None, :] + offset_by) % top, axis=1)


def portions_of(number_of, total, limit, skew, full):
    loads = [(1 << 20) // math.isqrt(rank ** skew) + 1 for rank in range(1, number_of + 1)]
    largest = limit if full else min(limit, max(-(-total // number_of), total * loads[0] // sum(loads)))
    least = 1 if total - largest >= number_of - 1 else 0
    counts, surplus = [largest] + [least] * (number_of - 1), total - largest - least * (number_of - 1)
    while surplus > 0:
        free = [i for i in range(1, number_of) if counts[i] < largest] or [i for i in range(1, number_of) if counts[i] < limit]
        pool, budget = sum([loads[i] for i in free]), surplus
        for i in free:
            extra = min(limit - counts[i], max(1, budget * loads[i] // pool), surplus)
            counts[i] = counts[i] + extra
            surplus = surplus - extra
    return np.array(counts)


def centred(own_key, dims, width, reach, cuts=(), held_as=jnp.bfloat16):
    values = width * jax.random.normal(own_key, dims, jnp.float32)
    if cuts:
        values = values * block_scale(own_key, dims, cuts, -0.22, 0.18)
    return jnp.clip(values, -reach, reach).astype(held_as)


def setup_inputs(seed: int = 0) -> dict:
    streams_of = jax.random.split(jax.random.key(seed), 14)
    stream_in = centred(streams_of[0], (TOKENS, D), 0.5, 3.0, ((0, 32),))
    queries = draw_queries(jax.random.fold_in(streams_of[13], 71), 0)
    keys = draw_keys(jax.random.fold_in(streams_of[13], 71), 0)
    values = centred(streams_of[3], (TOKENS, H * HD), 1.0, 6.0, ((0, 4), (1, 8)))
    out_weight = centred(streams_of[4], (H * HD, D), 0.05, 0.29882812, ((0, 8),))
    norm_gain = jnp.clip(1.0 + 0.18 * jax.random.normal(streams_of[5], (D,), jnp.float32), 0.1, 1.9)
    w_gate = centred(streams_of[6], (HALVES, D, FF // 2), D ** -0.5, 0.125, ((0, 32),))
    w_up = centred(streams_of[7], (HALVES, D, FF // 2), D ** -0.5, 0.125, ((0, 32),))
    w_down = centred(streams_of[8], (HALVES, FF // 2, D), FF ** -0.5, 0.1875, ((0, 32),))
    combine = jnp.clip(jnp.exp(math.log(0.6) - 2.4849067 * jax.random.uniform(streams_of[9], (TOKENS, TOPK), jnp.float32) ** block_scale(streams_of[9], (TOKENS, TOPK), ((0, 32),), -0.2, 0.2)), 0.05, 0.6)
    segment_ids = jax.vmap(lambda own: jnp.searchsorted(jnp.cumsum(uneven(own, SEGS, TOK_REQ, LEN_MAX, 2)), jnp.arange(TOK_REQ), side="right"))(jax.random.split(streams_of[10], N_REQ)).reshape((N_REQ, TOK_REQ)).astype(jnp.int32)
    routes_keys = jax.random.split(jax.random.fold_in(streams_of[11], 1), TOKENS // TOK_DEV)
    routes_turns = jax.random.permutation(jax.random.fold_in(streams_of[11], 3), TOKENS // TOK_DEV)
    routes = jax.vmap(lambda own, number: shared_out(jax.random.fold_in(streams_of[11], 2), own, number, TOK_DEV, EXPERTS, TOPK, MOST, 2))(routes_keys, routes_turns).reshape((TOKENS, TOPK))
    page_table = draw_page_table(jax.random.fold_in(streams_of[13], 71), 0)
    return {"stream_in": stream_in, "queries": queries, "keys": keys, "values": values, "out_weight": out_weight, "norm_gain": norm_gain, "w_gate": w_gate, "w_up": w_up, "w_down": w_down, "combine": combine, "segment_ids": segment_ids, "routes": routes, "page_table": page_table}


def attend_group(query_rows, key_rows, value_rows, segments):
    scaling = 1.0 / math.sqrt(HD)
    scores = jnp.dot(query_rows, key_rows.T, preferred_element_type=jnp.float32) * scaling
    allowed = segments[:, None] == segments[None, :]
    scores = jnp.where(allowed, scores, jnp.float32(-1e+30))
    highest = lax.optimization_barrier(jnp.max(scores, axis=1, keepdims=True))
    weights_exp = jnp.exp(scores - highest)
    totals = lax.optimization_barrier(jnp.sum(weights_exp, axis=1, keepdims=True))
    mixed = jnp.dot(weights_exp.astype(jnp.bfloat16), value_rows, preferred_element_type=jnp.float32) / totals
    return mixed.astype(jnp.bfloat16)

def by_head(tensor_in):
    return tensor_in.reshape(N_REQ, TOK_REQ, H, HD).transpose(0, 2, 1, 3).reshape(N_REQ * H, TOK_REQ, HD)

def reference(stream_in, queries, keys, values, out_weight, norm_gain, w_gate, w_up, w_down, combine, segment_ids, routes, page_table):
    segment_rows = jnp.repeat(segment_ids, H, axis=0)
    attended = lax.map(lambda group: attend_group(*group), (by_head(queries), by_head(keys), by_head(values), segment_rows))
    attended = attended.reshape(N_REQ, H, TOK_REQ, HD).transpose(0, 2, 1, 3).reshape(TOKENS, H * HD)
    projected = jnp.dot(attended, out_weight, preferred_element_type=jnp.float32)
    residual = stream_in.astype(jnp.float32) + projected
    scale_rows = lax.rsqrt(lax.optimization_barrier(jnp.mean(residual * residual, axis=1, keepdims=True)) + 1e-06)
    normed = (residual * scale_rows * norm_gain).astype(jnp.bfloat16)
    capacity = N_REQ * N_EXP * MOST
    expert_ids = routes.reshape(-1).astype(jnp.int32)
    pair_tokens = (jnp.arange(TOKENS * TOPK) // TOPK).astype(jnp.int32)
    owners = (expert_ids[:, None] == jnp.arange(EXPERTS, dtype=jnp.int32)[None, :]).astype(jnp.int32)
    ranking = (lax.optimization_barrier(jnp.sum(jnp.cumsum(owners, axis=0) * owners, axis=1)) - 1).astype(jnp.int32)
    table = jnp.full((EXPERTS, capacity), TOKENS, jnp.int32).at[expert_ids, ranking].set(pair_tokens)
    pair_weights = jnp.zeros((EXPERTS, capacity), jnp.float32).at[expert_ids, ranking].set(combine.reshape(-1))
    padded = jnp.concatenate([normed, jnp.zeros((1, D), jnp.bfloat16)], axis=0)
    gates = w_gate.reshape(EXPERTS, 2, D, FF // 2)
    ups = w_up.reshape(EXPERTS, 2, D, FF // 2)
    downs = w_down.reshape(EXPERTS, 2, FF // 2, D)

    def one_expert(running, pieces):
        rows_index, row_weights, gate_pair, up_pair, down_pair = pieces
        rows = padded[rows_index]
        summed = jnp.zeros((capacity, D), jnp.float32)
        for half_index in range(2):
            gate_val = jnp.dot(rows, gate_pair[half_index], preferred_element_type=jnp.float32)
            up_val = jnp.dot(rows, up_pair[half_index], preferred_element_type=jnp.float32)
            activated = (jax.nn.silu(gate_val) * up_val).astype(jnp.bfloat16)
            half_out = jnp.dot(activated, down_pair[half_index], preferred_element_type=jnp.float32).astype(jnp.bfloat16)
            half_out = lax.optimization_barrier(half_out)
            summed = summed + half_out.astype(jnp.float32)
        return (running.at[rows_index].add(summed * row_weights[:, None]), jnp.zeros((), jnp.float32))
    expert_sum = lax.scan(one_expert, jnp.zeros((TOKENS + 1, D), jnp.float32), (table, pair_weights, gates, ups, downs))[0]
    layer_out = (residual + expert_sum[:TOKENS]).astype(jnp.bfloat16)
    pages = jnp.stack([keys.reshape(PAGES, PAGE, H * HD), values.reshape(PAGES, PAGE, H * HD)], axis=1)
    kv_cache = jnp.zeros_like(pages).at[page_table].set(pages)
    return (layer_out, kv_cache)
```

```python
import math

import jax
import jax.numpy as jnp
import numpy as np
from jax import lax
from jax.experimental import pallas as pl
from jax.experimental.pallas import tpu as pltpu
from jax.sharding import Mesh
from jax.sharding import PartitionSpec as P

D = 2048
HD = 128
EXPERTS = 64
TOPK = 8
PAGE = 16
MOST = 20


def from_partner(block, axis, distance):
    count = lax.axis_size(axis)
    route = []
    for low in range(count):
        high = low | 1 << distance
        if high != low and high < count:
            route += [(low, high), (high, low)]
    return lax.ppermute(block, axis, route)


def attend_rows(queries, keys, values, segments):
    length = queries.shape[0]
    head_count = queries.shape[1] // HD
    query_heads = queries.reshape(length, head_count, HD)
    key_heads = keys.reshape(length, head_count, HD)
    value_heads = values.reshape(length, head_count, HD)
    scaling = 1.0 / math.sqrt(HD)
    rows_block = min(512, length)

    def attend_block(position):
        start = position * rows_block
        query_block = lax.dynamic_slice_in_dim(query_heads, start, rows_block, 0)
        segment_block = lax.dynamic_slice_in_dim(segments, start, rows_block, 0)
        scores = (
            jnp.einsum("qhd,khd->hqk", query_block, key_heads, preferred_element_type=jnp.float32)
            * scaling
        )
        allowed = (segment_block[:, None] == segments[None, :])[None, :, :]
        scores = jnp.where(allowed, scores, jnp.float32(-1e30))
        highest = jnp.max(scores, axis=2, keepdims=True)
        weights_exp = jnp.exp(scores - highest)
        totals = jnp.sum(weights_exp, axis=2)
        mixed = jnp.einsum(
            "hqk,khd->qhd",
            weights_exp.astype(jnp.bfloat16),
            value_heads,
            preferred_element_type=jnp.float32,
        )
        mixed = mixed / jnp.transpose(totals)[:, :, None]
        return mixed.astype(jnp.bfloat16)

    blocks = lax.map(attend_block, jnp.arange(length // rows_block))
    return blocks.reshape(length, head_count * HD)


def write_pages(keys, values, page_table):
    page_rows = keys.shape[0] // PAGE
    groups = lax.axis_size("req")
    per_group = page_rows // groups
    width = keys.shape[1]
    pages = jnp.stack(
        [keys.reshape(page_rows, PAGE, width), values.reshape(page_rows, PAGE, width)], axis=1
    )
    myself = lax.axis_index("req")
    whole_table = page_table.reshape(groups, page_rows)
    own_table = lax.dynamic_slice_in_dim(page_table, myself * page_rows, page_rows, 0)
    target = own_table // page_rows
    picked = (target[:, None] == jnp.arange(groups, dtype=jnp.int32)[None, :]).astype(jnp.int32)
    ranking = jnp.sum(jnp.cumsum(picked, axis=0) * picked, axis=1) - 1
    outgoing = jnp.zeros_like(pages).at[target * per_group + ranking].set(pages)
    incoming = lax.all_to_all(
        outgoing.reshape(groups, per_group, 2, PAGE, width),
        "req",
        split_axis=0,
        concat_axis=0,
        tiled=True,
    )
    arriving = whole_table // page_rows == myself
    arrival_rank = jnp.cumsum(arriving.astype(jnp.int32), axis=1) - 1
    placing = jnp.where(
        arriving, jnp.arange(groups, dtype=jnp.int32)[:, None] * per_group + arrival_rank, page_rows
    )
    slot_table = (
        jnp.zeros((page_rows + 1,), jnp.int32)
        .at[placing.reshape(-1)]
        .set((whole_table % page_rows).reshape(-1))
    )
    slot_table = slot_table[:page_rows]
    return jnp.zeros_like(pages).at[slot_table].set(incoming.reshape(page_rows, 2, PAGE, width))


def whole_experts(w_gate, w_up, w_down):
    local_halves = w_gate.shape[0]
    half_units = w_gate.shape[2]
    if local_halves == 1:
        packed = jnp.stack([w_gate[0], w_up[0], w_down[0].reshape(D, half_units)])
        partner = from_partner(packed, "exp", 0)
        leading = lax.axis_index("exp") % 2 == 0
        first = jnp.where(leading, packed, partner)
        second = jnp.where(leading, partner, packed)
        gate_full = jnp.stack([first[0], second[0]])[None]
        up_full = jnp.stack([first[1], second[1]])[None]
        down_full = jnp.stack([first[2].reshape(half_units, D), second[2].reshape(half_units, D)])[
            None
        ]
        return (gate_full, up_full, down_full, 1)
    gate_full = w_gate.reshape(local_halves // 2, 2, D, half_units)
    up_full = w_up.reshape(local_halves // 2, 2, D, half_units)
    down_full = w_down.reshape(local_halves // 2, 2, half_units, D)
    return (gate_full, up_full, down_full, 2)


def on_device_split(
    stream_in,
    queries,
    keys,
    values,
    out_weight,
    norm_gain,
    w_gate,
    w_up,
    w_down,
    combine,
    segment_ids,
    routes,
    page_table,
):
    attended = attend_rows(queries, keys, values, segment_ids[0])
    kv_cache = write_pages(keys, values, page_table)
    tok_rows = stream_in.shape[0]
    projected = lax.psum_scatter(
        jnp.dot(attended, out_weight, preferred_element_type=jnp.float32),
        "exp",
        scatter_dimension=0,
        tiled=True,
    )
    residual = stream_in.astype(jnp.float32) + projected
    scale_rows = lax.rsqrt(jnp.mean(residual * residual, axis=1, keepdims=True) + 1e-06)
    normed = (residual * scale_rows * norm_gain).astype(jnp.bfloat16)
    expert_ids = routes.reshape(-1)
    owners = (expert_ids[:, None] == jnp.arange(EXPERTS, dtype=jnp.int32)[None, :]).astype(
        jnp.int32
    )
    ranking = jnp.sum(jnp.cumsum(owners, axis=0) * owners, axis=1) - 1
    pair_rows = jnp.repeat(normed, TOPK, axis=0)
    devices = lax.axis_size(("req", "exp"))
    local_halves = w_gate.shape[0]
    slots = (MOST + 1) // 2
    holder = 2 * expert_ids + ranking % 2
    position = ranking // 2
    outgoing = jnp.zeros((devices * local_halves * slots, D), jnp.bfloat16)
    outgoing = outgoing.at[holder * slots + position].set(pair_rows)
    gate_full, up_full, down_full, copies = whole_experts(w_gate, w_up, w_down)
    local_experts = gate_full.shape[0]
    arrived = lax.all_to_all(
        outgoing.reshape(devices, local_halves, slots, D),
        ("req", "exp"),
        split_axis=0,
        concat_axis=0,
        tiled=True,
    )
    count = arrived.shape[2]
    grouped = arrived.reshape(devices, local_experts, copies, count, D)
    gate_val = jnp.einsum(
        "sercd,ejdf->serjcf", grouped, gate_full, preferred_element_type=jnp.float32
    )
    up_val = jnp.einsum("sercd,ejdf->serjcf", grouped, up_full, preferred_element_type=jnp.float32)
    activated = (jax.nn.silu(gate_val) * up_val).astype(jnp.bfloat16)
    halves_out = jnp.einsum(
        "serjcf,ejfd->serjcd", activated, down_full, preferred_element_type=jnp.float32
    ).astype(jnp.bfloat16)
    returned = lax.all_to_all(
        halves_out.reshape(devices, local_halves, 2, count, D),
        ("req", "exp"),
        split_axis=0,
        concat_axis=0,
        tiled=True,
    )
    flat_back = returned.reshape(devices * local_halves, 2, slots, D)
    combined = flat_back[holder, 0, position].astype(jnp.float32) + flat_back[
        holder, 1, position
    ].astype(jnp.float32)
    weighted = combined * combine.reshape(-1)[:, None]
    expert_sum = jnp.sum(weighted.reshape(tok_rows, TOPK, D), axis=1)
    layer_out = (residual + expert_sum).astype(jnp.bfloat16)
    return (layer_out, kv_cache)


PLANES = 4


def strictly_lower(size):
    return jnp.asarray(np.tril(np.ones((size, size), np.float32), -1), jnp.bfloat16)


def count_before(flags):
    return jnp.dot(
        strictly_lower(flags.shape[0]),
        flags.astype(jnp.bfloat16),
        preferred_element_type=jnp.float32,
    )


def move_pages(keys, values, page_table):
    rows = keys.shape[0]
    width = keys.shape[1]
    page_rows = rows // PAGE
    groups = lax.axis_size("req")
    per_group = page_rows // groups
    myself = lax.axis_index("req")
    whole_table = page_table.reshape(groups, page_rows)
    own_table = lax.dynamic_slice_in_dim(page_table, myself * page_rows, page_rows, 0)
    target = own_table // page_rows
    picked = target[:, None] == jnp.arange(groups, dtype=jnp.int32)[None, :]
    ranking = jnp.sum(jnp.where(picked, count_before(picked), 0.0), axis=1).astype(jnp.int32)
    slot = target * per_group + ranking
    within = jnp.arange(PAGE, dtype=jnp.int32)
    lines = jnp.arange(rows, dtype=jnp.int32)
    target_line = (slot[:, None] * PAGE + within[None, :]).reshape(-1)
    spread = (target_line[None, :] == lines[:, None]).astype(jnp.bfloat16)
    sent = [
        jnp.dot(spread, block, preferred_element_type=jnp.float32)
        .astype(jnp.bfloat16)
        .reshape(groups, rows // groups, width)
        for block in (keys, values)
    ]
    incoming = lax.all_to_all(
        jnp.stack(sent, axis=1), "req", split_axis=0, concat_axis=0, tiled=True
    )
    arriving = whole_table // page_rows == myself
    arrival = count_before(arriving.T).T.astype(jnp.int32)
    source = jnp.arange(groups, dtype=jnp.int32)[:, None] * per_group + arrival
    landing = jnp.where(arriving, whole_table % page_rows, -1).reshape(-1)
    slots = jnp.arange(page_rows, dtype=jnp.int32)
    source_page = jnp.sum(
        jnp.where(landing[None, :] == slots[:, None], source.reshape(-1)[None, :], 0), axis=1
    )
    source_line = (source_page[:, None] * PAGE + within[None, :]).reshape(-1)
    collect = (source_line[:, None] == lines[None, :]).astype(jnp.bfloat16)
    placed = [
        jnp.dot(
            collect, incoming[:, part].reshape(rows, width), preferred_element_type=jnp.float32
        )
        .astype(jnp.bfloat16)
        .reshape(page_rows, PAGE, width)
        for part in range(2)
    ]
    return jnp.stack(placed, axis=1)


def project_rows(attended, out_weight):
    groups = lax.axis_size("req")
    members = lax.axis_size("z") * lax.axis_size("x")
    tok_rows = attended.shape[0] // members
    strip = out_weight.shape[1] // groups
    start = lax.axis_index("req") * strip
    piece = lax.dynamic_slice_in_dim(out_weight, start, strip, 1)
    strips = lax.all_gather(piece, ("req", "z", "x"), axis=0, tiled=True)
    strips = strips.reshape(groups, members * out_weight.shape[0], strip)
    shares = lax.all_to_all(
        attended.reshape(members, tok_rows, attended.shape[1]),
        ("z", "x"),
        split_axis=0,
        concat_axis=0,
        tiled=True,
    )
    whole_rows = jnp.transpose(shares, (1, 0, 2)).reshape(tok_rows, -1)
    return jnp.concatenate(
        [
            jnp.dot(whole_rows, strips[index], preferred_element_type=jnp.float32)
            for index in range(groups)
        ],
        axis=1,
    )


def expert_kernel(rows_ref, order_ref, back_ref, gate_ref, up_ref, down_ref, out_ref, sorted_rows, total, outs):
    step = pl.program_id(0)
    count = sorted_rows.shape[0] // 2

    @pl.when(step == 0)
    def _():
        sorted_rows[...] = jnp.dot(
            order_ref[...], rows_ref[...], preferred_element_type=jnp.float32
        ).astype(jnp.bfloat16)

    first = pl.multiple_of((step // 2) * count, 16)
    tokens = sorted_rows[pl.ds(first, count), :]
    gate_val = jnp.dot(tokens, gate_ref[0], preferred_element_type=jnp.float32)
    up_val = jnp.dot(tokens, up_ref[0], preferred_element_type=jnp.float32)
    activated = (gate_val / (1.0 + jnp.exp(-gate_val)) * up_val).astype(jnp.bfloat16)
    half_out = jnp.dot(activated, down_ref[0], preferred_element_type=jnp.float32)

    @pl.when(step % 2 == 0)
    def _():
        total[...] = half_out

    @pl.when(step % 2 == 1)
    def _():
        outs[pl.ds(first, count), :] = (total[...] + half_out).astype(jnp.bfloat16)

    @pl.when(step == 3)
    def _():
        out_ref[...] = jnp.dot(
            back_ref[...], outs[...], preferred_element_type=jnp.float32
        ).astype(jnp.bfloat16)


def run_experts(rows, sources, w_gate, w_up, w_down):
    height, depth = rows.shape
    units = w_gate.shape[2]
    slots = height // (sources * 2)
    index = np.arange(height)
    wanted = (
        index % (height // 2) // slots * (2 * slots)
        + index // (height // 2) * slots
        + index % slots
    )
    order = (wanted[:, None] == index[None, :]).astype(np.float32)
    fixed = lambda i: (0, 0)
    return pl.pallas_call(
        expert_kernel,
        grid=(4,),
        in_specs=[
            pl.BlockSpec((height, depth), fixed),
            pl.BlockSpec((height, height), fixed),
            pl.BlockSpec((height, height), fixed),
            pl.BlockSpec((1, depth, units), lambda i: (i, 0, 0)),
            pl.BlockSpec((1, depth, units), lambda i: (i, 0, 0)),
            pl.BlockSpec((1, units, depth), lambda i: (i, 0, 0)),
        ],
        out_specs=pl.BlockSpec((height, depth), fixed),
        out_shape=jax.ShapeDtypeStruct((height, depth), jnp.bfloat16),
        scratch_shapes=[
            pltpu.VMEM((height, depth), jnp.bfloat16),
            pltpu.VMEM((height // 2, depth), jnp.float32),
            pltpu.VMEM((height, depth), jnp.bfloat16),
        ],
        compiler_params=pltpu.CompilerParams(vmem_limit_bytes=40 * 1024 * 1024),
        cost_estimate=pl.CostEstimate(
            flops=12 * height * depth * units + 4 * height * height * depth,
            bytes_accessed=12 * depth * units * 2 + 4 * height * depth,
            transcendentals=2 * height * units,
        ),
    )(
        rows,
        jnp.asarray(order, jnp.bfloat16),
        jnp.asarray(order.T, jnp.bfloat16),
        w_gate,
        w_up,
        w_down,
    )


def on_device_whole(
    stream_in,
    queries,
    keys,
    values,
    out_weight,
    norm_gain,
    w_gate,
    w_up,
    w_down,
    combine,
    segment_ids,
    routes,
    page_table,
):
    tok_rows = stream_in.shape[0]
    groups = lax.axis_size("req")
    lanes = lax.axis_size("x")
    sources = groups * lanes
    plane_experts = 2 * sources
    height = plane_experts * MOST
    level = lax.axis_index("z")

    matched = routes[:, :, None] == jnp.arange(EXPERTS, dtype=jnp.int32)[None, None, :]
    named = jnp.any(matched, axis=1)
    weight_of = jnp.sum(jnp.where(matched, combine[:, :, None], 0.0), axis=1)
    place = jnp.arange(EXPERTS, dtype=jnp.int32)
    in_plane = place // (PLANES * 2 * lanes) * (2 * lanes) + place % (2 * lanes)
    slot_of = jnp.where(named, count_before(named) + (in_plane * MOST)[None, :], -1.0)
    tables = jnp.stack([slot_of.T, weight_of.T])
    tables = tables.reshape(2, groups, PLANES, 2 * lanes, tok_rows)
    tables = jnp.transpose(tables, (2, 0, 1, 3, 4)).reshape(PLANES, 2, plane_experts, tok_rows)
    tables = lax.all_to_all(tables, "z", split_axis=0, concat_axis=0, tiled=True)

    attended = attend_rows(queries, keys, values, segment_ids[0])
    residual = stream_in.astype(jnp.float32) + project_rows(attended, out_weight)
    scale_rows = lax.rsqrt(jnp.mean(residual * residual, axis=1, keepdims=True) + 1e-06)
    normed = (residual * scale_rows * norm_gain).astype(jnp.bfloat16)
    kv_cache = move_pages(keys, values, page_table)

    lines = jnp.arange(height, dtype=jnp.float32)
    total = residual
    for turn in range(PLANES):
        pairs = [(low, low ^ turn) for low in range(PLANES)]
        table = lax.dynamic_index_in_dim(tables, level ^ turn, 0, keepdims=False)
        hits = table[0][:, None, :] == lines[None, :, None]
        picking = jnp.sum(hits.astype(jnp.float32), axis=0).astype(jnp.bfloat16)
        mixing = jnp.sum(jnp.where(hits, table[1][:, None, :], 0.0), axis=0)
        mixing_high = mixing.astype(jnp.bfloat16)
        mixing_low = (mixing - mixing_high.astype(jnp.float32)).astype(jnp.bfloat16)
        block = normed if turn == 0 else lax.ppermute(normed, "z", pairs)
        packed = jnp.dot(picking, block, preferred_element_type=jnp.float32).astype(jnp.bfloat16)
        arrived = lax.all_to_all(
            packed.reshape(sources, 2 * MOST, D),
            ("req", "x"),
            split_axis=0,
            concat_axis=0,
            tiled=True,
        )
        outs = run_experts(arrived.reshape(height, D), sources, w_gate, w_up, w_down)
        returned = lax.all_to_all(
            outs.reshape(sources, 2 * MOST, D),
            ("req", "x"),
            split_axis=0,
            concat_axis=0,
            tiled=True,
        ).reshape(height, D)
        share = sum(
            lax.dot_general(
                part, returned, (((0,), (0,)), ((), ())), preferred_element_type=jnp.float32
            )
            for part in (mixing_high, mixing_low)
        )
        if turn:
            share = lax.ppermute(share.astype(jnp.bfloat16), "z", pairs).astype(jnp.float32)
        total = total + share
    return (total.astype(jnp.bfloat16), kv_cache)


def solution(mesh):
    requests, members = mesh.shape["req"], mesh.shape["exp"]
    whole = 2 * EXPERTS == 4 * requests * members
    if whole:
        grid = mesh.devices.reshape(requests, PLANES, members // PLANES)
        mesh = Mesh(grid, ("req", "z", "x"))
    exp = ("z", "x") if whole else "exp"
    every = ("req", "z", "x") if whole else ("req", "exp")
    return jax.shard_map(
        on_device_whole if whole else on_device_split,
        mesh=mesh,
        in_specs=(
            P(every, None),
            P("req", exp),
            P("req", exp),
            P("req", exp),
            P(exp, None),
            P(),
            P(every, None, None),
            P(every, None, None),
            P(every, None, None),
            P(every, None),
            P("req", None),
            P(every, None),
            P(),
        ),
        out_specs=(P(every, None), P("req", None, None, exp)),
        check_vma=False,
    )
```

```python
import functools
import math

import jax
import jax.numpy as jnp
import numpy as np
from jax import lax
from jax.experimental import pallas as pl
from jax.experimental.pallas import tpu as pltpu
from jax.sharding import Mesh
from jax.sharding import PartitionSpec as P

D = 2048
HD = 128
EXPERTS = 64
TOPK = 8
PAGE = 16
MOST = 20


def from_partner(block, axis, distance):
    count = lax.axis_size(axis)
    route = []
    for low in range(count):
        high = low | 1 << distance
        if high != low and high < count:
            route += [(low, high), (high, low)]
    return lax.ppermute(block, axis, route)


def attend_rows(queries, keys, values, segments):
    length = queries.shape[0]
    head_count = queries.shape[1] // HD
    query_heads = queries.reshape(length, head_count, HD)
    key_heads = keys.reshape(length, head_count, HD)
    value_heads = values.reshape(length, head_count, HD)
    scaling = 1.0 / math.sqrt(HD)
    rows_block = min(512, length)

    def attend_block(position):
        start = position * rows_block
        query_block = lax.dynamic_slice_in_dim(query_heads, start, rows_block, 0)
        segment_block = lax.dynamic_slice_in_dim(segments, start, rows_block, 0)
        scores = (
            jnp.einsum("qhd,khd->hqk", query_block, key_heads, preferred_element_type=jnp.float32)
            * scaling
        )
        allowed = (segment_block[:, None] == segments[None, :])[None, :, :]
        scores = jnp.where(allowed, scores, jnp.float32(-1e30))
        highest = jnp.max(scores, axis=2, keepdims=True)
        weights_exp = jnp.exp(scores - highest)
        totals = jnp.sum(weights_exp, axis=2)
        mixed = jnp.einsum(
            "hqk,khd->qhd",
            weights_exp.astype(jnp.bfloat16),
            value_heads,
            preferred_element_type=jnp.float32,
        )
        mixed = mixed / jnp.transpose(totals)[:, :, None]
        return mixed.astype(jnp.bfloat16)

    blocks = lax.map(attend_block, jnp.arange(length // rows_block))
    return blocks.reshape(length, head_count * HD)


def write_pages(keys, values, page_table):
    page_rows = keys.shape[0] // PAGE
    groups = lax.axis_size("req")
    per_group = page_rows // groups
    width = keys.shape[1]
    pages = jnp.stack(
        [keys.reshape(page_rows, PAGE, width), values.reshape(page_rows, PAGE, width)], axis=1
    )
    myself = lax.axis_index("req")
    whole_table = page_table.reshape(groups, page_rows)
    own_table = lax.dynamic_slice_in_dim(page_table, myself * page_rows, page_rows, 0)
    target = own_table // page_rows
    picked = (target[:, None] == jnp.arange(groups, dtype=jnp.int32)[None, :]).astype(jnp.int32)
    ranking = jnp.sum(jnp.cumsum(picked, axis=0) * picked, axis=1) - 1
    outgoing = jnp.zeros_like(pages).at[target * per_group + ranking].set(pages)
    incoming = lax.all_to_all(
        outgoing.reshape(groups, per_group, 2, PAGE, width),
        "req",
        split_axis=0,
        concat_axis=0,
        tiled=True,
    )
    arriving = whole_table // page_rows == myself
    arrival_rank = jnp.cumsum(arriving.astype(jnp.int32), axis=1) - 1
    placing = jnp.where(
        arriving, jnp.arange(groups, dtype=jnp.int32)[:, None] * per_group + arrival_rank, page_rows
    )
    slot_table = (
        jnp.zeros((page_rows + 1,), jnp.int32)
        .at[placing.reshape(-1)]
        .set((whole_table % page_rows).reshape(-1))
    )
    slot_table = slot_table[:page_rows]
    return jnp.zeros_like(pages).at[slot_table].set(incoming.reshape(page_rows, 2, PAGE, width))


def whole_experts(w_gate, w_up, w_down):
    local_halves = w_gate.shape[0]
    half_units = w_gate.shape[2]
    if local_halves == 1:
        packed = jnp.stack([w_gate[0], w_up[0], w_down[0].reshape(D, half_units)])
        partner = from_partner(packed, "exp", 0)
        leading = lax.axis_index("exp") % 2 == 0
        first = jnp.where(leading, packed, partner)
        second = jnp.where(leading, partner, packed)
        gate_full = jnp.stack([first[0], second[0]])[None]
        up_full = jnp.stack([first[1], second[1]])[None]
        down_full = jnp.stack([first[2].reshape(half_units, D), second[2].reshape(half_units, D)])[
            None
        ]
        return (gate_full, up_full, down_full, 1)
    gate_full = w_gate.reshape(local_halves // 2, 2, D, half_units)
    up_full = w_up.reshape(local_halves // 2, 2, D, half_units)
    down_full = w_down.reshape(local_halves // 2, 2, half_units, D)
    return (gate_full, up_full, down_full, 2)


def on_device_split(
    stream_in,
    queries,
    keys,
    values,
    out_weight,
    norm_gain,
    w_gate,
    w_up,
    w_down,
    combine,
    segment_ids,
    routes,
    page_table,
):
    attended = attend_rows(queries, keys, values, segment_ids[0])
    kv_cache = write_pages(keys, values, page_table)
    tok_rows = stream_in.shape[0]
    projected = lax.psum_scatter(
        jnp.dot(attended, out_weight, preferred_element_type=jnp.float32),
        "exp",
        scatter_dimension=0,
        tiled=True,
    )
    residual = stream_in.astype(jnp.float32) + projected
    scale_rows = lax.rsqrt(jnp.mean(residual * residual, axis=1, keepdims=True) + 1e-06)
    normed = (residual * scale_rows * norm_gain).astype(jnp.bfloat16)
    expert_ids = routes.reshape(-1)
    owners = (expert_ids[:, None] == jnp.arange(EXPERTS, dtype=jnp.int32)[None, :]).astype(
        jnp.int32
    )
    ranking = jnp.sum(jnp.cumsum(owners, axis=0) * owners, axis=1) - 1
    pair_rows = jnp.repeat(normed, TOPK, axis=0)
    devices = lax.axis_size(("req", "exp"))
    local_halves = w_gate.shape[0]
    slots = (MOST + 1) // 2
    holder = 2 * expert_ids + ranking % 2
    position = ranking // 2
    outgoing = jnp.zeros((devices * local_halves * slots, D), jnp.bfloat16)
    outgoing = outgoing.at[holder * slots + position].set(pair_rows)
    gate_full, up_full, down_full, copies = whole_experts(w_gate, w_up, w_down)
    local_experts = gate_full.shape[0]
    arrived = lax.all_to_all(
        outgoing.reshape(devices, local_halves, slots, D),
        ("req", "exp"),
        split_axis=0,
        concat_axis=0,
        tiled=True,
    )
    count = arrived.shape[2]
    grouped = arrived.reshape(devices, local_experts, copies, count, D)
    gate_val = jnp.einsum(
        "sercd,ejdf->serjcf", grouped, gate_full, preferred_element_type=jnp.float32
    )
    up_val = jnp.einsum("sercd,ejdf->serjcf", grouped, up_full, preferred_element_type=jnp.float32)
    activated = (jax.nn.silu(gate_val) * up_val).astype(jnp.bfloat16)
    halves_out = jnp.einsum(
        "serjcf,ejfd->serjcd", activated, down_full, preferred_element_type=jnp.float32
    ).astype(jnp.bfloat16)
    returned = lax.all_to_all(
        halves_out.reshape(devices, local_halves, 2, count, D),
        ("req", "exp"),
        split_axis=0,
        concat_axis=0,
        tiled=True,
    )
    flat_back = returned.reshape(devices * local_halves, 2, slots, D)
    combined = flat_back[holder, 0, position].astype(jnp.float32) + flat_back[
        holder, 1, position
    ].astype(jnp.float32)
    weighted = combined * combine.reshape(-1)[:, None]
    expert_sum = jnp.sum(weighted.reshape(tok_rows, TOPK, D), axis=1)
    layer_out = (residual + expert_sum).astype(jnp.bfloat16)
    return (layer_out, kv_cache)


PLANES = 4


def strictly_lower(size):
    return jnp.asarray(np.tril(np.ones((size, size), np.float32), -1), jnp.bfloat16)


def count_before(flags):
    return jnp.dot(
        strictly_lower(flags.shape[0]),
        flags.astype(jnp.bfloat16),
        preferred_element_type=jnp.float32,
    )


def move_pages(keys, values, page_table):
    rows = keys.shape[0]
    width = keys.shape[1]
    page_rows = rows // PAGE
    groups = lax.axis_size("req")
    per_group = page_rows // groups
    myself = lax.axis_index("req")
    whole_table = page_table.reshape(groups, page_rows)
    own_table = lax.dynamic_slice_in_dim(page_table, myself * page_rows, page_rows, 0)
    target = own_table // page_rows
    picked = target[:, None] == jnp.arange(groups, dtype=jnp.int32)[None, :]
    ranking = jnp.sum(jnp.where(picked, count_before(picked), 0.0), axis=1).astype(jnp.int32)
    slot = target * per_group + ranking
    within = jnp.arange(PAGE, dtype=jnp.int32)
    lines = jnp.arange(rows, dtype=jnp.int32)
    target_line = (slot[:, None] * PAGE + within[None, :]).reshape(-1)
    spread = (target_line[None, :] == lines[:, None]).astype(jnp.bfloat16)
    sent = [
        jnp.dot(spread, block, preferred_element_type=jnp.float32)
        .astype(jnp.bfloat16)
        .reshape(groups, rows // groups, width)
        for block in (keys, values)
    ]
    incoming = lax.all_to_all(
        jnp.stack(sent, axis=1), "req", split_axis=0, concat_axis=0, tiled=True
    )
    arriving = whole_table // page_rows == myself
    arrival = count_before(arriving.T).T.astype(jnp.int32)
    source = jnp.arange(groups, dtype=jnp.int32)[:, None] * per_group + arrival
    landing = jnp.where(arriving, whole_table % page_rows, -1).reshape(-1)
    slots = jnp.arange(page_rows, dtype=jnp.int32)
    source_page = jnp.sum(
        jnp.where(landing[None, :] == slots[:, None], source.reshape(-1)[None, :], 0), axis=1
    )
    source_line = (source_page[:, None] * PAGE + within[None, :]).reshape(-1)
    collect = (source_line[:, None] == lines[None, :]).astype(jnp.bfloat16)
    placed = [
        jnp.dot(
            collect, incoming[:, part].reshape(rows, width), preferred_element_type=jnp.float32
        )
        .astype(jnp.bfloat16)
        .reshape(page_rows, PAGE, width)
        for part in range(2)
    ]
    return jnp.stack(placed, axis=1)


def gather_strips(out_weight):
    groups = lax.axis_size("req")
    strip = out_weight.shape[1] // groups
    start = lax.axis_index("req") * strip
    piece = lax.dynamic_slice_in_dim(out_weight, start, strip, 1)
    strips = lax.all_gather(piece, ("req", "z", "x"), axis=0, tiled=True)
    return strips.reshape(groups, -1, strip)


def share_attended(attended, tok_rows):
    lanes = lax.axis_size("x")
    width = attended.shape[1]
    columns = jnp.transpose(attended.reshape(PLANES, lanes, tok_rows, width), (1, 0, 2, 3))
    sent = jnp.broadcast_to(columns[None], (PLANES,) + columns.shape)
    return lax.all_to_all(
        sent.reshape(PLANES * lanes, PLANES * tok_rows, width),
        ("z", "x"),
        split_axis=0,
        concat_axis=0,
        tiled=True,
    )


def pack_rows(picking, block, shape):
    rows = jnp.dot(picking, block, preferred_element_type=jnp.float32)
    return rows.reshape(shape).astype(jnp.bfloat16)


def project_kernel(turns_ref, shares_ref, strip_ref, s0_ref, s1_ref, s2_ref, s3_ref, gain_ref, picking_ref,
                   normed_ref, residual_ref, packed_ref, rows, whole, squares):
    step = pl.program_id(0)
    steps = pl.num_programs(0)
    tok_rows = s0_ref.shape[0]
    members, _, width = shares_ref.shape
    strip = strip_ref.shape[2]
    depth = normed_ref.shape[2]

    @pl.when(step == 0)
    def _():
        squares[...] = jnp.zeros_like(squares)
        for turn in range(PLANES):
            first = pl.multiple_of(turns_ref[turn] * tok_rows, tok_rows)
            for member in range(members):
                rows[turn * tok_rows:(turn + 1) * tok_rows, member * width:(member + 1) * width] = (
                    shares_ref[member, pl.ds(first, tok_rows), :]
                )

    for turn, stream_ref in enumerate((s0_ref, s1_ref, s2_ref, s3_ref)):
        span = slice(turn * tok_rows, (turn + 1) * tok_rows)
        part = jnp.dot(rows[span, :], strip_ref[0], preferred_element_type=jnp.float32)
        part = part + stream_ref[...].astype(jnp.float32)
        whole[step, span, :] = part
        squares[span, :] += jnp.sum(part * part, axis=1, keepdims=True)

    @pl.when(step == steps - 1)
    def _():
        scale = lax.rsqrt(squares[...] * (1.0 / depth) + 1e-06)
        for index in range(depth // strip):
            span = slice(index * strip, (index + 1) * strip)
            residual_ref[:, span] = whole[index, :tok_rows, :]
            scaled = whole[index] * scale * gain_ref[:, span]
            normed_ref[:, :, span] = scaled.astype(jnp.bfloat16).reshape(PLANES, tok_rows, strip)
        packed_ref[:, 0] = pack_rows(
            picking_ref[...], normed_ref[PLANES - 1], (packed_ref.shape[0],) + packed_ref.shape[2:]
        )


def project_tokens(turns, shares, strips, streams, norm_gain, picking, sources):
    members, rows, width = shares.shape
    steps, depth, strip = strips.shape
    tok_rows = rows // PLANES
    height = picking.shape[0]
    return pl.pallas_call(
        project_kernel,
        grid_spec=pltpu.PrefetchScalarGridSpec(
            num_scalar_prefetch=1,
            grid=(steps,),
            in_specs=[
                pl.BlockSpec((members, rows, width), lambda i, t: (0, 0, 0)),
                pl.BlockSpec((1, depth, strip), lambda i, t: (i, 0, 0)),
            ]
            + [pl.BlockSpec((tok_rows, strip), lambda i, t: (0, i))] * PLANES
            + [
                pl.BlockSpec((1, D), lambda i, t: (0, 0)),
                pl.BlockSpec((height, tok_rows), lambda i, t: (0, 0)),
            ],
            out_specs=[
                pl.BlockSpec((PLANES, tok_rows, D), lambda i, t: (0, 0, 0)),
                pl.BlockSpec((tok_rows, D), lambda i, t: (0, 0)),
                pl.BlockSpec((sources, 1, height // sources, D), lambda i, t: (0, 0, 0, 0)),
            ],
            scratch_shapes=[
                pltpu.VMEM((rows, depth), jnp.bfloat16),
                pltpu.VMEM((steps, rows, strip), jnp.float32),
                pltpu.VMEM((rows, 1), jnp.float32),
            ],
        ),
        out_shape=[
            jax.ShapeDtypeStruct((PLANES, tok_rows, D), jnp.bfloat16),
            jax.ShapeDtypeStruct((tok_rows, D), jnp.float32),
            jax.ShapeDtypeStruct((sources, 1, height // sources, D), jnp.bfloat16),
        ],
        compiler_params=pltpu.CompilerParams(vmem_limit_bytes=56 * 1024 * 1024),
        cost_estimate=pl.CostEstimate(
            flops=2 * rows * depth * D + 2 * height * tok_rows * D,
            bytes_accessed=2 * depth * D + 12 * rows * D,
            transcendentals=rows,
        ),
    )(turns, shares, strips, *streams, norm_gain.reshape(1, D), picking)


def pack_kernel(after_ref, picking_ref, block_ref, out_ref):
    out_ref[:, 0] = pack_rows(
        picking_ref[...], block_ref[0], (out_ref.shape[0],) + out_ref.shape[2:]
    )


def pack_after(after, picking, normed, turn, sources):
    height, tok_rows = picking.shape
    return pl.pallas_call(
        pack_kernel,
        grid=(1,),
        in_specs=[
            pl.BlockSpec(memory_space=pl.ANY),
            pl.BlockSpec((height, tok_rows), lambda i: (0, 0)),
            pl.BlockSpec((1, tok_rows, D), lambda i: (turn, 0, 0)),
        ],
        out_specs=pl.BlockSpec((sources, 1, height // sources, D), lambda i: (0, 0, 0, 0)),
        out_shape=jax.ShapeDtypeStruct((sources, 1, height // sources, D), jnp.bfloat16),
        cost_estimate=pl.CostEstimate(
            flops=2 * height * tok_rows * D, bytes_accessed=4 * height * D, transcendentals=0
        ),
    )(after, picking, normed)


def expert_kernel(packs, *refs):
    (rows_ref, order_ref, back_ref, gate_ref, up_ref, down_ref, picking_ref, block_ref) = refs[-12:-4]
    out_ref, sorted_rows, total, outs = refs[-4:]
    step = pl.program_id(0)
    height, depth = sorted_rows.shape
    count = height // 2
    shape = (out_ref.shape[0],) + out_ref.shape[2:]

    @pl.when(step == 0)
    def _():
        rows = rows_ref[:, 0].astype(jnp.float32).reshape(height, depth).astype(jnp.bfloat16)
        sorted_rows[...] = jnp.dot(
            order_ref[...], rows, preferred_element_type=jnp.float32
        ).astype(jnp.bfloat16)

    if packs:

        @pl.when(step == 1)
        def _():
            out_ref[:, 1] = pack_rows(picking_ref[...], block_ref[0], shape)

    first = pl.multiple_of((step // 2) * count, 16)
    tokens = sorted_rows[pl.ds(first, count), :]
    gate_val = jnp.dot(tokens, gate_ref[0], preferred_element_type=jnp.float32)
    up_val = jnp.dot(tokens, up_ref[0], preferred_element_type=jnp.float32)
    activated = (gate_val / (1.0 + jnp.exp(-gate_val)) * up_val).astype(jnp.bfloat16)
    half_out = jnp.dot(activated, down_ref[0], preferred_element_type=jnp.float32)

    @pl.when(step % 2 == 0)
    def _():
        total[...] = half_out

    @pl.when(step % 2 == 1)
    def _():
        outs[pl.ds(first, count), :] = (total[...] + half_out).astype(jnp.bfloat16)

    @pl.when(step == 3)
    def _():
        out_ref[:, 0] = pack_rows(back_ref[...], outs[...], shape)


def run_experts(after, arrived, w_gate, w_up, w_down, picking, normed, turn):
    sources, parts, slots, depth = arrived.shape
    units = w_gate.shape[2]
    height = sources * slots
    tok_rows = picking.shape[1]
    packs = turn is not None
    index = np.arange(height)
    wanted = (
        index % (height // 2) // (slots // 2) * slots
        + index // (height // 2) * (slots // 2)
        + index % (slots // 2)
    )
    order = (wanted[:, None] == index[None, :]).astype(np.float32)
    fixed = lambda i: (0, 0)
    out_parts = 2 if packs else 1
    taken = turn if packs else 0
    return pl.pallas_call(
        functools.partial(expert_kernel, packs),
        grid=(4,),
        in_specs=[pl.BlockSpec(memory_space=pl.ANY)] * len(after)
        + [
            pl.BlockSpec((sources, 1, slots, depth), lambda i: (0, parts - 1, 0, 0)),
            pl.BlockSpec((height, height), fixed),
            pl.BlockSpec((height, height), fixed),
            pl.BlockSpec((1, depth, units), lambda i: (i, 0, 0)),
            pl.BlockSpec((1, depth, units), lambda i: (i, 0, 0)),
            pl.BlockSpec((1, units, depth), lambda i: (i, 0, 0)),
            pl.BlockSpec((height, tok_rows), fixed),
            pl.BlockSpec((1, tok_rows, depth), lambda i: (taken, 0, 0)),
        ],
        out_specs=pl.BlockSpec((sources, out_parts, slots, depth), lambda i: (0, 0, 0, 0)),
        out_shape=jax.ShapeDtypeStruct((sources, out_parts, slots, depth), jnp.bfloat16),
        scratch_shapes=[
            pltpu.VMEM((height, depth), jnp.bfloat16),
            pltpu.VMEM((height // 2, depth), jnp.float32),
            pltpu.VMEM((height, depth), jnp.bfloat16),
        ],
        compiler_params=pltpu.CompilerParams(vmem_limit_bytes=56 * 1024 * 1024),
        cost_estimate=pl.CostEstimate(
            flops=12 * height * depth * units + 4 * height * height * depth,
            bytes_accessed=12 * depth * units * 2 + 4 * height * depth,
            transcendentals=2 * height * units,
        ),
    )(
        *after,
        arrived,
        jnp.asarray(order, jnp.bfloat16),
        jnp.asarray(order.T, jnp.bfloat16),
        w_gate,
        w_up,
        w_down,
        picking,
        normed,
    )


def on_device_whole(
    stream_in,
    queries,
    keys,
    values,
    out_weight,
    norm_gain,
    w_gate,
    w_up,
    w_down,
    combine,
    segment_ids,
    routes,
    page_table,
):
    tok_rows = stream_in.shape[0]
    groups = lax.axis_size("req")
    lanes = lax.axis_size("x")
    sources = groups * lanes
    plane_experts = 2 * sources
    height = plane_experts * MOST
    level = lax.axis_index("z")
    pairs = [[(low, low ^ turn) for low in range(PLANES)] for turn in range(PLANES)]

    strips = gather_strips(out_weight)
    streams = [stream_in] + [lax.ppermute(stream_in, "z", pairs[turn]) for turn in range(1, PLANES)]

    matched = routes[:, :, None] == jnp.arange(EXPERTS, dtype=jnp.int32)[None, None, :]
    named = jnp.any(matched, axis=1)
    weight_of = jnp.sum(jnp.where(matched, combine[:, :, None], 0.0), axis=1)
    place = jnp.arange(EXPERTS, dtype=jnp.int32)
    in_plane = place // (PLANES * 2 * lanes) * (2 * lanes) + place % (2 * lanes)
    slot_of = jnp.where(named, count_before(named) + (in_plane * MOST)[None, :], -1.0)
    tables = jnp.stack([slot_of.T, weight_of.T])
    tables = tables.reshape(2, groups, PLANES, 2 * lanes, tok_rows)
    tables = jnp.transpose(tables, (2, 0, 1, 3, 4)).reshape(PLANES, 2, plane_experts, tok_rows)
    tables = lax.all_to_all(tables, "z", split_axis=0, concat_axis=0, tiled=True)
    lines = jnp.arange(height, dtype=jnp.float32)
    pickings, mixings = [], []
    for turn in range(PLANES):
        table = lax.dynamic_index_in_dim(tables, level ^ turn, 0, keepdims=False)
        hits = table[0][:, None, :] == lines[None, :, None]
        pickings.append(jnp.sum(hits.astype(jnp.float32), axis=0).astype(jnp.bfloat16))
        mixing = jnp.sum(jnp.where(hits, table[1][:, None, :], 0.0), axis=0)
        high = mixing.astype(jnp.bfloat16)
        mixings.append((high, (mixing - high.astype(jnp.float32)).astype(jnp.bfloat16)))

    attended = attend_rows(queries, keys, values, segment_ids[0])
    shares = share_attended(attended, tok_rows)
    kv_cache = move_pages(keys, values, page_table)
    turns = level ^ jnp.arange(PLANES, dtype=jnp.int32)
    normed, residual, packed = project_tokens(
        turns, shares, strips, streams, norm_gain, pickings[3], sources
    )

    def exchange(block):
        return lax.all_to_all(block, ("req", "x"), split_axis=0, concat_axis=0, tiled=True)

    def experts(after, arrived, turn):
        picking = pickings[0 if turn is None else turn]
        return run_experts(after, arrived, w_gate, w_up, w_down, picking, normed, turn)

    def mixed(turn, returned):
        return sum(
            lax.dot_general(
                part,
                returned.reshape(height, D),
                (((0,), (0,)), ((), ())),
                preferred_element_type=jnp.float32,
            )
            for part in mixings[turn]
        )

    def to_plane(turn, share):
        return lax.ppermute(share, "z", pairs[turn])

    third = exchange(packed)
    packed_second = pack_after(third, pickings[2], normed, 2, sources)
    second = exchange(packed_second)
    outs_third = experts([packed_second], third, 1)
    first = exchange(outs_third)
    outs_second = experts([outs_third], second, 0)
    own = exchange(outs_second)
    share_third = mixed(3, first[:, 0]).astype(jnp.bfloat16)
    outs_first = experts([outs_second, share_third], first, None)
    back_first = exchange(outs_first)
    got_third = to_plane(3, share_third)
    share_second = mixed(2, own[:, 0]).astype(jnp.bfloat16)
    outs_own = experts([outs_first, share_second, got_third], own, None)
    back_own = exchange(outs_own)
    share_first = mixed(1, back_first[:, 0]).astype(jnp.bfloat16)
    total = residual + got_third.astype(jnp.float32) + to_plane(2, share_second).astype(jnp.float32)
    total = total + to_plane(1, share_first).astype(jnp.float32)
    total = total + mixed(0, back_own[:, 0])
    return (total.astype(jnp.bfloat16), kv_cache)


def solution(mesh):
    requests, members = mesh.shape["req"], mesh.shape["exp"]
    whole = 2 * EXPERTS == 4 * requests * members
    if whole:
        grid = mesh.devices.reshape(requests, PLANES, members // PLANES)
        mesh = Mesh(grid, ("req", "z", "x"))
    exp = ("z", "x") if whole else "exp"
    every = ("req", "z", "x") if whole else ("req", "exp")
    return jax.shard_map(
        on_device_whole if whole else on_device_split,
        mesh=mesh,
        in_specs=(
            P(every, None),
            P("req", exp),
            P("req", exp),
            P("req", exp),
            P(exp, None),
            P(),
            P(every, None, None),
            P(every, None, None),
            P(every, None, None),
            P(every, None),
            P("req", None),
            P(every, None),
            P(),
        ),
        out_specs=(P(every, None), P("req", None, None, exp)),
        check_vma=False,
    )
```

```python
import math

import jax
import jax.numpy as jnp
import numpy as np
from jax import lax
from jax.experimental import pallas as pl
from jax.experimental.pallas import tpu as pltpu
from jax.sharding import Mesh
from jax.sharding import PartitionSpec as P

D = 2048
HD = 128
EXPERTS = 64
TOPK = 8
PAGE = 16
MOST = 20


def from_partner(block, axis, distance):
    count = lax.axis_size(axis)
    route = []
    for low in range(count):
        high = low | 1 << distance
        if high != low and high < count:
            route += [(low, high), (high, low)]
    return lax.ppermute(block, axis, route)


def attend_rows(queries, keys, values, segments):
    length = queries.shape[0]
    head_count = queries.shape[1] // HD
    query_heads = queries.reshape(length, head_count, HD)
    key_heads = keys.reshape(length, head_count, HD)
    value_heads = values.reshape(length, head_count, HD)
    scaling = 1.0 / math.sqrt(HD)
    rows_block = min(512, length)

    def attend_block(position):
        start = position * rows_block
        query_block = lax.dynamic_slice_in_dim(query_heads, start, rows_block, 0)
        segment_block = lax.dynamic_slice_in_dim(segments, start, rows_block, 0)
        scores = (
            jnp.einsum("qhd,khd->hqk", query_block, key_heads, preferred_element_type=jnp.float32)
            * scaling
        )
        allowed = (segment_block[:, None] == segments[None, :])[None, :, :]
        scores = jnp.where(allowed, scores, jnp.float32(-1e30))
        highest = jnp.max(scores, axis=2, keepdims=True)
        weights_exp = jnp.exp(scores - highest)
        totals = jnp.sum(weights_exp, axis=2)
        mixed = jnp.einsum(
            "hqk,khd->qhd",
            weights_exp.astype(jnp.bfloat16),
            value_heads,
            preferred_element_type=jnp.float32,
        )
        mixed = mixed / jnp.transpose(totals)[:, :, None]
        return mixed.astype(jnp.bfloat16)

    blocks = lax.map(attend_block, jnp.arange(length // rows_block))
    return blocks.reshape(length, head_count * HD)


def write_pages(keys, values, page_table):
    page_rows = keys.shape[0] // PAGE
    groups = lax.axis_size("req")
    per_group = page_rows // groups
    width = keys.shape[1]
    pages = jnp.stack(
        [keys.reshape(page_rows, PAGE, width), values.reshape(page_rows, PAGE, width)], axis=1
    )
    myself = lax.axis_index("req")
    whole_table = page_table.reshape(groups, page_rows)
    own_table = lax.dynamic_slice_in_dim(page_table, myself * page_rows, page_rows, 0)
    target = own_table // page_rows
    picked = (target[:, None] == jnp.arange(groups, dtype=jnp.int32)[None, :]).astype(jnp.int32)
    ranking = jnp.sum(jnp.cumsum(picked, axis=0) * picked, axis=1) - 1
    outgoing = jnp.zeros_like(pages).at[target * per_group + ranking].set(pages)
    incoming = lax.all_to_all(
        outgoing.reshape(groups, per_group, 2, PAGE, width),
        "req",
        split_axis=0,
        concat_axis=0,
        tiled=True,
    )
    arriving = whole_table // page_rows == myself
    arrival_rank = jnp.cumsum(arriving.astype(jnp.int32), axis=1) - 1
    placing = jnp.where(
        arriving, jnp.arange(groups, dtype=jnp.int32)[:, None] * per_group + arrival_rank, page_rows
    )
    slot_table = (
        jnp.zeros((page_rows + 1,), jnp.int32)
        .at[placing.reshape(-1)]
        .set((whole_table % page_rows).reshape(-1))
    )
    slot_table = slot_table[:page_rows]
    return jnp.zeros_like(pages).at[slot_table].set(incoming.reshape(page_rows, 2, PAGE, width))


def whole_experts(w_gate, w_up, w_down):
    local_halves = w_gate.shape[0]
    half_units = w_gate.shape[2]
    if local_halves == 1:
        packed = jnp.stack([w_gate[0], w_up[0], w_down[0].reshape(D, half_units)])
        partner = from_partner(packed, "exp", 0)
        leading = lax.axis_index("exp") % 2 == 0
        first = jnp.where(leading, packed, partner)
        second = jnp.where(leading, partner, packed)
        gate_full = jnp.stack([first[0], second[0]])[None]
        up_full = jnp.stack([first[1], second[1]])[None]
        down_full = jnp.stack([first[2].reshape(half_units, D), second[2].reshape(half_units, D)])[
            None
        ]
        return (gate_full, up_full, down_full, 1)
    gate_full = w_gate.reshape(local_halves // 2, 2, D, half_units)
    up_full = w_up.reshape(local_halves // 2, 2, D, half_units)
    down_full = w_down.reshape(local_halves // 2, 2, half_units, D)
    return (gate_full, up_full, down_full, 2)


def on_device_split(
    stream_in,
    queries,
    keys,
    values,
    out_weight,
    norm_gain,
    w_gate,
    w_up,
    w_down,
    combine,
    segment_ids,
    routes,
    page_table,
):
    attended = attend_rows(queries, keys, values, segment_ids[0])
    kv_cache = write_pages(keys, values, page_table)
    tok_rows = stream_in.shape[0]
    projected = lax.psum_scatter(
        jnp.dot(attended, out_weight, preferred_element_type=jnp.float32),
        "exp",
        scatter_dimension=0,
        tiled=True,
    )
    residual = stream_in.astype(jnp.float32) + projected
    scale_rows = lax.rsqrt(jnp.mean(residual * residual, axis=1, keepdims=True) + 1e-06)
    normed = (residual * scale_rows * norm_gain).astype(jnp.bfloat16)
    expert_ids = routes.reshape(-1)
    owners = (expert_ids[:, None] == jnp.arange(EXPERTS, dtype=jnp.int32)[None, :]).astype(
        jnp.int32
    )
    ranking = jnp.sum(jnp.cumsum(owners, axis=0) * owners, axis=1) - 1
    pair_rows = jnp.repeat(normed, TOPK, axis=0)
    devices = lax.axis_size(("req", "exp"))
    local_halves = w_gate.shape[0]
    slots = (MOST + 1) // 2
    holder = 2 * expert_ids + ranking % 2
    position = ranking // 2
    outgoing = jnp.zeros((devices * local_halves * slots, D), jnp.bfloat16)
    outgoing = outgoing.at[holder * slots + position].set(pair_rows)
    gate_full, up_full, down_full, copies = whole_experts(w_gate, w_up, w_down)
    local_experts = gate_full.shape[0]
    arrived = lax.all_to_all(
        outgoing.reshape(devices, local_halves, slots, D),
        ("req", "exp"),
        split_axis=0,
        concat_axis=0,
        tiled=True,
    )
    count = arrived.shape[2]
    grouped = arrived.reshape(devices, local_experts, copies, count, D)
    gate_val = jnp.einsum(
        "sercd,ejdf->serjcf", grouped, gate_full, preferred_element_type=jnp.float32
    )
    up_val = jnp.einsum("sercd,ejdf->serjcf", grouped, up_full, preferred_element_type=jnp.float32)
    activated = (jax.nn.silu(gate_val) * up_val).astype(jnp.bfloat16)
    halves_out = jnp.einsum(
        "serjcf,ejfd->serjcd", activated, down_full, preferred_element_type=jnp.float32
    ).astype(jnp.bfloat16)
    returned = lax.all_to_all(
        halves_out.reshape(devices, local_halves, 2, count, D),
        ("req", "exp"),
        split_axis=0,
        concat_axis=0,
        tiled=True,
    )
    flat_back = returned.reshape(devices * local_halves, 2, slots, D)
    combined = flat_back[holder, 0, position].astype(jnp.float32) + flat_back[
        holder, 1, position
    ].astype(jnp.float32)
    weighted = combined * combine.reshape(-1)[:, None]
    expert_sum = jnp.sum(weighted.reshape(tok_rows, TOPK, D), axis=1)
    layer_out = (residual + expert_sum).astype(jnp.bfloat16)
    return (layer_out, kv_cache)


PLANES = 4


def strictly_lower(size):
    return jnp.asarray(np.tril(np.ones((size, size), np.float32), -1), jnp.bfloat16)


def count_before(flags):
    return jnp.dot(
        strictly_lower(flags.shape[0]),
        flags.astype(jnp.bfloat16),
        preferred_element_type=jnp.float32,
    )


def move_pages(keys, values, page_table, after):
    rows, width = keys.shape
    page_rows = rows // PAGE
    groups = lax.axis_size("req")
    per_group = page_rows // groups
    myself = lax.axis_index("req")
    whole_table = page_table.reshape(groups, page_rows)
    own_table = lax.dynamic_slice_in_dim(page_table, myself * page_rows, page_rows, 0)
    target = own_table // page_rows
    picked = target[:, None] == jnp.arange(groups, dtype=jnp.int32)[None, :]
    ranking = jnp.sum(jnp.where(picked, count_before(picked), 0.0), axis=1).astype(jnp.int32)
    slot = (target ^ myself) * per_group + ranking
    within = jnp.arange(PAGE, dtype=jnp.int32)
    lines = jnp.arange(rows, dtype=jnp.int32)
    target_line = (slot[:, None] * PAGE + within[None, :]).reshape(-1, 128)
    target_line = tie(target_line, after).reshape(-1)
    spread = (target_line[None, :] == lines[:, None]).astype(jnp.bfloat16)
    both = jnp.concatenate([keys, values], axis=1)
    sent = jnp.dot(spread, both, preferred_element_type=jnp.float32).astype(jnp.bfloat16)
    sent = sent.reshape(groups, rows // groups, 2 * width)
    incoming = [sent[0]]
    for apart in range(1, groups):
        pairs = [(low, low ^ apart) for low in range(groups)]
        incoming.append(lax.ppermute(sent[apart], "req", pairs))

    def place():
        arriving = whole_table // page_rows == myself
        arrival = count_before(arriving.T).T.astype(jnp.int32)
        apart = jnp.arange(groups, dtype=jnp.int32)[:, None] ^ myself
        source = apart * per_group + arrival
        landing = jnp.where(arriving, whole_table % page_rows, -1).reshape(-1)
        slots = jnp.arange(page_rows, dtype=jnp.int32)
        source_page = jnp.sum(
            jnp.where(landing[None, :] == slots[:, None], source.reshape(-1)[None, :], 0), axis=1
        )
        source_line = (source_page[:, None] * PAGE + within[None, :]).reshape(-1)
        collect = (source_line[:, None] == lines[None, :]).astype(jnp.bfloat16)
        placed = jnp.dot(
            collect, jnp.concatenate(incoming, axis=0), preferred_element_type=jnp.float32
        ).astype(jnp.bfloat16)
        placed = placed.reshape(page_rows, PAGE, 2, width)
        return jnp.transpose(placed, (0, 2, 1, 3))

    return incoming, place


def attend_kernel(query_ref, key_ref, value_ref, line_ref, row_ref, out_ref):
    allowed = line_ref[...] == row_ref[...]
    half = out_ref.shape[1]
    scaling = 1.0 / math.sqrt(HD)
    for head in range(query_ref.shape[1] // HD):
        span = slice(head * HD, (head + 1) * HD)
        scores = lax.dot_general(
            query_ref[:, span],
            key_ref[:, span],
            (((1,), (1,)), ((), ())),
            preferred_element_type=jnp.float32,
        )
        scores = jnp.where(allowed, scores * scaling, jnp.float32(-1e30))
        weights = jnp.exp(scores - jnp.max(scores, axis=1, keepdims=True))
        totals = jnp.sum(weights, axis=1, keepdims=True)
        mixed = jnp.dot(
            weights.astype(jnp.bfloat16), value_ref[:, span], preferred_element_type=jnp.float32
        )
        mixed = (mixed / totals).astype(jnp.bfloat16)
        out_ref[0, :, span] = mixed[:half]
        out_ref[1, :, span] = mixed[half:]


def attend_columns(queries, keys, values, segments, tok_rows):
    rows, width = queries.shape
    block = 2 * tok_rows
    steps = rows // block
    return pl.pallas_call(
        attend_kernel,
        grid=(steps,),
        in_specs=[
            pl.BlockSpec((block, width), lambda i: (i, 0)),
            pl.BlockSpec((rows, width), lambda i: (0, 0)),
            pl.BlockSpec((rows, width), lambda i: (0, 0)),
            pl.BlockSpec((block, 1), lambda i: (i, 0)),
            pl.BlockSpec((1, rows), lambda i: (0, 0)),
        ],
        out_specs=pl.BlockSpec((2, tok_rows, width), lambda i: (0, i, 0)),
        out_shape=jax.ShapeDtypeStruct((2, rows // 2, width), jnp.bfloat16),
        compiler_params=pltpu.CompilerParams(vmem_limit_bytes=40 * 1024 * 1024),
        cost_estimate=pl.CostEstimate(
            flops=4 * rows * rows * width,
            bytes_accessed=8 * rows * width,
            transcendentals=rows * rows * width // HD,
        ),
    )(queries, keys, values, segments.reshape(rows, 1), segments.reshape(1, rows))


def partial_kernel(place_ref, mine_ref, other_ref, weight_ref, first_ref, rest_ref, out_ref, total):
    step = pl.program_id(0)
    total[...] = jnp.dot(mine_ref[0], weight_ref[...], preferred_element_type=jnp.float32)

    @pl.when(step < 2)
    def _():
        total[...] += jnp.dot(other_ref[...], first_ref[...], preferred_element_type=jnp.float32)

    @pl.when(step >= 2)
    def _():
        total[...] += jnp.dot(other_ref[...], rest_ref[...], preferred_element_type=jnp.float32)

    out_ref[...] = total[...].reshape(out_ref.shape).astype(jnp.bfloat16)


def partial_products(place, attended, other, out_weight, other_weight, other_rest):
    _, rows, width = attended.shape
    strip = D // 4
    column_of = lambda i, p: (i // 2 ^ p[1]) * 2 + i % 2
    return pl.pallas_call(
        partial_kernel,
        grid_spec=pltpu.PrefetchScalarGridSpec(
            num_scalar_prefetch=1,
            grid=(4,),
            in_specs=[
                pl.BlockSpec((1, rows, width), lambda i, p: (p[0], 0, 0)),
                pl.BlockSpec((rows, width), lambda i, p: (0, 0)),
                pl.BlockSpec((width, strip), lambda i, p: (0, column_of(i, p))),
                pl.BlockSpec((width, strip), lambda i, p: (0, jnp.minimum(i, 1))),
                pl.BlockSpec((width, strip), lambda i, p: (0, jnp.maximum(i - 2, 0))),
            ],
            out_specs=pl.BlockSpec(
                (PLANES, rows // PLANES, strip), lambda i, p: (0, 0, column_of(i, p))
            ),
            scratch_shapes=[pltpu.VMEM((rows, strip), jnp.float32)],
        ),
        out_shape=jax.ShapeDtypeStruct((PLANES, rows // PLANES, D), jnp.bfloat16),
        compiler_params=pltpu.CompilerParams(vmem_limit_bytes=40 * 1024 * 1024),
        cost_estimate=pl.CostEstimate(
            flops=4 * rows * width * D, bytes_accessed=2 * (rows + 2 * width) * D, transcendentals=0
        ),
    )(place, attended, other, out_weight, other_weight, other_rest)


def pack_rows(picking, block, shape):
    rows = jnp.dot(picking, block, preferred_element_type=jnp.float32)
    return rows.reshape(shape).astype(jnp.bfloat16)


def norm_kernel(*refs):
    stream_ref, parts_ref, gain_ref, picking_ref, normed_ref, residual_ref, packed_ref = refs[-7:]
    residual = stream_ref[...].astype(jnp.float32)
    for plane in range(PLANES):
        residual = residual + parts_ref[plane].astype(jnp.float32)
    residual_ref[...] = residual
    scale = lax.rsqrt(jnp.mean(residual * residual, axis=1, keepdims=True) + 1e-06)
    normed = (residual * scale * gain_ref[...]).astype(jnp.bfloat16)
    normed_ref[...] = normed
    packed_ref[:, 0] = pack_rows(
        picking_ref[...], normed, (packed_ref.shape[0],) + packed_ref.shape[2:]
    )


def norm_and_pack(after, stream_in, parts, norm_gain, picking, sources):
    tok_rows = stream_in.shape[0]
    height = picking.shape[0]
    operands = (stream_in, parts, norm_gain.reshape(1, D), picking)
    shapes = [
        jax.ShapeDtypeStruct((tok_rows, D), jnp.bfloat16),
        jax.ShapeDtypeStruct((tok_rows, D), jnp.float32),
        jax.ShapeDtypeStruct((sources, 1, height // sources, D), jnp.bfloat16),
    ]
    whole = lambda a: pl.BlockSpec(a.shape, lambda i, rank=len(a.shape): (0,) * rank)
    return pl.pallas_call(
        norm_kernel,
        grid=(1,),
        in_specs=[pl.BlockSpec(memory_space=pl.ANY)] * len(after) + [whole(a) for a in operands],
        out_specs=[whole(a) for a in shapes],
        out_shape=shapes,
        compiler_params=pltpu.CompilerParams(vmem_limit_bytes=40 * 1024 * 1024),
        cost_estimate=pl.CostEstimate(
            flops=2 * height * tok_rows * D + 10 * tok_rows * D,
            bytes_accessed=(16 * tok_rows + 2 * height) * D,
            transcendentals=tok_rows,
        ),
    )(*after, *operands)


def pack_kernel(after_ref, picking_ref, block_ref, out_ref):
    out_ref[:, 0] = pack_rows(
        picking_ref[...], block_ref[...], (out_ref.shape[0],) + out_ref.shape[2:]
    )


def pack_after(after, picking, block, sources, into=False):
    height, tok_rows = picking.shape
    parts = 2 if into else 1
    return pl.pallas_call(
        pack_kernel,
        grid=(1,),
        in_specs=[
            pl.BlockSpec(memory_space=pl.ANY),
            pl.BlockSpec((height, tok_rows), lambda i: (0, 0)),
            pl.BlockSpec((tok_rows, D), lambda i: (0, 0)),
        ],
        out_specs=pl.BlockSpec((sources, 1, height // sources, D), lambda i: (0, parts - 1, 0, 0)),
        out_shape=jax.ShapeDtypeStruct((sources, parts, height // sources, D), jnp.bfloat16),
        input_output_aliases={0: 0} if into else {},
        compiler_params=pltpu.CompilerParams(vmem_limit_bytes=40 * 1024 * 1024),
        cost_estimate=pl.CostEstimate(
            flops=2 * height * tok_rows * D, bytes_accessed=4 * height * D, transcendentals=0
        ),
    )(after, picking, block)


def tie_kernel(*refs):
    del refs


def tie(block, *after):
    return pl.pallas_call(
        tie_kernel,
        in_specs=[pl.BlockSpec(memory_space=pl.ANY)] * (1 + len(after)),
        out_specs=pl.BlockSpec(memory_space=pl.ANY),
        out_shape=jax.ShapeDtypeStruct(block.shape, block.dtype),
        input_output_aliases={0: 0},
    )(block, *after)


def expert_kernel(*refs):
    (rows_ref, order_ref, back_ref, gate_ref, up_ref, down_ref) = refs[-10:-4]
    out_ref, sorted_rows, total, outs = refs[-4:]
    step = pl.program_id(0)
    height, depth = sorted_rows.shape
    count = height // 2

    @pl.when(step == 0)
    def _():
        rows = rows_ref[:, 0].astype(jnp.float32).reshape(height, depth).astype(jnp.bfloat16)
        sorted_rows[...] = jnp.dot(
            order_ref[...], rows, preferred_element_type=jnp.float32
        ).astype(jnp.bfloat16)

    first = pl.multiple_of((step // 2) * count, 16)
    tokens = sorted_rows[pl.ds(first, count), :]
    gate_val = jnp.dot(tokens, gate_ref[0], preferred_element_type=jnp.float32)
    up_val = jnp.dot(tokens, up_ref[0], preferred_element_type=jnp.float32)
    activated = (gate_val / (1.0 + jnp.exp(-gate_val)) * up_val).astype(jnp.bfloat16)
    half_out = jnp.dot(activated, down_ref[0], preferred_element_type=jnp.float32)

    @pl.when(step % 2 == 0)
    def _():
        total[...] = half_out

    @pl.when(step % 2 == 1)
    def _():
        outs[pl.ds(first, count), :] = (total[...] + half_out).astype(jnp.bfloat16)

    @pl.when(step == 3)
    def _():
        out_ref[:, 0] = pack_rows(back_ref[...], outs[...], (out_ref.shape[0],) + out_ref.shape[2:])


def run_experts(after, arrived, w_gate, w_up, w_down, out_parts=1):
    sources, parts, slots, depth = arrived.shape
    units = w_gate.shape[2]
    height = sources * slots
    index = np.arange(height)
    wanted = (
        index % (height // 2) // (slots // 2) * slots
        + index // (height // 2) * (slots // 2)
        + index % (slots // 2)
    )
    order = (wanted[:, None] == index[None, :]).astype(np.float32)
    fixed = lambda i: (0, 0)
    return pl.pallas_call(
        expert_kernel,
        grid=(4,),
        in_specs=[pl.BlockSpec(memory_space=pl.ANY)] * len(after)
        + [
            pl.BlockSpec((sources, 1, slots, depth), lambda i: (0, parts - 1, 0, 0)),
            pl.BlockSpec((height, height), fixed),
            pl.BlockSpec((height, height), fixed),
            pl.BlockSpec((1, depth, units), lambda i: (i, 0, 0)),
            pl.BlockSpec((1, depth, units), lambda i: (i, 0, 0)),
            pl.BlockSpec((1, units, depth), lambda i: (i, 0, 0)),
        ],
        out_specs=pl.BlockSpec((sources, 1, slots, depth), lambda i: (0, 0, 0, 0)),
        out_shape=jax.ShapeDtypeStruct((sources, out_parts, slots, depth), jnp.bfloat16),
        scratch_shapes=[
            pltpu.VMEM((height, depth), jnp.bfloat16),
            pltpu.VMEM((height // 2, depth), jnp.float32),
            pltpu.VMEM((height, depth), jnp.bfloat16),
        ],
        compiler_params=pltpu.CompilerParams(vmem_limit_bytes=56 * 1024 * 1024),
        cost_estimate=pl.CostEstimate(
            flops=12 * height * depth * units + 4 * height * height * depth,
            bytes_accessed=12 * depth * units * 2 + 4 * height * depth,
            transcendentals=2 * height * units,
        ),
    )(
        *after,
        arrived,
        jnp.asarray(order, jnp.bfloat16),
        jnp.asarray(order.T, jnp.bfloat16),
        w_gate,
        w_up,
        w_down,
    )


def on_device_whole(
    stream_in,
    queries,
    keys,
    values,
    out_weight,
    norm_gain,
    w_gate,
    w_up,
    w_down,
    combine,
    segment_ids,
    routes,
    page_table,
):
    tok_rows = stream_in.shape[0]
    groups = lax.axis_size("req")
    lanes = lax.axis_size("x")
    sources = groups * lanes
    plane_experts = 2 * sources
    height = plane_experts * MOST
    level = lax.axis_index("z")
    column = lax.axis_index("x")
    swap = [(0, 1), (1, 0)]
    pairs = [[(low, low ^ turn) for low in range(PLANES)] for turn in range(PLANES)]

    core = lax.axis_index("req") % 2
    cores = [(low, low ^ 1) for low in range(groups)]
    half = lax.dynamic_slice_in_dim(out_weight, core * (D // 2), D // 2, 1)
    other_weight = lax.ppermute(half, "x", swap)
    other_rest = lax.ppermute(other_weight, "req", cores)
    attended = attend_columns(queries, keys, values, segment_ids[0], tok_rows)
    leaving = lax.dynamic_index_in_dim(attended, 1 - column, 0, keepdims=False)
    other = lax.ppermute(tie(leaving, other_weight), "x", swap)

    matched = routes[:, :, None] == jnp.arange(EXPERTS, dtype=jnp.int32)[None, None, :]
    named = jnp.any(matched, axis=1)
    weight_of = jnp.sum(jnp.where(matched, combine[:, :, None], 0.0), axis=1)
    place = jnp.arange(EXPERTS, dtype=jnp.int32)
    in_plane = place // (PLANES * 2 * lanes) * (2 * lanes) + place % (2 * lanes)
    slot_of = jnp.where(named, count_before(named) + (in_plane * MOST)[None, :], -1.0)
    tables = jnp.stack([slot_of.T, weight_of.T])
    tables = tables.reshape(2, groups, PLANES, 2 * lanes, tok_rows)
    tables = jnp.transpose(tables, (2, 0, 1, 3, 4)).reshape(PLANES, 2, plane_experts, tok_rows)
    lines = jnp.arange(height, dtype=jnp.float32)
    pickings, mixings = [], []
    for turn in range(PLANES):
        table = lax.dynamic_index_in_dim(tables, level ^ turn, 0, keepdims=False)
        if turn:
            table = lax.ppermute(table, "z", pairs[turn])
        hits = table[0][:, None, :] == lines[None, :, None]
        pickings.append(jnp.sum(hits.astype(jnp.float32), axis=0).astype(jnp.bfloat16))
        mixing = jnp.sum(jnp.where(hits, table[1][:, None, :], 0.0), axis=0)
        high = mixing.astype(jnp.bfloat16)
        mixings.append((high, (mixing - high.astype(jnp.float32)).astype(jnp.bfloat16)))

    partial = partial_products(
        jnp.stack([column, core]).astype(jnp.int32),
        attended,
        other,
        out_weight,
        other_weight,
        other_rest,
    )
    gathered = lax.all_to_all(partial, "z", split_axis=0, concat_axis=0, tiled=True)
    pages, place_pages = move_pages(keys, values, page_table, partial)
    normed, residual, packed = norm_and_pack(
        pages[1:], stream_in, gathered, norm_gain, pickings[0], sources
    )

    def exchange(block):
        return lax.all_to_all(block, ("req", "x"), split_axis=0, concat_axis=0, tiled=True)

    def experts(after, arrived, out_parts=1):
        return run_experts(after, arrived, w_gate, w_up, w_down, out_parts)

    def mixed(turn, returned):
        return sum(
            lax.dot_general(
                part,
                returned[:, 0].reshape(height, D),
                (((0,), (0,)), ((), ())),
                preferred_element_type=jnp.float32,
            )
            for part in mixings[turn]
        )

    def to_plane(turn, block):
        return lax.ppermute(block, "z", pairs[turn])

    blocks = [normed] + [to_plane(turn, normed) for turn in range(1, PLANES)]
    own = exchange(packed)
    packed_third = pack_after(own, pickings[3], blocks[3], sources)
    third = exchange(packed_third)
    packed_second = pack_after(third, pickings[2], blocks[2], sources)
    second = exchange(packed_second)
    outs_third = experts([packed_second], third, 2)
    outs_third = pack_after(outs_third, pickings[1], blocks[1], sources, into=True)
    first = exchange(outs_third)
    outs_second = experts([outs_third], second)
    back_second = exchange(outs_second)
    share_third = mixed(3, first).astype(jnp.bfloat16)
    outs_first = experts([outs_second, share_third], first)
    got_third = to_plane(3, share_third)
    back_first = exchange(outs_first)
    share_second = mixed(2, tie(back_second, got_third)).astype(jnp.bfloat16)
    outs_own = experts([share_second], own)
    got_second = to_plane(2, share_second)
    back_own = exchange(outs_own)
    share_first = mixed(1, tie(back_first, got_second)).astype(jnp.bfloat16)
    total = residual + got_third.astype(jnp.float32) + got_second.astype(jnp.float32)
    total = total + to_plane(1, share_first).astype(jnp.float32)
    total = total + mixed(0, back_own)
    return (total.astype(jnp.bfloat16), place_pages())


def solution(mesh):
    requests, members = mesh.shape["req"], mesh.shape["exp"]
    whole = 2 * EXPERTS == 4 * requests * members and members == 2 * PLANES
    if whole:
        grid = mesh.devices.reshape(requests, PLANES, members // PLANES)
        mesh = Mesh(grid, ("req", "z", "x"))
    exp = ("z", "x") if whole else "exp"
    every = ("req", "z", "x") if whole else ("req", "exp")
    return jax.shard_map(
        on_device_whole if whole else on_device_split,
        mesh=mesh,
        in_specs=(
            P(every, None),
            P("req", exp),
            P("req", exp),
            P("req", exp),
            P(exp, None),
            P(),
            P(every, None, None),
            P(every, None, None),
            P(every, None, None),
            P(every, None),
            P("req", None),
            P(every, None),
            P(),
        ),
        out_specs=(P(every, None), P("req", None, None, exp)),
        check_vma=False,
    )
```

```python
import math

import jax
import jax.numpy as jnp
import numpy as np
from jax import lax
from jax.experimental import pallas as pl
from jax.experimental.pallas import tpu as pltpu
from jax.sharding import Mesh
from jax.sharding import PartitionSpec as P

D = 2048
HD = 128
EXPERTS = 64
TOPK = 8
PAGE = 16
MOST = 20


def from_partner(block, axis, distance):
    count = lax.axis_size(axis)
    route = []
    for low in range(count):
        high = low | 1 << distance
        if high != low and high < count:
            route += [(low, high), (high, low)]
    return lax.ppermute(block, axis, route)


def attend_rows(queries, keys, values, segments):
    length = queries.shape[0]
    head_count = queries.shape[1] // HD
    query_heads = queries.reshape(length, head_count, HD)
    key_heads = keys.reshape(length, head_count, HD)
    value_heads = values.reshape(length, head_count, HD)
    scaling = 1.0 / math.sqrt(HD)
    rows_block = min(512, length)

    def attend_block(position):
        start = position * rows_block
        query_block = lax.dynamic_slice_in_dim(query_heads, start, rows_block, 0)
        segment_block = lax.dynamic_slice_in_dim(segments, start, rows_block, 0)
        scores = (
            jnp.einsum("qhd,khd->hqk", query_block, key_heads, preferred_element_type=jnp.float32)
            * scaling
        )
        allowed = (segment_block[:, None] == segments[None, :])[None, :, :]
        scores = jnp.where(allowed, scores, jnp.float32(-1e30))
        highest = jnp.max(scores, axis=2, keepdims=True)
        weights_exp = jnp.exp(scores - highest)
        totals = jnp.sum(weights_exp, axis=2)
        mixed = jnp.einsum(
            "hqk,khd->qhd",
            weights_exp.astype(jnp.bfloat16),
            value_heads,
            preferred_element_type=jnp.float32,
        )
        mixed = mixed / jnp.transpose(totals)[:, :, None]
        return mixed.astype(jnp.bfloat16)

    blocks = lax.map(attend_block, jnp.arange(length // rows_block))
    return blocks.reshape(length, head_count * HD)


def write_pages(keys, values, page_table):
    page_rows = keys.shape[0] // PAGE
    groups = lax.axis_size("req")
    per_group = page_rows // groups
    width = keys.shape[1]
    pages = jnp.stack(
        [keys.reshape(page_rows, PAGE, width), values.reshape(page_rows, PAGE, width)], axis=1
    )
    myself = lax.axis_index("req")
    whole_table = page_table.reshape(groups, page_rows)
    own_table = lax.dynamic_slice_in_dim(page_table, myself * page_rows, page_rows, 0)
    target = own_table // page_rows
    picked = (target[:, None] == jnp.arange(groups, dtype=jnp.int32)[None, :]).astype(jnp.int32)
    ranking = jnp.sum(jnp.cumsum(picked, axis=0) * picked, axis=1) - 1
    outgoing = jnp.zeros_like(pages).at[target * per_group + ranking].set(pages)
    incoming = lax.all_to_all(
        outgoing.reshape(groups, per_group, 2, PAGE, width),
        "req",
        split_axis=0,
        concat_axis=0,
        tiled=True,
    )
    arriving = whole_table // page_rows == myself
    arrival_rank = jnp.cumsum(arriving.astype(jnp.int32), axis=1) - 1
    placing = jnp.where(
        arriving, jnp.arange(groups, dtype=jnp.int32)[:, None] * per_group + arrival_rank, page_rows
    )
    slot_table = (
        jnp.zeros((page_rows + 1,), jnp.int32)
        .at[placing.reshape(-1)]
        .set((whole_table % page_rows).reshape(-1))
    )
    slot_table = slot_table[:page_rows]
    return jnp.zeros_like(pages).at[slot_table].set(incoming.reshape(page_rows, 2, PAGE, width))


def whole_experts(w_gate, w_up, w_down):
    local_halves = w_gate.shape[0]
    half_units = w_gate.shape[2]
    if local_halves == 1:
        packed = jnp.stack([w_gate[0], w_up[0], w_down[0].reshape(D, half_units)])
        partner = from_partner(packed, "exp", 0)
        leading = lax.axis_index("exp") % 2 == 0
        first = jnp.where(leading, packed, partner)
        second = jnp.where(leading, partner, packed)
        gate_full = jnp.stack([first[0], second[0]])[None]
        up_full = jnp.stack([first[1], second[1]])[None]
        down_full = jnp.stack([first[2].reshape(half_units, D), second[2].reshape(half_units, D)])[
            None
        ]
        return (gate_full, up_full, down_full, 1)
    gate_full = w_gate.reshape(local_halves // 2, 2, D, half_units)
    up_full = w_up.reshape(local_halves // 2, 2, D, half_units)
    down_full = w_down.reshape(local_halves // 2, 2, half_units, D)
    return (gate_full, up_full, down_full, 2)


def on_device_split(
    stream_in,
    queries,
    keys,
    values,
    out_weight,
    norm_gain,
    w_gate,
    w_up,
    w_down,
    combine,
    segment_ids,
    routes,
    page_table,
):
    attended = attend_rows(queries, keys, values, segment_ids[0])
    kv_cache = write_pages(keys, values, page_table)
    tok_rows = stream_in.shape[0]
    projected = lax.psum_scatter(
        jnp.dot(attended, out_weight, preferred_element_type=jnp.float32),
        "exp",
        scatter_dimension=0,
        tiled=True,
    )
    residual = stream_in.astype(jnp.float32) + projected
    scale_rows = lax.rsqrt(jnp.mean(residual * residual, axis=1, keepdims=True) + 1e-06)
    normed = (residual * scale_rows * norm_gain).astype(jnp.bfloat16)
    expert_ids = routes.reshape(-1)
    owners = (expert_ids[:, None] == jnp.arange(EXPERTS, dtype=jnp.int32)[None, :]).astype(
        jnp.int32
    )
    ranking = jnp.sum(jnp.cumsum(owners, axis=0) * owners, axis=1) - 1
    pair_rows = jnp.repeat(normed, TOPK, axis=0)
    devices = lax.axis_size(("req", "exp"))
    local_halves = w_gate.shape[0]
    slots = (MOST + 1) // 2
    holder = 2 * expert_ids + ranking % 2
    position = ranking // 2
    outgoing = jnp.zeros((devices * local_halves * slots, D), jnp.bfloat16)
    outgoing = outgoing.at[holder * slots + position].set(pair_rows)
    gate_full, up_full, down_full, copies = whole_experts(w_gate, w_up, w_down)
    local_experts = gate_full.shape[0]
    arrived = lax.all_to_all(
        outgoing.reshape(devices, local_halves, slots, D),
        ("req", "exp"),
        split_axis=0,
        concat_axis=0,
        tiled=True,
    )
    count = arrived.shape[2]
    grouped = arrived.reshape(devices, local_experts, copies, count, D)
    gate_val = jnp.einsum(
        "sercd,ejdf->serjcf", grouped, gate_full, preferred_element_type=jnp.float32
    )
    up_val = jnp.einsum("sercd,ejdf->serjcf", grouped, up_full, preferred_element_type=jnp.float32)
    activated = (jax.nn.silu(gate_val) * up_val).astype(jnp.bfloat16)
    halves_out = jnp.einsum(
        "serjcf,ejfd->serjcd", activated, down_full, preferred_element_type=jnp.float32
    ).astype(jnp.bfloat16)
    returned = lax.all_to_all(
        halves_out.reshape(devices, local_halves, 2, count, D),
        ("req", "exp"),
        split_axis=0,
        concat_axis=0,
        tiled=True,
    )
    flat_back = returned.reshape(devices * local_halves, 2, slots, D)
    combined = flat_back[holder, 0, position].astype(jnp.float32) + flat_back[
        holder, 1, position
    ].astype(jnp.float32)
    weighted = combined * combine.reshape(-1)[:, None]
    expert_sum = jnp.sum(weighted.reshape(tok_rows, TOPK, D), axis=1)
    layer_out = (residual + expert_sum).astype(jnp.bfloat16)
    return (layer_out, kv_cache)


PLANES = 4


def strictly_lower(size):
    return jnp.asarray(np.tril(np.ones((size, size), np.float32), -1), jnp.bfloat16)


def count_before(flags):
    return jnp.dot(
        strictly_lower(flags.shape[0]),
        flags.astype(jnp.bfloat16),
        preferred_element_type=jnp.float32,
    )


def move_pages(keys, values, page_table, after):
    rows, width = keys.shape
    page_rows = rows // PAGE
    groups = lax.axis_size("req")
    per_group = page_rows // groups
    myself = lax.axis_index("req")
    whole_table = page_table.reshape(groups, page_rows)
    own_table = lax.dynamic_slice_in_dim(page_table, myself * page_rows, page_rows, 0)
    target = own_table // page_rows
    picked = target[:, None] == jnp.arange(groups, dtype=jnp.int32)[None, :]
    ranking = jnp.sum(jnp.where(picked, count_before(picked), 0.0), axis=1).astype(jnp.int32)
    slot = (target ^ myself) * per_group + ranking
    within = jnp.arange(PAGE, dtype=jnp.int32)
    lines = jnp.arange(rows, dtype=jnp.int32)
    target_line = (slot[:, None] * PAGE + within[None, :]).reshape(-1, 128)
    target_line = tie(target_line, after).reshape(-1)
    spread = (target_line[None, :] == lines[:, None]).astype(jnp.bfloat16)
    both = jnp.concatenate([keys, values], axis=1)
    sent = jnp.dot(spread, both, preferred_element_type=jnp.float32).astype(jnp.bfloat16)
    sent = sent.reshape(groups, rows // groups, 2 * width)
    incoming = [sent[0]]
    for apart in range(1, groups):
        pairs = [(low, low ^ apart) for low in range(groups)]
        incoming.append(lax.ppermute(sent[apart], "req", pairs))

    def place():
        arriving = whole_table // page_rows == myself
        arrival = count_before(arriving.T).T.astype(jnp.int32)
        apart = jnp.arange(groups, dtype=jnp.int32)[:, None] ^ myself
        source = apart * per_group + arrival
        landing = jnp.where(arriving, whole_table % page_rows, -1).reshape(-1)
        slots = jnp.arange(page_rows, dtype=jnp.int32)
        source_page = jnp.sum(
            jnp.where(landing[None, :] == slots[:, None], source.reshape(-1)[None, :], 0), axis=1
        )
        source_line = (source_page[:, None] * PAGE + within[None, :]).reshape(-1)
        collect = (source_line[:, None] == lines[None, :]).astype(jnp.bfloat16)
        placed = jnp.dot(
            collect, jnp.concatenate(incoming, axis=0), preferred_element_type=jnp.float32
        ).astype(jnp.bfloat16)
        placed = placed.reshape(page_rows, PAGE, 2, width)
        return jnp.transpose(placed, (0, 2, 1, 3))

    return incoming, place


def attend_kernel(query_ref, key_ref, value_ref, line_ref, row_ref, out_ref):
    allowed = line_ref[...] == row_ref[...]
    half = out_ref.shape[1]
    scaling = 1.0 / math.sqrt(HD)
    for head in range(query_ref.shape[1] // HD):
        span = slice(head * HD, (head + 1) * HD)
        scores = lax.dot_general(
            query_ref[:, span],
            key_ref[:, span],
            (((1,), (1,)), ((), ())),
            preferred_element_type=jnp.float32,
        )
        scores = jnp.where(allowed, scores * scaling, jnp.float32(-1e30))
        weights = jnp.exp(scores - jnp.max(scores, axis=1, keepdims=True))
        totals = jnp.sum(weights, axis=1, keepdims=True)
        mixed = jnp.dot(
            weights.astype(jnp.bfloat16), value_ref[:, span], preferred_element_type=jnp.float32
        )
        mixed = (mixed / totals).astype(jnp.bfloat16)
        out_ref[0, :, span] = mixed[:half]
        out_ref[1, :, span] = mixed[half:]


def attend_columns(queries, keys, values, segments, tok_rows):
    rows, width = queries.shape
    block = 2 * tok_rows
    steps = rows // block
    return pl.pallas_call(
        attend_kernel,
        grid=(steps,),
        in_specs=[
            pl.BlockSpec((block, width), lambda i: (i, 0)),
            pl.BlockSpec((rows, width), lambda i: (0, 0)),
            pl.BlockSpec((rows, width), lambda i: (0, 0)),
            pl.BlockSpec((block, 1), lambda i: (i, 0)),
            pl.BlockSpec((1, rows), lambda i: (0, 0)),
        ],
        out_specs=pl.BlockSpec((2, tok_rows, width), lambda i: (0, i, 0)),
        out_shape=jax.ShapeDtypeStruct((2, rows // 2, width), jnp.bfloat16),
        compiler_params=pltpu.CompilerParams(vmem_limit_bytes=40 * 1024 * 1024),
        cost_estimate=pl.CostEstimate(
            flops=4 * rows * rows * width,
            bytes_accessed=8 * rows * width,
            transcendentals=rows * rows * width // HD,
        ),
    )(queries, keys, values, segments.reshape(rows, 1), segments.reshape(1, rows))


def partial_kernel(place_ref, mine_ref, other_ref, weight_ref, first_ref, rest_ref, out_ref, total):
    step = pl.program_id(0)
    total[...] = jnp.dot(mine_ref[0], weight_ref[...], preferred_element_type=jnp.float32)

    @pl.when(step < 2)
    def _():
        total[...] += jnp.dot(other_ref[...], first_ref[...], preferred_element_type=jnp.float32)

    @pl.when(step >= 2)
    def _():
        total[...] += jnp.dot(other_ref[...], rest_ref[...], preferred_element_type=jnp.float32)

    out_ref[...] = total[...].reshape(out_ref.shape).astype(jnp.bfloat16)


def partial_products(place, attended, other, out_weight, other_weight, other_rest):
    _, rows, width = attended.shape
    strip = D // 4
    column_of = lambda i, p: (i // 2 ^ p[1]) * 2 + i % 2
    return pl.pallas_call(
        partial_kernel,
        grid_spec=pltpu.PrefetchScalarGridSpec(
            num_scalar_prefetch=1,
            grid=(4,),
            in_specs=[
                pl.BlockSpec((1, rows, width), lambda i, p: (p[0], 0, 0)),
                pl.BlockSpec((rows, width), lambda i, p: (0, 0)),
                pl.BlockSpec((width, strip), lambda i, p: (0, column_of(i, p))),
                pl.BlockSpec((width, strip), lambda i, p: (0, jnp.minimum(i, 1))),
                pl.BlockSpec((width, strip), lambda i, p: (0, jnp.maximum(i - 2, 0))),
            ],
            out_specs=pl.BlockSpec(
                (PLANES, rows // PLANES, strip), lambda i, p: (0, 0, column_of(i, p))
            ),
            scratch_shapes=[pltpu.VMEM((rows, strip), jnp.float32)],
        ),
        out_shape=jax.ShapeDtypeStruct((PLANES, rows // PLANES, D), jnp.bfloat16),
        compiler_params=pltpu.CompilerParams(vmem_limit_bytes=40 * 1024 * 1024),
        cost_estimate=pl.CostEstimate(
            flops=4 * rows * width * D, bytes_accessed=2 * (rows + 2 * width) * D, transcendentals=0
        ),
    )(place, attended, other, out_weight, other_weight, other_rest)


def pack_rows(picking, block, shape):
    rows = jnp.dot(picking, block, preferred_element_type=jnp.float32)
    return rows.reshape(shape).astype(jnp.bfloat16)


def norm_kernel(*refs):
    stream_ref, parts_ref, gain_ref, picking_ref, normed_ref, residual_ref, packed_ref = refs[-7:]
    residual = stream_ref[...].astype(jnp.float32)
    for plane in range(PLANES):
        residual = residual + parts_ref[plane].astype(jnp.float32)
    residual_ref[...] = residual
    scale = lax.rsqrt(jnp.mean(residual * residual, axis=1, keepdims=True) + 1e-06)
    normed = (residual * scale * gain_ref[...]).astype(jnp.bfloat16)
    normed_ref[...] = normed
    packed_ref[:, 0] = pack_rows(
        picking_ref[...], normed, (packed_ref.shape[0],) + packed_ref.shape[2:]
    )


def norm_and_pack(after, stream_in, parts, norm_gain, picking, sources):
    tok_rows = stream_in.shape[0]
    height = picking.shape[0]
    operands = (stream_in, parts, norm_gain.reshape(1, D), picking)
    shapes = [
        jax.ShapeDtypeStruct((tok_rows, D), jnp.bfloat16),
        jax.ShapeDtypeStruct((tok_rows, D), jnp.float32),
        jax.ShapeDtypeStruct((sources, 1, height // sources, D), jnp.bfloat16),
    ]
    whole = lambda a: pl.BlockSpec(a.shape, lambda i, rank=len(a.shape): (0,) * rank)
    return pl.pallas_call(
        norm_kernel,
        grid=(1,),
        in_specs=[pl.BlockSpec(memory_space=pl.ANY)] * len(after) + [whole(a) for a in operands],
        out_specs=[whole(a) for a in shapes],
        out_shape=shapes,
        compiler_params=pltpu.CompilerParams(vmem_limit_bytes=40 * 1024 * 1024),
        cost_estimate=pl.CostEstimate(
            flops=2 * height * tok_rows * D + 10 * tok_rows * D,
            bytes_accessed=(16 * tok_rows + 2 * height) * D,
            transcendentals=tok_rows,
        ),
    )(*after, *operands)


def pack_kernel(after_ref, picking_ref, block_ref, out_ref):
    out_ref[:, 0] = pack_rows(
        picking_ref[...], block_ref[...], (out_ref.shape[0],) + out_ref.shape[2:]
    )


def pack_after(after, picking, block, sources, into=False):
    height, tok_rows = picking.shape
    parts = 2 if into else 1
    return pl.pallas_call(
        pack_kernel,
        grid=(1,),
        in_specs=[
            pl.BlockSpec(memory_space=pl.ANY),
            pl.BlockSpec((height, tok_rows), lambda i: (0, 0)),
            pl.BlockSpec((tok_rows, D), lambda i: (0, 0)),
        ],
        out_specs=pl.BlockSpec((sources, 1, height // sources, D), lambda i: (0, parts - 1, 0, 0)),
        out_shape=jax.ShapeDtypeStruct((sources, parts, height // sources, D), jnp.bfloat16),
        input_output_aliases={0: 0} if into else {},
        compiler_params=pltpu.CompilerParams(vmem_limit_bytes=40 * 1024 * 1024),
        cost_estimate=pl.CostEstimate(
            flops=2 * height * tok_rows * D, bytes_accessed=4 * height * D, transcendentals=0
        ),
    )(after, picking, block)


def tie_kernel(*refs):
    del refs


def tie(block, *after):
    return pl.pallas_call(
        tie_kernel,
        in_specs=[pl.BlockSpec(memory_space=pl.ANY)] * (1 + len(after)),
        out_specs=pl.BlockSpec(memory_space=pl.ANY),
        out_shape=jax.ShapeDtypeStruct(block.shape, block.dtype),
        input_output_aliases={0: 0},
    )(block, *after)


def expert_kernel(*refs):
    (rows_ref, order_ref, back_ref, gate_ref, up_ref, down_ref) = refs[-10:-4]
    out_ref, sorted_rows, total, outs = refs[-4:]
    step = pl.program_id(0)
    height, depth = sorted_rows.shape
    count = height // 2

    @pl.when(step == 0)
    def _():
        rows = rows_ref[:, 0].astype(jnp.float32).reshape(height, depth).astype(jnp.bfloat16)
        sorted_rows[...] = jnp.dot(
            order_ref[...], rows, preferred_element_type=jnp.float32
        ).astype(jnp.bfloat16)

    first = pl.multiple_of((step // 2) * count, 16)
    tokens = sorted_rows[pl.ds(first, count), :]
    gate_val = jnp.dot(tokens, gate_ref[0], preferred_element_type=jnp.float32)
    up_val = jnp.dot(tokens, up_ref[0], preferred_element_type=jnp.float32)
    activated = (gate_val / (1.0 + jnp.exp(-gate_val)) * up_val).astype(jnp.bfloat16)
    half_out = jnp.dot(activated, down_ref[0], preferred_element_type=jnp.float32)

    @pl.when(step % 2 == 0)
    def _():
        total[...] = half_out

    @pl.when(step % 2 == 1)
    def _():
        outs[pl.ds(first, count), :] = (total[...] + half_out).astype(jnp.bfloat16)

    @pl.when(step == 3)
    def _():
        out_ref[:, 0] = pack_rows(back_ref[...], outs[...], (out_ref.shape[0],) + out_ref.shape[2:])


def run_experts(after, arrived, w_gate, w_up, w_down, out_parts=1):
    sources, parts, slots, depth = arrived.shape
    units = w_gate.shape[2]
    height = sources * slots
    index = np.arange(height)
    wanted = (
        index % (height // 2) // (slots // 2) * slots
        + index // (height // 2) * (slots // 2)
        + index % (slots // 2)
    )
    order = (wanted[:, None] == index[None, :]).astype(np.float32)
    fixed = lambda i: (0, 0)
    return pl.pallas_call(
        expert_kernel,
        grid=(4,),
        in_specs=[pl.BlockSpec(memory_space=pl.ANY)] * len(after)
        + [
            pl.BlockSpec((sources, 1, slots, depth), lambda i: (0, parts - 1, 0, 0)),
            pl.BlockSpec((height, height), fixed),
            pl.BlockSpec((height, height), fixed),
            pl.BlockSpec((1, depth, units), lambda i: (i, 0, 0)),
            pl.BlockSpec((1, depth, units), lambda i: (i, 0, 0)),
            pl.BlockSpec((1, units, depth), lambda i: (i, 0, 0)),
        ],
        out_specs=pl.BlockSpec((sources, 1, slots, depth), lambda i: (0, 0, 0, 0)),
        out_shape=jax.ShapeDtypeStruct((sources, out_parts, slots, depth), jnp.bfloat16),
        scratch_shapes=[
            pltpu.VMEM((height, depth), jnp.bfloat16),
            pltpu.VMEM((height // 2, depth), jnp.float32),
            pltpu.VMEM((height, depth), jnp.bfloat16),
        ],
        compiler_params=pltpu.CompilerParams(vmem_limit_bytes=56 * 1024 * 1024),
        cost_estimate=pl.CostEstimate(
            flops=12 * height * depth * units + 4 * height * height * depth,
            bytes_accessed=12 * depth * units * 2 + 4 * height * depth,
            transcendentals=2 * height * units,
        ),
    )(
        *after,
        arrived,
        jnp.asarray(order, jnp.bfloat16),
        jnp.asarray(order.T, jnp.bfloat16),
        w_gate,
        w_up,
        w_down,
    )


def on_device_whole(
    stream_in,
    queries,
    keys,
    values,
    out_weight,
    norm_gain,
    w_gate,
    w_up,
    w_down,
    combine,
    segment_ids,
    routes,
    page_table,
):
    tok_rows = stream_in.shape[0]
    groups = lax.axis_size("req")
    lanes = lax.axis_size("x")
    sources = groups * lanes
    plane_experts = 2 * sources
    height = plane_experts * MOST
    level = lax.axis_index("z")
    column = lax.axis_index("x")
    swap = [(0, 1), (1, 0)]
    pairs = [[(low, low ^ turn) for low in range(PLANES)] for turn in range(PLANES)]

    core = lax.axis_index("req") % 2
    cores = [(low, low ^ 1) for low in range(groups)]
    half = lax.dynamic_slice_in_dim(out_weight, core * (D // 2), D // 2, 1)
    other_weight = lax.ppermute(half, "x", swap)
    attended = attend_columns(queries, keys, values, segment_ids[0], tok_rows)
    leaving = lax.dynamic_index_in_dim(attended, 1 - column, 0, keepdims=False)
    other = lax.ppermute(leaving, "x", swap)
    other_weight = tie(other_weight, attended)
    other_rest = lax.ppermute(other_weight, "req", cores)

    partial = partial_products(
        jnp.stack([column, core]).astype(jnp.int32),
        attended,
        other,
        out_weight,
        other_weight,
        other_rest,
    )

    routes = tie(routes, partial)
    matched = routes[:, :, None] == jnp.arange(EXPERTS, dtype=jnp.int32)[None, None, :]
    named = jnp.any(matched, axis=1)
    weight_of = jnp.sum(jnp.where(matched, combine[:, :, None], 0.0), axis=1)
    place = jnp.arange(EXPERTS, dtype=jnp.int32)
    in_plane = place // (PLANES * 2 * lanes) * (2 * lanes) + place % (2 * lanes)
    slot_of = jnp.where(named, count_before(named) + (in_plane * MOST)[None, :], -1.0)
    tables = jnp.stack([slot_of.T, weight_of.T])
    tables = tables.reshape(2, groups, PLANES, 2 * lanes, tok_rows)
    tables = jnp.transpose(tables, (2, 0, 1, 3, 4)).reshape(PLANES, 2, plane_experts, tok_rows)
    lines = jnp.arange(height, dtype=jnp.float32)
    pickings, mixings = [], []
    for turn in range(PLANES):
        table = lax.dynamic_index_in_dim(tables, level ^ turn, 0, keepdims=False)
        if turn:
            table = lax.ppermute(table, "z", pairs[turn])
        hits = table[0][:, None, :] == lines[None, :, None]
        pickings.append(jnp.sum(hits.astype(jnp.float32), axis=0).astype(jnp.bfloat16))
        mixing = jnp.sum(jnp.where(hits, table[1][:, None, :], 0.0), axis=0)
        high = mixing.astype(jnp.bfloat16)
        mixings.append((high, (mixing - high.astype(jnp.float32)).astype(jnp.bfloat16)))

    gathered = lax.all_to_all(partial, "z", split_axis=0, concat_axis=0, tiled=True)
    pages, place_pages = move_pages(keys, values, page_table, partial)
    normed, residual, packed = norm_and_pack(
        pages[1:], stream_in, gathered, norm_gain, pickings[0], sources
    )

    def exchange(block):
        return lax.all_to_all(block, ("req", "x"), split_axis=0, concat_axis=0, tiled=True)

    def experts(after, arrived, out_parts=1):
        return run_experts(after, arrived, w_gate, w_up, w_down, out_parts)

    def mixed(turn, returned):
        return sum(
            lax.dot_general(
                part,
                returned[:, 0].reshape(height, D),
                (((0,), (0,)), ((), ())),
                preferred_element_type=jnp.float32,
            )
            for part in mixings[turn]
        )

    def to_plane(turn, block):
        return lax.ppermute(block, "z", pairs[turn])

    blocks = [normed] + [to_plane(turn, normed) for turn in range(1, PLANES)]
    own = exchange(packed)
    packed_first = pack_after(own, pickings[1], blocks[1], sources)
    first = exchange(packed_first)
    outs_own = experts([packed_first], own)
    packed_third = pack_after(first, pickings[3], blocks[3], sources)
    third = exchange(packed_third)
    outs_first = experts([outs_own, packed_third], first, 2)
    outs_first = pack_after(outs_first, pickings[2], blocks[2], sources, into=True)
    second = exchange(outs_first)
    outs_third = experts([outs_first], third)
    back_third = exchange(outs_third)
    share_first = mixed(1, second).astype(jnp.bfloat16)
    outs_second = experts([outs_third, share_first], second)
    got_first = to_plane(1, share_first)
    back_second = exchange(outs_second)
    share_third = mixed(3, tie(back_third, got_first)).astype(jnp.bfloat16)
    got_third = to_plane(3, share_third)
    back_own = exchange(tie(outs_own, back_second))
    share_second = mixed(2, tie(back_second, got_third)).astype(jnp.bfloat16)
    got_second = to_plane(2, share_second)
    total = residual + got_first.astype(jnp.float32) + got_third.astype(jnp.float32)
    total = total + mixed(0, back_own) + got_second.astype(jnp.float32)
    return (total.astype(jnp.bfloat16), place_pages())


def solution(mesh):
    requests, members = mesh.shape["req"], mesh.shape["exp"]
    whole = 2 * EXPERTS == 4 * requests * members and members == 2 * PLANES
    if whole:
        grid = mesh.devices.reshape(requests, PLANES, members // PLANES)
        mesh = Mesh(grid, ("req", "z", "x"))
    exp = ("z", "x") if whole else "exp"
    every = ("req", "z", "x") if whole else ("req", "exp")
    return jax.shard_map(
        on_device_whole if whole else on_device_split,
        mesh=mesh,
        in_specs=(
            P(every, None),
            P("req", exp),
            P("req", exp),
            P("req", exp),
            P(exp, None),
            P(),
            P(every, None, None),
            P(every, None, None),
            P(every, None, None),
            P(every, None),
            P("req", None),
            P(every, None),
            P(),
        ),
        out_specs=(P(every, None), P("req", None, None, exp)),
        check_vma=False,
    )
```

```python
import math

import jax
import jax.numpy as jnp
import numpy as np
from jax import lax
from jax.experimental import pallas as pl
from jax.experimental.pallas import tpu as pltpu
from jax.sharding import Mesh
from jax.sharding import PartitionSpec as P

D = 2048
HD = 128
EXPERTS = 64
TOPK = 8
PAGE = 16
MOST = 20


def from_partner(block, axis, distance):
    count = lax.axis_size(axis)
    route = []
    for low in range(count):
        high = low | 1 << distance
        if high != low and high < count:
            route += [(low, high), (high, low)]
    return lax.ppermute(block, axis, route)


def attend_rows(queries, keys, values, segments):
    length = queries.shape[0]
    head_count = queries.shape[1] // HD
    query_heads = queries.reshape(length, head_count, HD)
    key_heads = keys.reshape(length, head_count, HD)
    value_heads = values.reshape(length, head_count, HD)
    scaling = 1.0 / math.sqrt(HD)
    rows_block = min(512, length)

    def attend_block(position):
        start = position * rows_block
        query_block = lax.dynamic_slice_in_dim(query_heads, start, rows_block, 0)
        segment_block = lax.dynamic_slice_in_dim(segments, start, rows_block, 0)
        scores = (
            jnp.einsum("qhd,khd->hqk", query_block, key_heads, preferred_element_type=jnp.float32)
            * scaling
        )
        allowed = (segment_block[:, None] == segments[None, :])[None, :, :]
        scores = jnp.where(allowed, scores, jnp.float32(-1e30))
        highest = jnp.max(scores, axis=2, keepdims=True)
        weights_exp = jnp.exp(scores - highest)
        totals = jnp.sum(weights_exp, axis=2)
        mixed = jnp.einsum(
            "hqk,khd->qhd",
            weights_exp.astype(jnp.bfloat16),
            value_heads,
            preferred_element_type=jnp.float32,
        )
        mixed = mixed / jnp.transpose(totals)[:, :, None]
        return mixed.astype(jnp.bfloat16)

    blocks = lax.map(attend_block, jnp.arange(length // rows_block))
    return blocks.reshape(length, head_count * HD)


def write_pages(keys, values, page_table):
    page_rows = keys.shape[0] // PAGE
    groups = lax.axis_size("req")
    per_group = page_rows // groups
    width = keys.shape[1]
    pages = jnp.stack(
        [keys.reshape(page_rows, PAGE, width), values.reshape(page_rows, PAGE, width)], axis=1
    )
    myself = lax.axis_index("req")
    whole_table = page_table.reshape(groups, page_rows)
    own_table = lax.dynamic_slice_in_dim(page_table, myself * page_rows, page_rows, 0)
    target = own_table // page_rows
    picked = (target[:, None] == jnp.arange(groups, dtype=jnp.int32)[None, :]).astype(jnp.int32)
    ranking = jnp.sum(jnp.cumsum(picked, axis=0) * picked, axis=1) - 1
    outgoing = jnp.zeros_like(pages).at[target * per_group + ranking].set(pages)
    incoming = lax.all_to_all(
        outgoing.reshape(groups, per_group, 2, PAGE, width),
        "req",
        split_axis=0,
        concat_axis=0,
        tiled=True,
    )
    arriving = whole_table // page_rows == myself
    arrival_rank = jnp.cumsum(arriving.astype(jnp.int32), axis=1) - 1
    placing = jnp.where(
        arriving, jnp.arange(groups, dtype=jnp.int32)[:, None] * per_group + arrival_rank, page_rows
    )
    slot_table = (
        jnp.zeros((page_rows + 1,), jnp.int32)
        .at[placing.reshape(-1)]
        .set((whole_table % page_rows).reshape(-1))
    )
    slot_table = slot_table[:page_rows]
    return jnp.zeros_like(pages).at[slot_table].set(incoming.reshape(page_rows, 2, PAGE, width))


def whole_experts(w_gate, w_up, w_down):
    local_halves = w_gate.shape[0]
    half_units = w_gate.shape[2]
    if local_halves == 1:
        packed = jnp.stack([w_gate[0], w_up[0], w_down[0].reshape(D, half_units)])
        partner = from_partner(packed, "exp", 0)
        leading = lax.axis_index("exp") % 2 == 0
        first = jnp.where(leading, packed, partner)
        second = jnp.where(leading, partner, packed)
        gate_full = jnp.stack([first[0], second[0]])[None]
        up_full = jnp.stack([first[1], second[1]])[None]
        down_full = jnp.stack([first[2].reshape(half_units, D), second[2].reshape(half_units, D)])[
            None
        ]
        return (gate_full, up_full, down_full, 1)
    gate_full = w_gate.reshape(local_halves // 2, 2, D, half_units)
    up_full = w_up.reshape(local_halves // 2, 2, D, half_units)
    down_full = w_down.reshape(local_halves // 2, 2, half_units, D)
    return (gate_full, up_full, down_full, 2)


def on_device_split(
    stream_in,
    queries,
    keys,
    values,
    out_weight,
    norm_gain,
    w_gate,
    w_up,
    w_down,
    combine,
    segment_ids,
    routes,
    page_table,
):
    attended = attend_rows(queries, keys, values, segment_ids[0])
    kv_cache = write_pages(keys, values, page_table)
    tok_rows = stream_in.shape[0]
    projected = lax.psum_scatter(
        jnp.dot(attended, out_weight, preferred_element_type=jnp.float32),
        "exp",
        scatter_dimension=0,
        tiled=True,
    )
    residual = stream_in.astype(jnp.float32) + projected
    scale_rows = lax.rsqrt(jnp.mean(residual * residual, axis=1, keepdims=True) + 1e-06)
    normed = (residual * scale_rows * norm_gain).astype(jnp.bfloat16)
    expert_ids = routes.reshape(-1)
    owners = (expert_ids[:, None] == jnp.arange(EXPERTS, dtype=jnp.int32)[None, :]).astype(
        jnp.int32
    )
    ranking = jnp.sum(jnp.cumsum(owners, axis=0) * owners, axis=1) - 1
    pair_rows = jnp.repeat(normed, TOPK, axis=0)
    devices = lax.axis_size(("req", "exp"))
    local_halves = w_gate.shape[0]
    slots = (MOST + 1) // 2
    holder = 2 * expert_ids + ranking % 2
    position = ranking // 2
    outgoing = jnp.zeros((devices * local_halves * slots, D), jnp.bfloat16)
    outgoing = outgoing.at[holder * slots + position].set(pair_rows)
    gate_full, up_full, down_full, copies = whole_experts(w_gate, w_up, w_down)
    local_experts = gate_full.shape[0]
    arrived = lax.all_to_all(
        outgoing.reshape(devices, local_halves, slots, D),
        ("req", "exp"),
        split_axis=0,
        concat_axis=0,
        tiled=True,
    )
    count = arrived.shape[2]
    grouped = arrived.reshape(devices, local_experts, copies, count, D)
    gate_val = jnp.einsum(
        "sercd,ejdf->serjcf", grouped, gate_full, preferred_element_type=jnp.float32
    )
    up_val = jnp.einsum("sercd,ejdf->serjcf", grouped, up_full, preferred_element_type=jnp.float32)
    activated = (jax.nn.silu(gate_val) * up_val).astype(jnp.bfloat16)
    halves_out = jnp.einsum(
        "serjcf,ejfd->serjcd", activated, down_full, preferred_element_type=jnp.float32
    ).astype(jnp.bfloat16)
    returned = lax.all_to_all(
        halves_out.reshape(devices, local_halves, 2, count, D),
        ("req", "exp"),
        split_axis=0,
        concat_axis=0,
        tiled=True,
    )
    flat_back = returned.reshape(devices * local_halves, 2, slots, D)
    combined = flat_back[holder, 0, position].astype(jnp.float32) + flat_back[
        holder, 1, position
    ].astype(jnp.float32)
    weighted = combined * combine.reshape(-1)[:, None]
    expert_sum = jnp.sum(weighted.reshape(tok_rows, TOPK, D), axis=1)
    layer_out = (residual + expert_sum).astype(jnp.bfloat16)
    return (layer_out, kv_cache)


PLANES = 4


def strictly_lower(size):
    return jnp.asarray(np.tril(np.ones((size, size), np.float32), -1), jnp.bfloat16)


def count_before(flags):
    return jnp.dot(
        strictly_lower(flags.shape[0]),
        flags.astype(jnp.bfloat16),
        preferred_element_type=jnp.float32,
    )


def move_pages(keys, values, page_table, after):
    rows, width = keys.shape
    page_rows = rows // PAGE
    groups = lax.axis_size("req")
    per_group = page_rows // groups
    myself = lax.axis_index("req")
    whole_table = page_table.reshape(groups, page_rows)
    own_table = lax.dynamic_slice_in_dim(page_table, myself * page_rows, page_rows, 0)
    target = own_table // page_rows
    picked = target[:, None] == jnp.arange(groups, dtype=jnp.int32)[None, :]
    ranking = jnp.sum(jnp.where(picked, count_before(picked), 0.0), axis=1).astype(jnp.int32)
    slot = (target ^ myself) * per_group + ranking
    within = jnp.arange(PAGE, dtype=jnp.int32)
    lines = jnp.arange(rows, dtype=jnp.int32)
    target_line = (slot[:, None] * PAGE + within[None, :]).reshape(-1, 128)
    target_line = tie(target_line, after).reshape(-1)
    spread = (target_line[None, :] == lines[:, None]).astype(jnp.bfloat16)
    both = jnp.concatenate([keys, values], axis=1)
    sent = jnp.dot(spread, both, preferred_element_type=jnp.float32).astype(jnp.bfloat16)
    sent = sent.reshape(groups, rows // groups, 2 * width)
    incoming = [sent[0]]
    for apart in range(1, groups):
        pairs = [(low, low ^ apart) for low in range(groups)]
        incoming.append(lax.ppermute(sent[apart], "req", pairs))

    arriving = whole_table // page_rows == myself
    arrival = count_before(arriving.T).T.astype(jnp.int32)
    apart = jnp.arange(groups, dtype=jnp.int32)[:, None] ^ myself
    source = apart * per_group + arrival
    landing = jnp.where(arriving, whole_table % page_rows, -1).reshape(-1)
    slots = jnp.arange(page_rows, dtype=jnp.int32)
    source_page = jnp.sum(
        jnp.where(landing[None, :] == slots[:, None], source.reshape(-1)[None, :], 0), axis=1
    )
    source_line = (source_page[:, None] * PAGE + within[None, :]).reshape(-1)
    collect = (source_line[:, None] == lines[None, :]).astype(jnp.bfloat16)
    placed = jnp.dot(
        collect, jnp.concatenate(incoming, axis=0), preferred_element_type=jnp.float32
    ).astype(jnp.bfloat16)
    placed = placed.reshape(page_rows, PAGE, 2, width)
    return jnp.transpose(placed, (0, 2, 1, 3))


def attend_kernel(query_ref, key_ref, value_ref, line_ref, row_ref, out_ref):
    allowed = line_ref[...] == row_ref[...]
    half = out_ref.shape[1]
    scaling = 1.0 / math.sqrt(HD)
    for head in range(query_ref.shape[1] // HD):
        span = slice(head * HD, (head + 1) * HD)
        scores = lax.dot_general(
            query_ref[:, span],
            key_ref[:, span],
            (((1,), (1,)), ((), ())),
            preferred_element_type=jnp.float32,
        )
        scores = jnp.where(allowed, scores * scaling, jnp.float32(-1e30))
        weights = jnp.exp(scores - jnp.max(scores, axis=1, keepdims=True))
        totals = jnp.sum(weights, axis=1, keepdims=True)
        mixed = jnp.dot(
            weights.astype(jnp.bfloat16), value_ref[:, span], preferred_element_type=jnp.float32
        )
        mixed = (mixed / totals).astype(jnp.bfloat16)
        out_ref[0, :, span] = mixed[:half]
        out_ref[1, :, span] = mixed[half:]


def attend_columns(queries, keys, values, segments, tok_rows):
    rows, width = queries.shape
    block = 2 * tok_rows
    steps = rows // block
    return pl.pallas_call(
        attend_kernel,
        grid=(steps,),
        in_specs=[
            pl.BlockSpec((block, width), lambda i: (i, 0)),
            pl.BlockSpec((rows, width), lambda i: (0, 0)),
            pl.BlockSpec((rows, width), lambda i: (0, 0)),
            pl.BlockSpec((block, 1), lambda i: (i, 0)),
            pl.BlockSpec((1, rows), lambda i: (0, 0)),
        ],
        out_specs=pl.BlockSpec((2, tok_rows, width), lambda i: (0, i, 0)),
        out_shape=jax.ShapeDtypeStruct((2, rows // 2, width), jnp.bfloat16),
        compiler_params=pltpu.CompilerParams(vmem_limit_bytes=56 * 1024 * 1024),
        cost_estimate=pl.CostEstimate(
            flops=4 * rows * rows * width,
            bytes_accessed=8 * rows * width,
            transcendentals=rows * rows * width // HD,
        ),
    )(queries, keys, values, segments.reshape(rows, 1), segments.reshape(1, rows))


def partial_kernel(place_ref, mine_ref, other_ref, weight_ref, first_ref, rest_ref, out_ref, total):
    step = pl.program_id(0)
    total[...] = jnp.dot(mine_ref[0], weight_ref[...], preferred_element_type=jnp.float32)

    @pl.when(step < 2)
    def _():
        total[...] += jnp.dot(other_ref[...], first_ref[...], preferred_element_type=jnp.float32)

    @pl.when(step >= 2)
    def _():
        total[...] += jnp.dot(other_ref[...], rest_ref[...], preferred_element_type=jnp.float32)

    out_ref[...] = total[...].reshape(out_ref.shape).astype(jnp.bfloat16)


def partial_products(place, attended, other, out_weight, other_weight, other_rest):
    _, rows, width = attended.shape
    strip = D // 4
    column_of = lambda i, p: (i // 2 ^ p[1]) * 2 + i % 2
    return pl.pallas_call(
        partial_kernel,
        grid_spec=pltpu.PrefetchScalarGridSpec(
            num_scalar_prefetch=1,
            grid=(4,),
            in_specs=[
                pl.BlockSpec((1, rows, width), lambda i, p: (p[0], 0, 0)),
                pl.BlockSpec((rows, width), lambda i, p: (0, 0)),
                pl.BlockSpec((width, strip), lambda i, p: (0, column_of(i, p))),
                pl.BlockSpec((width, strip), lambda i, p: (0, jnp.minimum(i, 1))),
                pl.BlockSpec((width, strip), lambda i, p: (0, jnp.maximum(i - 2, 0))),
            ],
            out_specs=pl.BlockSpec(
                (PLANES, rows // PLANES, strip), lambda i, p: (0, 0, column_of(i, p))
            ),
            scratch_shapes=[pltpu.VMEM((rows, strip), jnp.float32)],
        ),
        out_shape=jax.ShapeDtypeStruct((PLANES, rows // PLANES, D), jnp.bfloat16),
        compiler_params=pltpu.CompilerParams(vmem_limit_bytes=40 * 1024 * 1024),
        cost_estimate=pl.CostEstimate(
            flops=4 * rows * width * D, bytes_accessed=2 * (rows + 2 * width) * D, transcendentals=0
        ),
    )(place, attended, other, out_weight, other_weight, other_rest)


def pack_rows(picking, block, shape):
    rows = jnp.dot(picking, block, preferred_element_type=jnp.float32)
    return rows.reshape(shape).astype(jnp.bfloat16)


def norm_kernel(*refs):
    stream_ref, parts_ref, gain_ref, picking_ref, normed_ref, residual_ref, packed_ref = refs[-7:]
    residual = stream_ref[...].astype(jnp.float32)
    for plane in range(PLANES):
        residual = residual + parts_ref[plane].astype(jnp.float32)
    residual_ref[...] = residual
    scale = lax.rsqrt(jnp.mean(residual * residual, axis=1, keepdims=True) + 1e-06)
    normed = (residual * scale * gain_ref[...]).astype(jnp.bfloat16)
    normed_ref[...] = normed
    packed_ref[:, 0] = pack_rows(
        picking_ref[...], normed, (packed_ref.shape[0],) + packed_ref.shape[2:]
    )


def norm_and_pack(after, stream_in, parts, norm_gain, picking, sources):
    tok_rows = stream_in.shape[0]
    height = picking.shape[0]
    operands = (stream_in, parts, norm_gain.reshape(1, D), picking)
    shapes = [
        jax.ShapeDtypeStruct((tok_rows, D), jnp.bfloat16),
        jax.ShapeDtypeStruct((tok_rows, D), jnp.float32),
        jax.ShapeDtypeStruct((sources, 1, height // sources, D), jnp.bfloat16),
    ]
    whole = lambda a: pl.BlockSpec(a.shape, lambda i, rank=len(a.shape): (0,) * rank)
    return pl.pallas_call(
        norm_kernel,
        grid=(1,),
        in_specs=[pl.BlockSpec(memory_space=pl.ANY)] * len(after) + [whole(a) for a in operands],
        out_specs=[whole(a) for a in shapes],
        out_shape=shapes,
        compiler_params=pltpu.CompilerParams(vmem_limit_bytes=40 * 1024 * 1024),
        cost_estimate=pl.CostEstimate(
            flops=2 * height * tok_rows * D + 10 * tok_rows * D,
            bytes_accessed=(16 * tok_rows + 2 * height) * D,
            transcendentals=tok_rows,
        ),
    )(*after, *operands)


def pack_kernel(after_ref, picking_ref, block_ref, out_ref):
    out_ref[:, 0] = pack_rows(
        picking_ref[...], block_ref[...], (out_ref.shape[0],) + out_ref.shape[2:]
    )


def pack_after(after, picking, block, sources, into=False):
    height, tok_rows = picking.shape
    parts = 2 if into else 1
    return pl.pallas_call(
        pack_kernel,
        grid=(1,),
        in_specs=[
            pl.BlockSpec(memory_space=pl.ANY),
            pl.BlockSpec((height, tok_rows), lambda i: (0, 0)),
            pl.BlockSpec((tok_rows, D), lambda i: (0, 0)),
        ],
        out_specs=pl.BlockSpec((sources, 1, height // sources, D), lambda i: (0, parts - 1, 0, 0)),
        out_shape=jax.ShapeDtypeStruct((sources, parts, height // sources, D), jnp.bfloat16),
        input_output_aliases={0: 0} if into else {},
        compiler_params=pltpu.CompilerParams(vmem_limit_bytes=40 * 1024 * 1024),
        cost_estimate=pl.CostEstimate(
            flops=2 * height * tok_rows * D, bytes_accessed=4 * height * D, transcendentals=0
        ),
    )(after, picking, block)


def tie_kernel(*refs):
    del refs


def tie(block, *after):
    return pl.pallas_call(
        tie_kernel,
        in_specs=[pl.BlockSpec(memory_space=pl.ANY)] * (1 + len(after)),
        out_specs=pl.BlockSpec(memory_space=pl.ANY),
        out_shape=jax.ShapeDtypeStruct(block.shape, block.dtype),
        input_output_aliases={0: 0},
    )(block, *after)


def expert_kernel(*refs):
    (rows_ref, order_ref, back_ref, gate_ref, up_ref, down_ref) = refs[-10:-4]
    out_ref, sorted_rows, total, outs = refs[-4:]
    step = pl.program_id(0)
    height, depth = sorted_rows.shape
    count = height // 2

    @pl.when(step == 0)
    def _():
        rows = rows_ref[:, 0].astype(jnp.float32).reshape(height, depth).astype(jnp.bfloat16)
        sorted_rows[...] = jnp.dot(
            order_ref[...], rows, preferred_element_type=jnp.float32
        ).astype(jnp.bfloat16)

    first = pl.multiple_of((step // 2) * count, 16)
    tokens = sorted_rows[pl.ds(first, count), :]
    gate_val = jnp.dot(tokens, gate_ref[0], preferred_element_type=jnp.float32)
    up_val = jnp.dot(tokens, up_ref[0], preferred_element_type=jnp.float32)
    activated = (gate_val / (1.0 + jnp.exp(-gate_val)) * up_val).astype(jnp.bfloat16)
    half_out = jnp.dot(activated, down_ref[0], preferred_element_type=jnp.float32)

    @pl.when(step % 2 == 0)
    def _():
        total[...] = half_out

    @pl.when(step % 2 == 1)
    def _():
        outs[pl.ds(first, count), :] = (total[...] + half_out).astype(jnp.bfloat16)

    @pl.when(step == 3)
    def _():
        out_ref[:, 0] = pack_rows(back_ref[...], outs[...], (out_ref.shape[0],) + out_ref.shape[2:])


def run_experts(after, arrived, w_gate, w_up, w_down, out_parts=1):
    sources, parts, slots, depth = arrived.shape
    units = w_gate.shape[2]
    height = sources * slots
    index = np.arange(height)
    wanted = (
        index % (height // 2) // (slots // 2) * slots
        + index // (height // 2) * (slots // 2)
        + index % (slots // 2)
    )
    order = (wanted[:, None] == index[None, :]).astype(np.float32)
    fixed = lambda i: (0, 0)
    return pl.pallas_call(
        expert_kernel,
        grid=(4,),
        in_specs=[pl.BlockSpec(memory_space=pl.ANY)] * len(after)
        + [
            pl.BlockSpec((sources, 1, slots, depth), lambda i: (0, parts - 1, 0, 0)),
            pl.BlockSpec((height, height), fixed),
            pl.BlockSpec((height, height), fixed),
            pl.BlockSpec((1, depth, units), lambda i: (i, 0, 0)),
            pl.BlockSpec((1, depth, units), lambda i: (i, 0, 0)),
            pl.BlockSpec((1, units, depth), lambda i: (i, 0, 0)),
        ],
        out_specs=pl.BlockSpec((sources, 1, slots, depth), lambda i: (0, 0, 0, 0)),
        out_shape=jax.ShapeDtypeStruct((sources, out_parts, slots, depth), jnp.bfloat16),
        scratch_shapes=[
            pltpu.VMEM((height, depth), jnp.bfloat16),
            pltpu.VMEM((height // 2, depth), jnp.float32),
            pltpu.VMEM((height, depth), jnp.bfloat16),
        ],
        compiler_params=pltpu.CompilerParams(vmem_limit_bytes=56 * 1024 * 1024),
        cost_estimate=pl.CostEstimate(
            flops=12 * height * depth * units + 4 * height * height * depth,
            bytes_accessed=12 * depth * units * 2 + 4 * height * depth,
            transcendentals=2 * height * units,
        ),
    )(
        *after,
        arrived,
        jnp.asarray(order, jnp.bfloat16),
        jnp.asarray(order.T, jnp.bfloat16),
        w_gate,
        w_up,
        w_down,
    )


def on_device_whole(
    stream_in,
    queries,
    keys,
    values,
    out_weight,
    norm_gain,
    w_gate,
    w_up,
    w_down,
    combine,
    segment_ids,
    routes,
    page_table,
):
    tok_rows = stream_in.shape[0]
    groups = lax.axis_size("req")
    lanes = lax.axis_size("x")
    sources = groups * lanes
    plane_experts = 2 * sources
    height = plane_experts * MOST
    level = lax.axis_index("z")
    column = lax.axis_index("x")
    swap = [(0, 1), (1, 0)]
    pairs = [[(low, low ^ turn) for low in range(PLANES)] for turn in range(PLANES)]

    core = lax.axis_index("req") % 2
    cores = [(low, low ^ 1) for low in range(groups)]
    half = lax.dynamic_slice_in_dim(out_weight, core * (D // 2), D // 2, 1)
    other_weight = lax.ppermute(half, "x", swap)
    attended = attend_columns(queries, keys, values, segment_ids[0], tok_rows)
    leaving = lax.dynamic_index_in_dim(attended, 1 - column, 0, keepdims=False)
    other = lax.ppermute(leaving, "x", swap)
    other_weight = tie(other_weight, attended)
    other_rest = lax.ppermute(other_weight, "req", cores)

    partial = partial_products(
        jnp.stack([column, core]).astype(jnp.int32),
        attended,
        other,
        out_weight,
        other_weight,
        other_rest,
    )

    routes = tie(routes, partial)
    matched = routes[:, :, None] == jnp.arange(EXPERTS, dtype=jnp.int32)[None, None, :]
    named = jnp.any(matched, axis=1)
    weight_of = jnp.sum(jnp.where(matched, combine[:, :, None], 0.0), axis=1)
    place = jnp.arange(EXPERTS, dtype=jnp.int32)
    in_plane = place // (PLANES * 2 * lanes) * (2 * lanes) + place % (2 * lanes)
    slot_of = jnp.where(named, count_before(named) + (in_plane * MOST)[None, :], -1.0)
    tables = jnp.stack([slot_of.T, weight_of.T])
    tables = tables.reshape(2, groups, PLANES, 2 * lanes, tok_rows)
    tables = jnp.transpose(tables, (2, 0, 1, 3, 4)).reshape(PLANES, 2, plane_experts, tok_rows)
    lines = jnp.arange(height, dtype=jnp.float32)
    pickings, mixings = [], []
    for turn in range(PLANES):
        table = lax.dynamic_index_in_dim(tables, level ^ turn, 0, keepdims=False)
        if turn:
            table = lax.ppermute(table, "z", pairs[turn])
        hits = table[0][:, None, :] == lines[None, :, None]
        pickings.append(jnp.sum(hits.astype(jnp.float32), axis=0).astype(jnp.bfloat16))
        mixing = jnp.sum(jnp.where(hits, table[1][:, None, :], 0.0), axis=0)
        high = mixing.astype(jnp.bfloat16)
        mixings.append((high, (mixing - high.astype(jnp.float32)).astype(jnp.bfloat16)))

    gathered = lax.all_to_all(partial, "z", split_axis=0, concat_axis=0, tiled=True)
    kv_cache = move_pages(keys, values, page_table, partial)
    normed, residual, packed = norm_and_pack(
        [kv_cache] + pickings[1:], stream_in, gathered, norm_gain, pickings[0], sources
    )

    def exchange(block):
        return lax.all_to_all(block, ("req", "x"), split_axis=0, concat_axis=0, tiled=True)

    def experts(after, arrived, out_parts=1):
        return run_experts(after, arrived, w_gate, w_up, w_down, out_parts)

    def mixed(turn, returned):
        return sum(
            lax.dot_general(
                part,
                returned[:, 0].reshape(height, D),
                (((0,), (0,)), ((), ())),
                preferred_element_type=jnp.float32,
            )
            for part in mixings[turn]
        )

    def to_plane(turn, block):
        return lax.ppermute(block, "z", pairs[turn])

    blocks = [normed] + [to_plane(turn, normed) for turn in range(1, PLANES)]
    own = exchange(packed)
    packed_first = pack_after(own, pickings[1], blocks[1], sources)
    first = exchange(packed_first)
    packed_third = pack_after(first, pickings[3], blocks[3], sources)
    third = exchange(packed_third)
    outs_first = experts([packed_third], first, 2)
    outs_first = pack_after(outs_first, pickings[2], blocks[2], sources, into=True)
    second = exchange(outs_first)
    outs_third = experts([outs_first], third)
    back_third = exchange(outs_third)
    share_first = mixed(1, second).astype(jnp.bfloat16)
    outs_second = experts([outs_third, share_first], second)
    got_first = to_plane(1, share_first)
    outs_second = tie(outs_second, got_first)
    back_second = exchange(outs_second)
    share_third = mixed(3, tie(back_third, outs_second)).astype(jnp.bfloat16)
    outs_own = experts([share_third], own)
    got_third = to_plane(3, share_third)
    outs_own = tie(outs_own, got_third)
    back_own = exchange(outs_own)
    share_second = mixed(2, tie(back_second, outs_own)).astype(jnp.bfloat16)
    got_second = to_plane(2, share_second)
    total = residual + got_first.astype(jnp.float32) + got_third.astype(jnp.float32)
    total = total + mixed(0, back_own) + got_second.astype(jnp.float32)
    return (total.astype(jnp.bfloat16), kv_cache)


def solution(mesh):
    requests, members = mesh.shape["req"], mesh.shape["exp"]
    whole = 2 * EXPERTS == 4 * requests * members and members == 2 * PLANES
    if whole:
        grid = mesh.devices.reshape(requests, PLANES, members // PLANES)
        mesh = Mesh(grid, ("req", "z", "x"))
    exp = ("z", "x") if whole else "exp"
    every = ("req", "z", "x") if whole else ("req", "exp")
    return jax.shard_map(
        on_device_whole if whole else on_device_split,
        mesh=mesh,
        in_specs=(
            P(every, None),
            P("req", exp),
            P("req", exp),
            P("req", exp),
            P(exp, None),
            P(),
            P(every, None, None),
            P(every, None, None),
            P(every, None, None),
            P(every, None),
            P("req", None),
            P(every, None),
            P(),
        ),
        out_specs=(P(every, None), P("req", None, None, exp)),
        check_vma=False,
    )
```

```python
import math

import jax
import jax.numpy as jnp
import numpy as np
from jax import lax
from jax.experimental import pallas as pl
from jax.experimental.pallas import tpu as pltpu
from jax.sharding import Mesh
from jax.sharding import PartitionSpec as P

D = 2048
HD = 128
EXPERTS = 64
TOPK = 8
PAGE = 16
MOST = 20


def from_partner(block, axis, distance):
    count = lax.axis_size(axis)
    route = []
    for low in range(count):
        high = low | 1 << distance
        if high != low and high < count:
            route += [(low, high), (high, low)]
    return lax.ppermute(block, axis, route)


def attend_rows(queries, keys, values, segments):
    length = queries.shape[0]
    head_count = queries.shape[1] // HD
    query_heads = queries.reshape(length, head_count, HD)
    key_heads = keys.reshape(length, head_count, HD)
    value_heads = values.reshape(length, head_count, HD)
    scaling = 1.0 / math.sqrt(HD)
    rows_block = min(512, length)

    def attend_block(position):
        start = position * rows_block
        query_block = lax.dynamic_slice_in_dim(query_heads, start, rows_block, 0)
        segment_block = lax.dynamic_slice_in_dim(segments, start, rows_block, 0)
        scores = (
            jnp.einsum("qhd,khd->hqk", query_block, key_heads, preferred_element_type=jnp.float32)
            * scaling
        )
        allowed = (segment_block[:, None] == segments[None, :])[None, :, :]
        scores = jnp.where(allowed, scores, jnp.float32(-1e30))
        highest = jnp.max(scores, axis=2, keepdims=True)
        weights_exp = jnp.exp(scores - highest)
        totals = jnp.sum(weights_exp, axis=2)
        mixed = jnp.einsum(
            "hqk,khd->qhd",
            weights_exp.astype(jnp.bfloat16),
            value_heads,
            preferred_element_type=jnp.float32,
        )
        mixed = mixed / jnp.transpose(totals)[:, :, None]
        return mixed.astype(jnp.bfloat16)

    blocks = lax.map(attend_block, jnp.arange(length // rows_block))
    return blocks.reshape(length, head_count * HD)


def write_pages(keys, values, page_table):
    page_rows = keys.shape[0] // PAGE
    groups = lax.axis_size("req")
    per_group = page_rows // groups
    width = keys.shape[1]
    pages = jnp.stack(
        [keys.reshape(page_rows, PAGE, width), values.reshape(page_rows, PAGE, width)], axis=1
    )
    myself = lax.axis_index("req")
    whole_table = page_table.reshape(groups, page_rows)
    own_table = lax.dynamic_slice_in_dim(page_table, myself * page_rows, page_rows, 0)
    target = own_table // page_rows
    picked = (target[:, None] == jnp.arange(groups, dtype=jnp.int32)[None, :]).astype(jnp.int32)
    ranking = jnp.sum(jnp.cumsum(picked, axis=0) * picked, axis=1) - 1
    outgoing = jnp.zeros_like(pages).at[target * per_group + ranking].set(pages)
    incoming = lax.all_to_all(
        outgoing.reshape(groups, per_group, 2, PAGE, width),
        "req",
        split_axis=0,
        concat_axis=0,
        tiled=True,
    )
    arriving = whole_table // page_rows == myself
    arrival_rank = jnp.cumsum(arriving.astype(jnp.int32), axis=1) - 1
    placing = jnp.where(
        arriving, jnp.arange(groups, dtype=jnp.int32)[:, None] * per_group + arrival_rank, page_rows
    )
    slot_table = (
        jnp.zeros((page_rows + 1,), jnp.int32)
        .at[placing.reshape(-1)]
        .set((whole_table % page_rows).reshape(-1))
    )
    slot_table = slot_table[:page_rows]
    return jnp.zeros_like(pages).at[slot_table].set(incoming.reshape(page_rows, 2, PAGE, width))


def whole_experts(w_gate, w_up, w_down):
    local_halves = w_gate.shape[0]
    half_units = w_gate.shape[2]
    if local_halves == 1:
        packed = jnp.stack([w_gate[0], w_up[0], w_down[0].reshape(D, half_units)])
        partner = from_partner(packed, "exp", 0)
        leading = lax.axis_index("exp") % 2 == 0
        first = jnp.where(leading, packed, partner)
        second = jnp.where(leading, partner, packed)
        gate_full = jnp.stack([first[0], second[0]])[None]
        up_full = jnp.stack([first[1], second[1]])[None]
        down_full = jnp.stack([first[2].reshape(half_units, D), second[2].reshape(half_units, D)])[
            None
        ]
        return (gate_full, up_full, down_full, 1)
    gate_full = w_gate.reshape(local_halves // 2, 2, D, half_units)
    up_full = w_up.reshape(local_halves // 2, 2, D, half_units)
    down_full = w_down.reshape(local_halves // 2, 2, half_units, D)
    return (gate_full, up_full, down_full, 2)


def on_device_split(
    stream_in,
    queries,
    keys,
    values,
    out_weight,
    norm_gain,
    w_gate,
    w_up,
    w_down,
    combine,
    segment_ids,
    routes,
    page_table,
):
    attended = attend_rows(queries, keys, values, segment_ids[0])
    kv_cache = write_pages(keys, values, page_table)
    tok_rows = stream_in.shape[0]
    projected = lax.psum_scatter(
        jnp.dot(attended, out_weight, preferred_element_type=jnp.float32),
        "exp",
        scatter_dimension=0,
        tiled=True,
    )
    residual = stream_in.astype(jnp.float32) + projected
    scale_rows = lax.rsqrt(jnp.mean(residual * residual, axis=1, keepdims=True) + 1e-06)
    normed = (residual * scale_rows * norm_gain).astype(jnp.bfloat16)
    expert_ids = routes.reshape(-1)
    owners = (expert_ids[:, None] == jnp.arange(EXPERTS, dtype=jnp.int32)[None, :]).astype(
        jnp.int32
    )
    ranking = jnp.sum(jnp.cumsum(owners, axis=0) * owners, axis=1) - 1
    pair_rows = jnp.repeat(normed, TOPK, axis=0)
    devices = lax.axis_size(("req", "exp"))
    local_halves = w_gate.shape[0]
    slots = (MOST + 1) // 2
    holder = 2 * expert_ids + ranking % 2
    position = ranking // 2
    outgoing = jnp.zeros((devices * local_halves * slots, D), jnp.bfloat16)
    outgoing = outgoing.at[holder * slots + position].set(pair_rows)
    gate_full, up_full, down_full, copies = whole_experts(w_gate, w_up, w_down)
    local_experts = gate_full.shape[0]
    arrived = lax.all_to_all(
        outgoing.reshape(devices, local_halves, slots, D),
        ("req", "exp"),
        split_axis=0,
        concat_axis=0,
        tiled=True,
    )
    count = arrived.shape[2]
    grouped = arrived.reshape(devices, local_experts, copies, count, D)
    gate_val = jnp.einsum(
        "sercd,ejdf->serjcf", grouped, gate_full, preferred_element_type=jnp.float32
    )
    up_val = jnp.einsum("sercd,ejdf->serjcf", grouped, up_full, preferred_element_type=jnp.float32)
    activated = (jax.nn.silu(gate_val) * up_val).astype(jnp.bfloat16)
    halves_out = jnp.einsum(
        "serjcf,ejfd->serjcd", activated, down_full, preferred_element_type=jnp.float32
    ).astype(jnp.bfloat16)
    returned = lax.all_to_all(
        halves_out.reshape(devices, local_halves, 2, count, D),
        ("req", "exp"),
        split_axis=0,
        concat_axis=0,
        tiled=True,
    )
    flat_back = returned.reshape(devices * local_halves, 2, slots, D)
    combined = flat_back[holder, 0, position].astype(jnp.float32) + flat_back[
        holder, 1, position
    ].astype(jnp.float32)
    weighted = combined * combine.reshape(-1)[:, None]
    expert_sum = jnp.sum(weighted.reshape(tok_rows, TOPK, D), axis=1)
    layer_out = (residual + expert_sum).astype(jnp.bfloat16)
    return (layer_out, kv_cache)


PLANES = 4


def strictly_lower(size):
    return jnp.asarray(np.tril(np.ones((size, size), np.float32), -1), jnp.bfloat16)


def count_before(flags):
    return jnp.dot(
        strictly_lower(flags.shape[0]),
        flags.astype(jnp.bfloat16),
        preferred_element_type=jnp.float32,
    )


def move_pages(keys, values, page_table, after):
    rows, width = keys.shape
    page_rows = rows // PAGE
    groups = lax.axis_size("req")
    per_group = page_rows // groups
    myself = lax.axis_index("req")
    whole_table = page_table.reshape(groups, page_rows)
    own_table = lax.dynamic_slice_in_dim(page_table, myself * page_rows, page_rows, 0)
    target = own_table // page_rows
    picked = target[:, None] == jnp.arange(groups, dtype=jnp.int32)[None, :]
    ranking = jnp.sum(jnp.where(picked, count_before(picked), 0.0), axis=1).astype(jnp.int32)
    slot = (target ^ myself) * per_group + ranking
    within = jnp.arange(PAGE, dtype=jnp.int32)
    lines = jnp.arange(rows, dtype=jnp.int32)
    target_line = (slot[:, None] * PAGE + within[None, :]).reshape(-1, 128)
    target_line = tie(target_line, after).reshape(-1)
    spread = (target_line[None, :] == lines[:, None]).astype(jnp.bfloat16)
    both = jnp.concatenate([keys, values], axis=1)
    sent = jnp.dot(spread, both, preferred_element_type=jnp.float32).astype(jnp.bfloat16)
    sent = sent.reshape(groups, rows // groups, 2 * width)
    incoming = [sent[0]]
    for apart in range(1, groups):
        pairs = [(low, low ^ apart) for low in range(groups)]
        incoming.append(lax.ppermute(sent[apart], "req", pairs))

    arriving = whole_table // page_rows == myself
    arrival = count_before(arriving.T).T.astype(jnp.int32)
    apart = jnp.arange(groups, dtype=jnp.int32)[:, None] ^ myself
    source = apart * per_group + arrival
    landing = jnp.where(arriving, whole_table % page_rows, -1).reshape(-1)
    slots = jnp.arange(page_rows, dtype=jnp.int32)
    source_page = jnp.sum(
        jnp.where(landing[None, :] == slots[:, None], source.reshape(-1)[None, :], 0), axis=1
    )
    source_line = (source_page[:, None] * PAGE + within[None, :]).reshape(-1)
    collect = (source_line[:, None] == lines[None, :]).astype(jnp.bfloat16)
    placed = jnp.dot(
        collect, jnp.concatenate(incoming, axis=0), preferred_element_type=jnp.float32
    ).astype(jnp.bfloat16)
    placed = placed.reshape(page_rows, PAGE, 2, width)
    return jnp.transpose(placed, (0, 2, 1, 3))


def attend_kernel(query_ref, key_ref, value_ref, line_ref, row_ref, out_ref):
    allowed = line_ref[...] == row_ref[...]
    half = out_ref.shape[1]
    scaling = 1.0 / math.sqrt(HD)
    for head in range(query_ref.shape[1] // HD):
        span = slice(head * HD, (head + 1) * HD)
        scores = lax.dot_general(
            query_ref[:, span],
            key_ref[:, span],
            (((1,), (1,)), ((), ())),
            preferred_element_type=jnp.float32,
        )
        scores = jnp.where(allowed, scores * scaling, jnp.float32(-1e30))
        weights = jnp.exp(scores - jnp.max(scores, axis=1, keepdims=True))
        totals = jnp.sum(weights, axis=1, keepdims=True)
        mixed = jnp.dot(
            weights.astype(jnp.bfloat16), value_ref[:, span], preferred_element_type=jnp.float32
        )
        mixed = (mixed / totals).astype(jnp.bfloat16)
        out_ref[0, :, span] = mixed[:half]
        out_ref[1, :, span] = mixed[half:]


def attend_columns(queries, keys, values, segments, tok_rows):
    rows, width = queries.shape
    block = 2 * tok_rows
    steps = rows // block
    return pl.pallas_call(
        attend_kernel,
        grid=(steps,),
        in_specs=[
            pl.BlockSpec((block, width), lambda i: (i, 0)),
            pl.BlockSpec((rows, width), lambda i: (0, 0)),
            pl.BlockSpec((rows, width), lambda i: (0, 0)),
            pl.BlockSpec((block, 1), lambda i: (i, 0)),
            pl.BlockSpec((1, rows), lambda i: (0, 0)),
        ],
        out_specs=pl.BlockSpec((2, tok_rows, width), lambda i: (0, i, 0)),
        out_shape=jax.ShapeDtypeStruct((2, rows // 2, width), jnp.bfloat16),
        compiler_params=pltpu.CompilerParams(vmem_limit_bytes=40 * 1024 * 1024),
        cost_estimate=pl.CostEstimate(
            flops=4 * rows * rows * width,
            bytes_accessed=8 * rows * width,
            transcendentals=rows * rows * width // HD,
        ),
    )(queries, keys, values, segments.reshape(rows, 1), segments.reshape(1, rows))


def partial_kernel(place_ref, mine_ref, other_ref, weight_ref, first_ref, rest_ref, out_ref, total):
    step = pl.program_id(0)
    total[...] = jnp.dot(mine_ref[0], weight_ref[...], preferred_element_type=jnp.float32)

    @pl.when(step < 2)
    def _():
        total[...] += jnp.dot(other_ref[...], first_ref[...], preferred_element_type=jnp.float32)

    @pl.when(step >= 2)
    def _():
        total[...] += jnp.dot(other_ref[...], rest_ref[...], preferred_element_type=jnp.float32)

    out_ref[...] = total[...].reshape(out_ref.shape).astype(jnp.bfloat16)


def partial_products(place, attended, other, out_weight, other_weight, other_rest):
    _, rows, width = attended.shape
    strip = D // 4
    column_of = lambda i, p: (i // 2 ^ p[1]) * 2 + i % 2
    return pl.pallas_call(
        partial_kernel,
        grid_spec=pltpu.PrefetchScalarGridSpec(
            num_scalar_prefetch=1,
            grid=(4,),
            in_specs=[
                pl.BlockSpec((1, rows, width), lambda i, p: (p[0], 0, 0)),
                pl.BlockSpec((rows, width), lambda i, p: (0, 0)),
                pl.BlockSpec((width, strip), lambda i, p: (0, column_of(i, p))),
                pl.BlockSpec((width, strip), lambda i, p: (0, jnp.minimum(i, 1))),
                pl.BlockSpec((width, strip), lambda i, p: (0, jnp.maximum(i - 2, 0))),
            ],
            out_specs=pl.BlockSpec(
                (PLANES, rows // PLANES, strip), lambda i, p: (0, 0, column_of(i, p))
            ),
            scratch_shapes=[pltpu.VMEM((rows, strip), jnp.float32)],
        ),
        out_shape=jax.ShapeDtypeStruct((PLANES, rows // PLANES, D), jnp.bfloat16),
        compiler_params=pltpu.CompilerParams(vmem_limit_bytes=40 * 1024 * 1024),
        cost_estimate=pl.CostEstimate(
            flops=4 * rows * width * D, bytes_accessed=2 * (rows + 2 * width) * D, transcendentals=0
        ),
    )(place, attended, other, out_weight, other_weight, other_rest)


def pack_rows(picking, block, shape):
    rows = jnp.dot(picking, block, preferred_element_type=jnp.float32)
    return rows.reshape(shape).astype(jnp.bfloat16)


def norm_kernel(*refs):
    stream_ref, parts_ref, gain_ref, picking_ref, normed_ref, residual_ref, packed_ref = refs[-7:]
    residual = stream_ref[...].astype(jnp.float32)
    for plane in range(PLANES):
        residual = residual + parts_ref[plane].astype(jnp.float32)
    residual_ref[...] = residual
    scale = lax.rsqrt(jnp.mean(residual * residual, axis=1, keepdims=True) + 1e-06)
    normed = (residual * scale * gain_ref[...]).astype(jnp.bfloat16)
    normed_ref[...] = normed
    packed_ref[:, 0] = pack_rows(
        picking_ref[...], normed, (packed_ref.shape[0],) + packed_ref.shape[2:]
    )


def norm_and_pack(after, stream_in, parts, norm_gain, picking, sources):
    tok_rows = stream_in.shape[0]
    height = picking.shape[0]
    operands = (stream_in, parts, norm_gain.reshape(1, D), picking)
    shapes = [
        jax.ShapeDtypeStruct((tok_rows, D), jnp.bfloat16),
        jax.ShapeDtypeStruct((tok_rows, D), jnp.float32),
        jax.ShapeDtypeStruct((sources, 1, height // sources, D), jnp.bfloat16),
    ]
    whole = lambda a: pl.BlockSpec(a.shape, lambda i, rank=len(a.shape): (0,) * rank)
    return pl.pallas_call(
        norm_kernel,
        grid=(1,),
        in_specs=[pl.BlockSpec(memory_space=pl.ANY)] * len(after) + [whole(a) for a in operands],
        out_specs=[whole(a) for a in shapes],
        out_shape=shapes,
        compiler_params=pltpu.CompilerParams(vmem_limit_bytes=40 * 1024 * 1024),
        cost_estimate=pl.CostEstimate(
            flops=2 * height * tok_rows * D + 10 * tok_rows * D,
            bytes_accessed=(16 * tok_rows + 2 * height) * D,
            transcendentals=tok_rows,
        ),
    )(*after, *operands)


def pack_kernel(*refs):
    picking_ref, block_ref, out_ref = refs[-3:]
    out_ref[:, 0] = pack_rows(
        picking_ref[...], block_ref[...], (out_ref.shape[0],) + out_ref.shape[2:]
    )


def pack_after(after, picking, block, sources):
    height, tok_rows = picking.shape
    return pl.pallas_call(
        pack_kernel,
        grid=(1,),
        in_specs=[pl.BlockSpec(memory_space=pl.ANY)] * len(after)
        + [
            pl.BlockSpec((height, tok_rows), lambda i: (0, 0)),
            pl.BlockSpec((tok_rows, D), lambda i: (0, 0)),
        ],
        out_specs=pl.BlockSpec((sources, 1, height // sources, D), lambda i: (0, 0, 0, 0)),
        out_shape=jax.ShapeDtypeStruct((sources, 1, height // sources, D), jnp.bfloat16),
        compiler_params=pltpu.CompilerParams(vmem_limit_bytes=40 * 1024 * 1024),
        cost_estimate=pl.CostEstimate(
            flops=2 * height * tok_rows * D, bytes_accessed=4 * height * D, transcendentals=0
        ),
    )(*after, picking, block)


def tie_kernel(*refs):
    del refs


def tie(block, *after):
    return pl.pallas_call(
        tie_kernel,
        in_specs=[pl.BlockSpec(memory_space=pl.ANY)] * (1 + len(after)),
        out_specs=pl.BlockSpec(memory_space=pl.ANY),
        out_shape=jax.ShapeDtypeStruct(block.shape, block.dtype),
        input_output_aliases={0: 0},
    )(block, *after)


def expert_kernel(*refs):
    (rows_ref, order_ref, back_ref, gate_ref, up_ref, down_ref) = refs[-10:-4]
    out_ref, sorted_rows, total, outs = refs[-4:]
    step = pl.program_id(0)
    height, depth = sorted_rows.shape
    count = height // 2

    @pl.when(step == 0)
    def _():
        rows = rows_ref[:, 0].astype(jnp.float32).reshape(height, depth).astype(jnp.bfloat16)
        sorted_rows[...] = jnp.dot(
            order_ref[...], rows, preferred_element_type=jnp.float32
        ).astype(jnp.bfloat16)

    first = pl.multiple_of((step // 2) * count, 16)
    tokens = sorted_rows[pl.ds(first, count), :]
    gate_val = jnp.dot(tokens, gate_ref[0], preferred_element_type=jnp.float32)
    up_val = jnp.dot(tokens, up_ref[0], preferred_element_type=jnp.float32)
    activated = (gate_val / (1.0 + jnp.exp(-gate_val)) * up_val).astype(jnp.bfloat16)
    half_out = jnp.dot(activated, down_ref[0], preferred_element_type=jnp.float32)

    @pl.when(step % 2 == 0)
    def _():
        total[...] = half_out

    @pl.when(step % 2 == 1)
    def _():
        outs[pl.ds(first, count), :] = (total[...] + half_out).astype(jnp.bfloat16)

    @pl.when(step == 3)
    def _():
        out_ref[:, 0] = pack_rows(back_ref[...], outs[...], (out_ref.shape[0],) + out_ref.shape[2:])


def run_experts(after, arrived, w_gate, w_up, w_down):
    sources, _, slots, depth = arrived.shape
    units = w_gate.shape[2]
    height = sources * slots
    index = np.arange(height)
    wanted = (
        index % (height // 2) // (slots // 2) * slots
        + index // (height // 2) * (slots // 2)
        + index % (slots // 2)
    )
    order = (wanted[:, None] == index[None, :]).astype(np.float32)
    fixed = lambda i: (0, 0)
    return pl.pallas_call(
        expert_kernel,
        grid=(4,),
        in_specs=[pl.BlockSpec(memory_space=pl.ANY)] * len(after)
        + [
            pl.BlockSpec((sources, 1, slots, depth), lambda i: (0, 0, 0, 0)),
            pl.BlockSpec((height, height), fixed),
            pl.BlockSpec((height, height), fixed),
            pl.BlockSpec((1, depth, units), lambda i: (i, 0, 0)),
            pl.BlockSpec((1, depth, units), lambda i: (i, 0, 0)),
            pl.BlockSpec((1, units, depth), lambda i: (i, 0, 0)),
        ],
        out_specs=pl.BlockSpec((sources, 1, slots, depth), lambda i: (0, 0, 0, 0)),
        out_shape=jax.ShapeDtypeStruct((sources, 1, slots, depth), jnp.bfloat16),
        scratch_shapes=[
            pltpu.VMEM((height, depth), jnp.bfloat16),
            pltpu.VMEM((height // 2, depth), jnp.float32),
            pltpu.VMEM((height, depth), jnp.bfloat16),
        ],
        compiler_params=pltpu.CompilerParams(vmem_limit_bytes=56 * 1024 * 1024),
        cost_estimate=pl.CostEstimate(
            flops=12 * height * depth * units + 4 * height * height * depth,
            bytes_accessed=12 * depth * units * 2 + 4 * height * depth,
            transcendentals=2 * height * units,
        ),
    )(
        *after,
        arrived,
        jnp.asarray(order, jnp.bfloat16),
        jnp.asarray(order.T, jnp.bfloat16),
        w_gate,
        w_up,
        w_down,
    )


def on_device_whole(
    stream_in,
    queries,
    keys,
    values,
    out_weight,
    norm_gain,
    w_gate,
    w_up,
    w_down,
    combine,
    segment_ids,
    routes,
    page_table,
):
    tok_rows = stream_in.shape[0]
    groups = lax.axis_size("req")
    lanes = lax.axis_size("x")
    sources = groups * lanes
    plane_experts = 2 * sources
    height = plane_experts * MOST
    level = lax.axis_index("z")
    column = lax.axis_index("x")
    swap = [(0, 1), (1, 0)]
    pairs = [[(low, low ^ turn) for low in range(PLANES)] for turn in range(PLANES)]

    core = lax.axis_index("req") % 2
    cores = [(low, low ^ 1) for low in range(groups)]
    half = lax.dynamic_slice_in_dim(out_weight, core * (D // 2), D // 2, 1)
    other_weight = lax.ppermute(half, "x", swap)
    attended = attend_columns(queries, keys, values, segment_ids[0], tok_rows)
    leaving = lax.dynamic_index_in_dim(attended, 1 - column, 0, keepdims=False)
    other = lax.ppermute(leaving, "x", swap)
    other_weight = tie(other_weight, attended)
    other_rest = lax.ppermute(other_weight, "req", cores)

    partial = partial_products(
        jnp.stack([column, core]).astype(jnp.int32),
        attended,
        other,
        out_weight,
        other_weight,
        other_rest,
    )

    matched = routes[:, :, None] == jnp.arange(EXPERTS, dtype=jnp.int32)[None, None, :]
    named = jnp.any(matched, axis=1)
    weight_of = jnp.sum(jnp.where(matched, combine[:, :, None], 0.0), axis=1)
    place = jnp.arange(EXPERTS, dtype=jnp.int32)
    in_plane = place // (PLANES * 2 * lanes) * (2 * lanes) + place % (2 * lanes)
    slot_of = jnp.where(named, count_before(named) + (in_plane * MOST)[None, :], -1.0)
    tables = jnp.stack([slot_of.T, weight_of.T])
    tables = tables.reshape(2, groups, PLANES, 2 * lanes, tok_rows)
    tables = jnp.transpose(tables, (2, 0, 1, 3, 4)).reshape(PLANES, 2, plane_experts, tok_rows)
    lines = jnp.arange(height, dtype=jnp.float32)
    received = []
    for turn in range(PLANES):
        table = lax.dynamic_index_in_dim(tables, level ^ turn, 0, keepdims=False)
        received.append(lax.ppermute(table, "z", pairs[turn]) if turn else table)
    partial = tie(partial, *received[1:])
    pickings, mixings = [], []
    for table in received:
        hits = table[0][:, None, :] == lines[None, :, None]
        pickings.append(jnp.sum(hits.astype(jnp.float32), axis=0).astype(jnp.bfloat16))
        mixing = jnp.sum(jnp.where(hits, table[1][:, None, :], 0.0), axis=0)
        high = mixing.astype(jnp.bfloat16)
        mixings.append((high, (mixing - high.astype(jnp.float32)).astype(jnp.bfloat16)))

    gathered = lax.all_to_all(partial, "z", split_axis=0, concat_axis=0, tiled=True)
    kv_cache = move_pages(keys, values, page_table, partial)
    normed, residual, packed = norm_and_pack(
        [kv_cache] + pickings[1:], stream_in, gathered, norm_gain, pickings[0], sources
    )

    def exchange(block):
        return lax.all_to_all(block, ("req", "x"), split_axis=0, concat_axis=0, tiled=True)

    def experts(after, arrived):
        return run_experts(after, arrived, w_gate, w_up, w_down)

    def mixed(turn, returned):
        return sum(
            lax.dot_general(
                part,
                returned[:, 0].reshape(height, D),
                (((0,), (0,)), ((), ())),
                preferred_element_type=jnp.float32,
            )
            for part in mixings[turn]
        )

    def to_plane(turn, block):
        return lax.ppermute(block, "z", pairs[turn])

    blocks = [normed] + [to_plane(turn, normed) for turn in range(1, PLANES)]
    own = exchange(packed)
    packed_first = pack_after([own], pickings[1], blocks[1], sources)
    first = exchange(packed_first)
    outs_own = experts([packed_first], own)
    packed_third = pack_after([first, outs_own], pickings[3], blocks[3], sources)
    third = exchange(packed_third)
    outs_first = experts([packed_third], first)
    back_first = exchange(outs_first)
    outs_third = experts([outs_first], third)
    packed_second = pack_after([back_first], pickings[2], blocks[2], sources)
    second = exchange(packed_second)
    share_first = mixed(1, back_first).astype(jnp.bfloat16)
    got_first = to_plane(1, share_first)
    outs_third = tie(outs_third, second, got_first)
    back_third = exchange(outs_third)
    outs_second = experts([outs_third], second)
    share_third = mixed(3, back_third).astype(jnp.bfloat16)
    got_third = to_plane(3, share_third)
    back_second = exchange(tie(outs_second, back_third))
    share_second = mixed(2, back_second).astype(jnp.bfloat16)
    back_own = exchange(tie(outs_own, back_second, got_third))
    got_second = to_plane(2, share_second)
    total = residual + got_first.astype(jnp.float32) + got_third.astype(jnp.float32)
    total = total + mixed(0, back_own) + got_second.astype(jnp.float32)
    return (total.astype(jnp.bfloat16), kv_cache)


def solution(mesh):
    requests, members = mesh.shape["req"], mesh.shape["exp"]
    whole = 2 * EXPERTS == 4 * requests * members and members == 2 * PLANES
    if whole:
        grid = mesh.devices.reshape(requests, PLANES, members // PLANES)
        mesh = Mesh(grid, ("req", "z", "x"))
    exp = ("z", "x") if whole else "exp"
    every = ("req", "z", "x") if whole else ("req", "exp")
    return jax.shard_map(
        on_device_whole if whole else on_device_split,
        mesh=mesh,
        in_specs=(
            P(every, None),
            P("req", exp),
            P("req", exp),
            P("req", exp),
            P(exp, None),
            P(),
            P(every, None, None),
            P(every, None, None),
            P(every, None, None),
            P(every, None),
            P("req", None),
            P(every, None),
            P(),
        ),
        out_specs=(P(every, None), P("req", None, None, exp)),
        check_vma=False,
    )
```

```python
import math

import jax
import jax.numpy as jnp
import numpy as np
from jax import lax
from jax.experimental import pallas as pl
from jax.experimental.pallas import tpu as pltpu
from jax.sharding import Mesh
from jax.sharding import PartitionSpec as P

D = 2048
HD = 128
EXPERTS = 64
TOPK = 8
PAGE = 16
MOST = 20


def from_partner(block, axis, distance):
    count = lax.axis_size(axis)
    route = []
    for low in range(count):
        high = low | 1 << distance
        if high != low and high < count:
            route += [(low, high), (high, low)]
    return lax.ppermute(block, axis, route)


def attend_rows(queries, keys, values, segments):
    length = queries.shape[0]
    head_count = queries.shape[1] // HD
    query_heads = queries.reshape(length, head_count, HD)
    key_heads = keys.reshape(length, head_count, HD)
    value_heads = values.reshape(length, head_count, HD)
    scaling = 1.0 / math.sqrt(HD)
    rows_block = min(512, length)

    def attend_block(position):
        start = position * rows_block
        query_block = lax.dynamic_slice_in_dim(query_heads, start, rows_block, 0)
        segment_block = lax.dynamic_slice_in_dim(segments, start, rows_block, 0)
        scores = (
            jnp.einsum("qhd,khd->hqk", query_block, key_heads, preferred_element_type=jnp.float32)
            * scaling
        )
        allowed = (segment_block[:, None] == segments[None, :])[None, :, :]
        scores = jnp.where(allowed, scores, jnp.float32(-1e30))
        highest = jnp.max(scores, axis=2, keepdims=True)
        weights_exp = jnp.exp(scores - highest)
        totals = jnp.sum(weights_exp, axis=2)
        mixed = jnp.einsum(
            "hqk,khd->qhd",
            weights_exp.astype(jnp.bfloat16),
            value_heads,
            preferred_element_type=jnp.float32,
        )
        mixed = mixed / jnp.transpose(totals)[:, :, None]
        return mixed.astype(jnp.bfloat16)

    blocks = lax.map(attend_block, jnp.arange(length // rows_block))
    return blocks.reshape(length, head_count * HD)


def write_pages(keys, values, page_table):
    page_rows = keys.shape[0] // PAGE
    groups = lax.axis_size("req")
    per_group = page_rows // groups
    width = keys.shape[1]
    pages = jnp.stack(
        [keys.reshape(page_rows, PAGE, width), values.reshape(page_rows, PAGE, width)], axis=1
    )
    myself = lax.axis_index("req")
    whole_table = page_table.reshape(groups, page_rows)
    own_table = lax.dynamic_slice_in_dim(page_table, myself * page_rows, page_rows, 0)
    target = own_table // page_rows
    picked = (target[:, None] == jnp.arange(groups, dtype=jnp.int32)[None, :]).astype(jnp.int32)
    ranking = jnp.sum(jnp.cumsum(picked, axis=0) * picked, axis=1) - 1
    outgoing = jnp.zeros_like(pages).at[target * per_group + ranking].set(pages)
    incoming = lax.all_to_all(
        outgoing.reshape(groups, per_group, 2, PAGE, width),
        "req",
        split_axis=0,
        concat_axis=0,
        tiled=True,
    )
    arriving = whole_table // page_rows == myself
    arrival_rank = jnp.cumsum(arriving.astype(jnp.int32), axis=1) - 1
    placing = jnp.where(
        arriving, jnp.arange(groups, dtype=jnp.int32)[:, None] * per_group + arrival_rank, page_rows
    )
    slot_table = (
        jnp.zeros((page_rows + 1,), jnp.int32)
        .at[placing.reshape(-1)]
        .set((whole_table % page_rows).reshape(-1))
    )
    slot_table = slot_table[:page_rows]
    return jnp.zeros_like(pages).at[slot_table].set(incoming.reshape(page_rows, 2, PAGE, width))


def whole_experts(w_gate, w_up, w_down):
    local_halves = w_gate.shape[0]
    half_units = w_gate.shape[2]
    if local_halves == 1:
        packed = jnp.stack([w_gate[0], w_up[0], w_down[0].reshape(D, half_units)])
        partner = from_partner(packed, "exp", 0)
        leading = lax.axis_index("exp") % 2 == 0
        first = jnp.where(leading, packed, partner)
        second = jnp.where(leading, partner, packed)
        gate_full = jnp.stack([first[0], second[0]])[None]
        up_full = jnp.stack([first[1], second[1]])[None]
        down_full = jnp.stack([first[2].reshape(half_units, D), second[2].reshape(half_units, D)])[
            None
        ]
        return (gate_full, up_full, down_full, 1)
    gate_full = w_gate.reshape(local_halves // 2, 2, D, half_units)
    up_full = w_up.reshape(local_halves // 2, 2, D, half_units)
    down_full = w_down.reshape(local_halves // 2, 2, half_units, D)
    return (gate_full, up_full, down_full, 2)


def on_device_split(
    stream_in,
    queries,
    keys,
    values,
    out_weight,
    norm_gain,
    w_gate,
    w_up,
    w_down,
    combine,
    segment_ids,
    routes,
    page_table,
):
    attended = attend_rows(queries, keys, values, segment_ids[0])
    kv_cache = write_pages(keys, values, page_table)
    tok_rows = stream_in.shape[0]
    projected = lax.psum_scatter(
        jnp.dot(attended, out_weight, preferred_element_type=jnp.float32),
        "exp",
        scatter_dimension=0,
        tiled=True,
    )
    residual = stream_in.astype(jnp.float32) + projected
    scale_rows = lax.rsqrt(jnp.mean(residual * residual, axis=1, keepdims=True) + 1e-06)
    normed = (residual * scale_rows * norm_gain).astype(jnp.bfloat16)
    expert_ids = routes.reshape(-1)
    owners = (expert_ids[:, None] == jnp.arange(EXPERTS, dtype=jnp.int32)[None, :]).astype(
        jnp.int32
    )
    ranking = jnp.sum(jnp.cumsum(owners, axis=0) * owners, axis=1) - 1
    pair_rows = jnp.repeat(normed, TOPK, axis=0)
    devices = lax.axis_size(("req", "exp"))
    local_halves = w_gate.shape[0]
    slots = (MOST + 1) // 2
    holder = 2 * expert_ids + ranking % 2
    position = ranking // 2
    outgoing = jnp.zeros((devices * local_halves * slots, D), jnp.bfloat16)
    outgoing = outgoing.at[holder * slots + position].set(pair_rows)
    gate_full, up_full, down_full, copies = whole_experts(w_gate, w_up, w_down)
    local_experts = gate_full.shape[0]
    arrived = lax.all_to_all(
        outgoing.reshape(devices, local_halves, slots, D),
        ("req", "exp"),
        split_axis=0,
        concat_axis=0,
        tiled=True,
    )
    count = arrived.shape[2]
    grouped = arrived.reshape(devices, local_experts, copies, count, D)
    gate_val = jnp.einsum(
        "sercd,ejdf->serjcf", grouped, gate_full, preferred_element_type=jnp.float32
    )
    up_val = jnp.einsum("sercd,ejdf->serjcf", grouped, up_full, preferred_element_type=jnp.float32)
    activated = (jax.nn.silu(gate_val) * up_val).astype(jnp.bfloat16)
    halves_out = jnp.einsum(
        "serjcf,ejfd->serjcd", activated, down_full, preferred_element_type=jnp.float32
    ).astype(jnp.bfloat16)
    returned = lax.all_to_all(
        halves_out.reshape(devices, local_halves, 2, count, D),
        ("req", "exp"),
        split_axis=0,
        concat_axis=0,
        tiled=True,
    )
    flat_back = returned.reshape(devices * local_halves, 2, slots, D)
    combined = flat_back[holder, 0, position].astype(jnp.float32) + flat_back[
        holder, 1, position
    ].astype(jnp.float32)
    weighted = combined * combine.reshape(-1)[:, None]
    expert_sum = jnp.sum(weighted.reshape(tok_rows, TOPK, D), axis=1)
    layer_out = (residual + expert_sum).astype(jnp.bfloat16)
    return (layer_out, kv_cache)


PLANES = 4


def strictly_lower(size):
    return jnp.asarray(np.tril(np.ones((size, size), np.float32), -1), jnp.bfloat16)


def count_before(flags):
    return jnp.dot(
        strictly_lower(flags.shape[0]),
        flags.astype(jnp.bfloat16),
        preferred_element_type=jnp.float32,
    )


def move_pages(keys, values, page_table, after):
    rows, width = keys.shape
    page_rows = rows // PAGE
    groups = lax.axis_size("req")
    per_group = page_rows // groups
    myself = lax.axis_index("req")
    whole_table = page_table.reshape(groups, page_rows)
    own_table = lax.dynamic_slice_in_dim(page_table, myself * page_rows, page_rows, 0)
    target = own_table // page_rows
    picked = target[:, None] == jnp.arange(groups, dtype=jnp.int32)[None, :]
    ranking = jnp.sum(jnp.where(picked, count_before(picked), 0.0), axis=1).astype(jnp.int32)
    slot = (target ^ myself) * per_group + ranking
    within = jnp.arange(PAGE, dtype=jnp.int32)
    lines = jnp.arange(rows, dtype=jnp.int32)
    target_line = (slot[:, None] * PAGE + within[None, :]).reshape(-1, 128)
    target_line = tie(target_line, after).reshape(-1)
    spread = (target_line[None, :] == lines[:, None]).astype(jnp.bfloat16)
    both = jnp.concatenate([keys, values], axis=1)
    sent = jnp.dot(spread, both, preferred_element_type=jnp.float32).astype(jnp.bfloat16)
    sent = sent.reshape(groups, rows // groups, 2 * width)
    incoming = [sent[0]]
    for apart in range(1, groups):
        pairs = [(low, low ^ apart) for low in range(groups)]
        incoming.append(lax.ppermute(sent[apart], "req", pairs))

    arriving = whole_table // page_rows == myself
    arrival = count_before(arriving.T).T.astype(jnp.int32)
    apart = jnp.arange(groups, dtype=jnp.int32)[:, None] ^ myself
    source = apart * per_group + arrival
    landing = jnp.where(arriving, whole_table % page_rows, -1).reshape(-1)
    slots = jnp.arange(page_rows, dtype=jnp.int32)
    source_page = jnp.sum(
        jnp.where(landing[None, :] == slots[:, None], source.reshape(-1)[None, :], 0), axis=1
    )
    source_line = (source_page[:, None] * PAGE + within[None, :]).reshape(-1)
    collect = (source_line[:, None] == lines[None, :]).astype(jnp.bfloat16)
    placed = jnp.dot(
        collect, jnp.concatenate(incoming, axis=0), preferred_element_type=jnp.float32
    ).astype(jnp.bfloat16)
    placed = placed.reshape(page_rows, PAGE, 2, width)
    return jnp.transpose(placed, (0, 2, 1, 3))


def attend_kernel(query_ref, key_ref, value_ref, line_ref, row_ref, out_ref):
    allowed = line_ref[...] == row_ref[...]
    half = out_ref.shape[1]
    scaling = 1.0 / math.sqrt(HD)
    for head in range(query_ref.shape[1] // HD):
        span = slice(head * HD, (head + 1) * HD)
        scores = lax.dot_general(
            query_ref[:, span],
            key_ref[:, span],
            (((1,), (1,)), ((), ())),
            preferred_element_type=jnp.float32,
        )
        scores = jnp.where(allowed, scores * scaling, jnp.float32(-1e30))
        weights = jnp.exp(scores - jnp.max(scores, axis=1, keepdims=True))
        totals = jnp.sum(weights, axis=1, keepdims=True)
        mixed = jnp.dot(
            weights.astype(jnp.bfloat16), value_ref[:, span], preferred_element_type=jnp.float32
        )
        mixed = (mixed / totals).astype(jnp.bfloat16)
        out_ref[0, :, span] = mixed[:half]
        out_ref[1, :, span] = mixed[half:]


def attend_columns(queries, keys, values, segments, tok_rows):
    rows, width = queries.shape
    block = 2 * tok_rows
    steps = rows // block
    return pl.pallas_call(
        attend_kernel,
        grid=(steps,),
        in_specs=[
            pl.BlockSpec((block, width), lambda i: (i, 0)),
            pl.BlockSpec((rows, width), lambda i: (0, 0)),
            pl.BlockSpec((rows, width), lambda i: (0, 0)),
            pl.BlockSpec((block, 1), lambda i: (i, 0)),
            pl.BlockSpec((1, rows), lambda i: (0, 0)),
        ],
        out_specs=pl.BlockSpec((2, tok_rows, width), lambda i: (0, i, 0)),
        out_shape=jax.ShapeDtypeStruct((2, rows // 2, width), jnp.bfloat16),
        compiler_params=pltpu.CompilerParams(vmem_limit_bytes=40 * 1024 * 1024),
        cost_estimate=pl.CostEstimate(
            flops=4 * rows * rows * width,
            bytes_accessed=8 * rows * width,
            transcendentals=rows * rows * width // HD,
        ),
    )(queries, keys, values, segments.reshape(rows, 1), segments.reshape(1, rows))


def partial_kernel(place_ref, mine_ref, other_ref, weight_ref, first_ref, rest_ref, out_ref, total):
    step = pl.program_id(0)
    total[...] = jnp.dot(mine_ref[0], weight_ref[...], preferred_element_type=jnp.float32)

    @pl.when(step < 2)
    def _():
        total[...] += jnp.dot(other_ref[...], first_ref[...], preferred_element_type=jnp.float32)

    @pl.when(step >= 2)
    def _():
        total[...] += jnp.dot(other_ref[...], rest_ref[...], preferred_element_type=jnp.float32)

    out_ref[...] = total[...].reshape(out_ref.shape).astype(jnp.bfloat16)


def partial_products(place, attended, other, out_weight, other_weight, other_rest):
    _, rows, width = attended.shape
    strip = D // 4
    column_of = lambda i, p: (i // 2 ^ p[1]) * 2 + i % 2
    return pl.pallas_call(
        partial_kernel,
        grid_spec=pltpu.PrefetchScalarGridSpec(
            num_scalar_prefetch=1,
            grid=(4,),
            in_specs=[
                pl.BlockSpec((1, rows, width), lambda i, p: (p[0], 0, 0)),
                pl.BlockSpec((rows, width), lambda i, p: (0, 0)),
                pl.BlockSpec((width, strip), lambda i, p: (0, column_of(i, p))),
                pl.BlockSpec((width, strip), lambda i, p: (0, jnp.minimum(i, 1))),
                pl.BlockSpec((width, strip), lambda i, p: (0, jnp.maximum(i - 2, 0))),
            ],
            out_specs=pl.BlockSpec(
                (PLANES, rows // PLANES, strip), lambda i, p: (0, 0, column_of(i, p))
            ),
            scratch_shapes=[pltpu.VMEM((rows, strip), jnp.float32)],
        ),
        out_shape=jax.ShapeDtypeStruct((PLANES, rows // PLANES, D), jnp.bfloat16),
        compiler_params=pltpu.CompilerParams(vmem_limit_bytes=40 * 1024 * 1024),
        cost_estimate=pl.CostEstimate(
            flops=4 * rows * width * D, bytes_accessed=2 * (rows + 2 * width) * D, transcendentals=0
        ),
    )(place, attended, other, out_weight, other_weight, other_rest)


def pack_rows(picking, block, shape):
    rows = jnp.dot(picking, block, preferred_element_type=jnp.float32)
    return rows.reshape(shape).astype(jnp.bfloat16)


def norm_kernel(*refs):
    stream_ref, parts_ref, gain_ref, picking_ref, normed_ref, residual_ref, packed_ref = refs[-7:]
    residual = stream_ref[...].astype(jnp.float32)
    for plane in range(PLANES):
        residual = residual + parts_ref[plane].astype(jnp.float32)
    residual_ref[...] = residual
    scale = lax.rsqrt(jnp.mean(residual * residual, axis=1, keepdims=True) + 1e-06)
    normed = (residual * scale * gain_ref[...]).astype(jnp.bfloat16)
    normed_ref[...] = normed
    packed_ref[:, 0] = pack_rows(
        picking_ref[...], normed, (packed_ref.shape[0],) + packed_ref.shape[2:]
    )


def norm_and_pack(after, stream_in, parts, norm_gain, picking, sources):
    tok_rows = stream_in.shape[0]
    height = picking.shape[0]
    operands = (stream_in, parts, norm_gain.reshape(1, D), picking)
    shapes = [
        jax.ShapeDtypeStruct((tok_rows, D), jnp.bfloat16),
        jax.ShapeDtypeStruct((tok_rows, D), jnp.float32),
        jax.ShapeDtypeStruct((sources, 1, height // sources, D), jnp.bfloat16),
    ]
    whole = lambda a: pl.BlockSpec(a.shape, lambda i, rank=len(a.shape): (0,) * rank)
    return pl.pallas_call(
        norm_kernel,
        grid=(1,),
        in_specs=[pl.BlockSpec(memory_space=pl.ANY)] * len(after) + [whole(a) for a in operands],
        out_specs=[whole(a) for a in shapes],
        out_shape=shapes,
        compiler_params=pltpu.CompilerParams(vmem_limit_bytes=40 * 1024 * 1024),
        cost_estimate=pl.CostEstimate(
            flops=2 * height * tok_rows * D + 10 * tok_rows * D,
            bytes_accessed=(16 * tok_rows + 2 * height) * D,
            transcendentals=tok_rows,
        ),
    )(*after, *operands)


def pack_kernel(*refs):
    picking_ref, block_ref, out_ref = refs[-3:]
    out_ref[:, 0] = pack_rows(
        picking_ref[...], block_ref[...], (out_ref.shape[0],) + out_ref.shape[2:]
    )


def pack_after(after, picking, block, sources, into=False):
    height, tok_rows = picking.shape
    parts = 2 if into else 1
    return pl.pallas_call(
        pack_kernel,
        grid=(1,),
        in_specs=[pl.BlockSpec(memory_space=pl.ANY)] * len(after)
        + [
            pl.BlockSpec((height, tok_rows), lambda i: (0, 0)),
            pl.BlockSpec((tok_rows, D), lambda i: (0, 0)),
        ],
        out_specs=pl.BlockSpec((sources, 1, height // sources, D), lambda i: (0, parts - 1, 0, 0)),
        out_shape=jax.ShapeDtypeStruct((sources, parts, height // sources, D), jnp.bfloat16),
        input_output_aliases={0: 0} if into else {},
        compiler_params=pltpu.CompilerParams(vmem_limit_bytes=40 * 1024 * 1024),
        cost_estimate=pl.CostEstimate(
            flops=2 * height * tok_rows * D, bytes_accessed=4 * height * D, transcendentals=0
        ),
    )(*after, picking, block)


def tie_kernel(*refs):
    del refs


def tie(block, *after):
    return pl.pallas_call(
        tie_kernel,
        in_specs=[pl.BlockSpec(memory_space=pl.ANY)] * (1 + len(after)),
        out_specs=pl.BlockSpec(memory_space=pl.ANY),
        out_shape=jax.ShapeDtypeStruct(block.shape, block.dtype),
        input_output_aliases={0: 0},
    )(block, *after)


def expert_kernel(*refs):
    (rows_ref, order_ref, back_ref, gate_ref, up_ref, down_ref) = refs[-10:-4]
    out_ref, sorted_rows, total, outs = refs[-4:]
    step = pl.program_id(0)
    height, depth = sorted_rows.shape
    count = height // 2

    @pl.when(step == 0)
    def _():
        rows = rows_ref[:, 0].astype(jnp.float32).reshape(height, depth).astype(jnp.bfloat16)
        sorted_rows[...] = jnp.dot(
            order_ref[...], rows, preferred_element_type=jnp.float32
        ).astype(jnp.bfloat16)

    first = pl.multiple_of((step // 2) * count, 16)
    tokens = sorted_rows[pl.ds(first, count), :]
    gate_val = jnp.dot(tokens, gate_ref[0], preferred_element_type=jnp.float32)
    up_val = jnp.dot(tokens, up_ref[0], preferred_element_type=jnp.float32)
    activated = (gate_val / (1.0 + jnp.exp(-gate_val)) * up_val).astype(jnp.bfloat16)
    half_out = jnp.dot(activated, down_ref[0], preferred_element_type=jnp.float32)

    @pl.when(step % 2 == 0)
    def _():
        total[...] = half_out

    @pl.when(step % 2 == 1)
    def _():
        outs[pl.ds(first, count), :] = (total[...] + half_out).astype(jnp.bfloat16)

    @pl.when(step == 3)
    def _():
        out_ref[:, 0] = pack_rows(back_ref[...], outs[...], (out_ref.shape[0],) + out_ref.shape[2:])


def run_experts(after, arrived, w_gate, w_up, w_down, out_parts=1):
    sources, parts, slots, depth = arrived.shape
    units = w_gate.shape[2]
    height = sources * slots
    index = np.arange(height)
    wanted = (
        index % (height // 2) // (slots // 2) * slots
        + index // (height // 2) * (slots // 2)
        + index % (slots // 2)
    )
    order = (wanted[:, None] == index[None, :]).astype(np.float32)
    fixed = lambda i: (0, 0)
    return pl.pallas_call(
        expert_kernel,
        grid=(4,),
        in_specs=[pl.BlockSpec(memory_space=pl.ANY)] * len(after)
        + [
            pl.BlockSpec((sources, 1, slots, depth), lambda i: (0, parts - 1, 0, 0)),
            pl.BlockSpec((height, height), fixed),
            pl.BlockSpec((height, height), fixed),
            pl.BlockSpec((1, depth, units), lambda i: (i, 0, 0)),
            pl.BlockSpec((1, depth, units), lambda i: (i, 0, 0)),
            pl.BlockSpec((1, units, depth), lambda i: (i, 0, 0)),
        ],
        out_specs=pl.BlockSpec((sources, 1, slots, depth), lambda i: (0, 0, 0, 0)),
        out_shape=jax.ShapeDtypeStruct((sources, out_parts, slots, depth), jnp.bfloat16),
        scratch_shapes=[
            pltpu.VMEM((height, depth), jnp.bfloat16),
            pltpu.VMEM((height // 2, depth), jnp.float32),
            pltpu.VMEM((height, depth), jnp.bfloat16),
        ],
        compiler_params=pltpu.CompilerParams(vmem_limit_bytes=56 * 1024 * 1024),
        cost_estimate=pl.CostEstimate(
            flops=12 * height * depth * units + 4 * height * height * depth,
            bytes_accessed=12 * depth * units * 2 + 4 * height * depth,
            transcendentals=2 * height * units,
        ),
    )(
        *after,
        arrived,
        jnp.asarray(order, jnp.bfloat16),
        jnp.asarray(order.T, jnp.bfloat16),
        w_gate,
        w_up,
        w_down,
    )


def on_device_whole(
    stream_in,
    queries,
    keys,
    values,
    out_weight,
    norm_gain,
    w_gate,
    w_up,
    w_down,
    combine,
    segment_ids,
    routes,
    page_table,
):
    tok_rows = stream_in.shape[0]
    groups = lax.axis_size("req")
    lanes = lax.axis_size("x")
    sources = groups * lanes
    plane_experts = 2 * sources
    height = plane_experts * MOST
    level = lax.axis_index("z")
    column = lax.axis_index("x")
    swap = [(0, 1), (1, 0)]
    pairs = [[(low, low ^ turn) for low in range(PLANES)] for turn in range(PLANES)]

    core = lax.axis_index("req") % 2
    cores = [(low, low ^ 1) for low in range(groups)]
    half = lax.dynamic_slice_in_dim(out_weight, core * (D // 2), D // 2, 1)
    other_weight = lax.ppermute(half, "x", swap)
    attended = attend_columns(queries, keys, values, segment_ids[0], tok_rows)
    leaving = lax.dynamic_index_in_dim(attended, 1 - column, 0, keepdims=False)
    other = lax.ppermute(tie(leaving, other_weight), "x", swap)
    other_weight = tie(other_weight, attended)
    other_rest = lax.ppermute(other_weight, "req", cores)

    partial = partial_products(
        jnp.stack([column, core]).astype(jnp.int32),
        attended,
        other,
        out_weight,
        other_weight,
        other_rest,
    )

    matched = routes[:, :, None] == jnp.arange(EXPERTS, dtype=jnp.int32)[None, None, :]
    named = jnp.any(matched, axis=1)
    weight_of = jnp.sum(jnp.where(matched, combine[:, :, None], 0.0), axis=1)
    place = jnp.arange(EXPERTS, dtype=jnp.int32)
    in_plane = place // (PLANES * 2 * lanes) * (2 * lanes) + place % (2 * lanes)
    slot_of = jnp.where(named, count_before(named) + (in_plane * MOST)[None, :], -1.0)
    tables = jnp.stack([slot_of.T, weight_of.T])
    tables = tables.reshape(2, groups, PLANES, 2 * lanes, tok_rows)
    tables = jnp.transpose(tables, (2, 0, 1, 3, 4)).reshape(PLANES, 2, plane_experts, tok_rows)
    lines = jnp.arange(height, dtype=jnp.float32)
    received = []
    for turn in range(PLANES):
        table = lax.dynamic_index_in_dim(tables, level ^ turn, 0, keepdims=False)
        received.append(lax.ppermute(table, "z", pairs[turn]) if turn else table)
    partial = tie(partial, *received[1:])
    pickings, mixings = [], []
    for table in received:
        hits = table[0][:, None, :] == lines[None, :, None]
        pickings.append(jnp.sum(hits.astype(jnp.float32), axis=0).astype(jnp.bfloat16))
        mixing = jnp.sum(jnp.where(hits, table[1][:, None, :], 0.0), axis=0)
        high = mixing.astype(jnp.bfloat16)
        mixings.append((high, (mixing - high.astype(jnp.float32)).astype(jnp.bfloat16)))

    gathered = lax.all_to_all(partial, "z", split_axis=0, concat_axis=0, tiled=True)
    kv_cache = move_pages(keys, values, page_table, partial)
    normed, residual, packed = norm_and_pack(
        [kv_cache] + pickings[1:], stream_in, gathered, norm_gain, pickings[0], sources
    )

    def exchange(block):
        return lax.all_to_all(block, ("req", "x"), split_axis=0, concat_axis=0, tiled=True)

    def experts(after, arrived, out_parts=1):
        return run_experts(after, arrived, w_gate, w_up, w_down, out_parts)

    def mixed(turn, returned):
        return sum(
            lax.dot_general(
                part,
                returned[:, 0].reshape(height, D),
                (((0,), (0,)), ((), ())),
                preferred_element_type=jnp.float32,
            )
            for part in mixings[turn]
        )

    def to_plane(turn, block):
        return lax.ppermute(block, "z", pairs[turn])

    blocks = [normed] + [to_plane(turn, normed) for turn in range(1, PLANES)]
    own = exchange(packed)
    packed_first = pack_after([own], pickings[1], blocks[1], sources)
    first = exchange(packed_first)
    outs_own = experts([packed_first], own)
    packed_third = pack_after([first, outs_own], pickings[3], blocks[3], sources)
    third = exchange(packed_third)
    outs_first = experts([packed_third], first, 2)
    outs_first = pack_after([outs_first], pickings[2], blocks[2], sources, into=True)
    second = exchange(outs_first)
    outs_third = experts([outs_first], third)
    back_third = exchange(outs_third)
    share_first = mixed(1, second).astype(jnp.bfloat16)
    outs_second = experts([outs_third, share_first], second)
    got_first = to_plane(1, share_first)
    outs_second = tie(outs_second, got_first)
    back_second = exchange(outs_second)
    share_third = mixed(3, tie(back_third, outs_second)).astype(jnp.bfloat16)
    got_third = to_plane(3, share_third)
    back_own = exchange(tie(outs_own, back_second))
    share_second = mixed(2, tie(back_second, got_third)).astype(jnp.bfloat16)
    got_second = to_plane(2, share_second)
    total = residual + got_first.astype(jnp.float32) + got_third.astype(jnp.float32)
    total = total + mixed(0, back_own) + got_second.astype(jnp.float32)
    return (total.astype(jnp.bfloat16), kv_cache)


def solution(mesh):
    requests, members = mesh.shape["req"], mesh.shape["exp"]
    whole = 2 * EXPERTS == 4 * requests * members and members == 2 * PLANES
    if whole:
        grid = mesh.devices.reshape(requests, PLANES, members // PLANES)
        mesh = Mesh(grid, ("req", "z", "x"))
    exp = ("z", "x") if whole else "exp"
    every = ("req", "z", "x") if whole else ("req", "exp")
    return jax.shard_map(
        on_device_whole if whole else on_device_split,
        mesh=mesh,
        in_specs=(
            P(every, None),
            P("req", exp),
            P("req", exp),
            P("req", exp),
            P(exp, None),
            P(),
            P(every, None, None),
            P(every, None, None),
            P(every, None, None),
            P(every, None),
            P("req", None),
            P(every, None),
            P(),
        ),
        out_specs=(P(every, None), P("req", None, None, exp)),
        check_vma=False,
    )
```

```python
import math

import jax
import jax.numpy as jnp
import numpy as np
from jax import lax
from jax.experimental import pallas as pl
from jax.experimental.pallas import tpu as pltpu
from jax.sharding import Mesh
from jax.sharding import PartitionSpec as P

D = 2048
HD = 128
EXPERTS = 64
TOPK = 8
PAGE = 16
MOST = 20


def from_partner(block, axis, distance):
    count = lax.axis_size(axis)
    route = []
    for low in range(count):
        high = low | 1 << distance
        if high != low and high < count:
            route += [(low, high), (high, low)]
    return lax.ppermute(block, axis, route)


def attend_rows(queries, keys, values, segments):
    length = queries.shape[0]
    head_count = queries.shape[1] // HD
    query_heads = queries.reshape(length, head_count, HD)
    key_heads = keys.reshape(length, head_count, HD)
    value_heads = values.reshape(length, head_count, HD)
    scaling = 1.0 / math.sqrt(HD)
    rows_block = min(512, length)

    def attend_block(position):
        start = position * rows_block
        query_block = lax.dynamic_slice_in_dim(query_heads, start, rows_block, 0)
        segment_block = lax.dynamic_slice_in_dim(segments, start, rows_block, 0)
        scores = (
            jnp.einsum("qhd,khd->hqk", query_block, key_heads, preferred_element_type=jnp.float32)
            * scaling
        )
        allowed = (segment_block[:, None] == segments[None, :])[None, :, :]
        scores = jnp.where(allowed, scores, jnp.float32(-1e30))
        highest = jnp.max(scores, axis=2, keepdims=True)
        weights_exp = jnp.exp(scores - highest)
        totals = jnp.sum(weights_exp, axis=2)
        mixed = jnp.einsum(
            "hqk,khd->qhd",
            weights_exp.astype(jnp.bfloat16),
            value_heads,
            preferred_element_type=jnp.float32,
        )
        mixed = mixed / jnp.transpose(totals)[:, :, None]
        return mixed.astype(jnp.bfloat16)

    blocks = lax.map(attend_block, jnp.arange(length // rows_block))
    return blocks.reshape(length, head_count * HD)


def write_pages(keys, values, page_table):
    page_rows = keys.shape[0] // PAGE
    groups = lax.axis_size("req")
    per_group = page_rows // groups
    width = keys.shape[1]
    pages = jnp.stack(
        [keys.reshape(page_rows, PAGE, width), values.reshape(page_rows, PAGE, width)], axis=1
    )
    myself = lax.axis_index("req")
    whole_table = page_table.reshape(groups, page_rows)
    own_table = lax.dynamic_slice_in_dim(page_table, myself * page_rows, page_rows, 0)
    target = own_table // page_rows
    picked = (target[:, None] == jnp.arange(groups, dtype=jnp.int32)[None, :]).astype(jnp.int32)
    ranking = jnp.sum(jnp.cumsum(picked, axis=0) * picked, axis=1) - 1
    outgoing = jnp.zeros_like(pages).at[target * per_group + ranking].set(pages)
    incoming = lax.all_to_all(
        outgoing.reshape(groups, per_group, 2, PAGE, width),
        "req",
        split_axis=0,
        concat_axis=0,
        tiled=True,
    )
    arriving = whole_table // page_rows == myself
    arrival_rank = jnp.cumsum(arriving.astype(jnp.int32), axis=1) - 1
    placing = jnp.where(
        arriving, jnp.arange(groups, dtype=jnp.int32)[:, None] * per_group + arrival_rank, page_rows
    )
    slot_table = (
        jnp.zeros((page_rows + 1,), jnp.int32)
        .at[placing.reshape(-1)]
        .set((whole_table % page_rows).reshape(-1))
    )
    slot_table = slot_table[:page_rows]
    return jnp.zeros_like(pages).at[slot_table].set(incoming.reshape(page_rows, 2, PAGE, width))


def whole_experts(w_gate, w_up, w_down):
    local_halves = w_gate.shape[0]
    half_units = w_gate.shape[2]
    if local_halves == 1:
        packed = jnp.stack([w_gate[0], w_up[0], w_down[0].reshape(D, half_units)])
        partner = from_partner(packed, "exp", 0)
        leading = lax.axis_index("exp") % 2 == 0
        first = jnp.where(leading, packed, partner)
        second = jnp.where(leading, partner, packed)
        gate_full = jnp.stack([first[0], second[0]])[None]
        up_full = jnp.stack([first[1], second[1]])[None]
        down_full = jnp.stack([first[2].reshape(half_units, D), second[2].reshape(half_units, D)])[
            None
        ]
        return (gate_full, up_full, down_full, 1)
    gate_full = w_gate.reshape(local_halves // 2, 2, D, half_units)
    up_full = w_up.reshape(local_halves // 2, 2, D, half_units)
    down_full = w_down.reshape(local_halves // 2, 2, half_units, D)
    return (gate_full, up_full, down_full, 2)


def on_device_split(
    stream_in,
    queries,
    keys,
    values,
    out_weight,
    norm_gain,
    w_gate,
    w_up,
    w_down,
    combine,
    segment_ids,
    routes,
    page_table,
):
    attended = attend_rows(queries, keys, values, segment_ids[0])
    kv_cache = write_pages(keys, values, page_table)
    tok_rows = stream_in.shape[0]
    projected = lax.psum_scatter(
        jnp.dot(attended, out_weight, preferred_element_type=jnp.float32),
        "exp",
        scatter_dimension=0,
        tiled=True,
    )
    residual = stream_in.astype(jnp.float32) + projected
    scale_rows = lax.rsqrt(jnp.mean(residual * residual, axis=1, keepdims=True) + 1e-06)
    normed = (residual * scale_rows * norm_gain).astype(jnp.bfloat16)
    expert_ids = routes.reshape(-1)
    owners = (expert_ids[:, None] == jnp.arange(EXPERTS, dtype=jnp.int32)[None, :]).astype(
        jnp.int32
    )
    ranking = jnp.sum(jnp.cumsum(owners, axis=0) * owners, axis=1) - 1
    pair_rows = jnp.repeat(normed, TOPK, axis=0)
    devices = lax.axis_size(("req", "exp"))
    local_halves = w_gate.shape[0]
    slots = (MOST + 1) // 2
    holder = 2 * expert_ids + ranking % 2
    position = ranking // 2
    outgoing = jnp.zeros((devices * local_halves * slots, D), jnp.bfloat16)
    outgoing = outgoing.at[holder * slots + position].set(pair_rows)
    gate_full, up_full, down_full, copies = whole_experts(w_gate, w_up, w_down)
    local_experts = gate_full.shape[0]
    arrived = lax.all_to_all(
        outgoing.reshape(devices, local_halves, slots, D),
        ("req", "exp"),
        split_axis=0,
        concat_axis=0,
        tiled=True,
    )
    count = arrived.shape[2]
    grouped = arrived.reshape(devices, local_experts, copies, count, D)
    gate_val = jnp.einsum(
        "sercd,ejdf->serjcf", grouped, gate_full, preferred_element_type=jnp.float32
    )
    up_val = jnp.einsum("sercd,ejdf->serjcf", grouped, up_full, preferred_element_type=jnp.float32)
    activated = (jax.nn.silu(gate_val) * up_val).astype(jnp.bfloat16)
    halves_out = jnp.einsum(
        "serjcf,ejfd->serjcd", activated, down_full, preferred_element_type=jnp.float32
    ).astype(jnp.bfloat16)
    returned = lax.all_to_all(
        halves_out.reshape(devices, local_halves, 2, count, D),
        ("req", "exp"),
        split_axis=0,
        concat_axis=0,
        tiled=True,
    )
    flat_back = returned.reshape(devices * local_halves, 2, slots, D)
    combined = flat_back[holder, 0, position].astype(jnp.float32) + flat_back[
        holder, 1, position
    ].astype(jnp.float32)
    weighted = combined * combine.reshape(-1)[:, None]
    expert_sum = jnp.sum(weighted.reshape(tok_rows, TOPK, D), axis=1)
    layer_out = (residual + expert_sum).astype(jnp.bfloat16)
    return (layer_out, kv_cache)


PLANES = 4


def strictly_lower(size):
    return jnp.asarray(np.tril(np.ones((size, size), np.float32), -1), jnp.bfloat16)


def count_before(flags):
    return jnp.dot(
        strictly_lower(flags.shape[0]),
        flags.astype(jnp.bfloat16),
        preferred_element_type=jnp.float32,
    )


def move_pages(keys, values, page_table, after):
    rows, width = keys.shape
    page_rows = rows // PAGE
    groups = lax.axis_size("req")
    per_group = page_rows // groups
    myself = lax.axis_index("req")
    whole_table = page_table.reshape(groups, page_rows)
    own_table = lax.dynamic_slice_in_dim(page_table, myself * page_rows, page_rows, 0)
    target = own_table // page_rows
    picked = target[:, None] == jnp.arange(groups, dtype=jnp.int32)[None, :]
    ranking = jnp.sum(jnp.where(picked, count_before(picked), 0.0), axis=1).astype(jnp.int32)
    slot = (target ^ myself) * per_group + ranking
    within = jnp.arange(PAGE, dtype=jnp.int32)
    lines = jnp.arange(rows, dtype=jnp.int32)
    target_line = (slot[:, None] * PAGE + within[None, :]).reshape(-1, 128)
    target_line = tie(target_line, after).reshape(-1)
    spread = (target_line[None, :] == lines[:, None]).astype(jnp.bfloat16)
    both = jnp.concatenate([keys, values], axis=1)
    sent = jnp.dot(spread, both, preferred_element_type=jnp.float32).astype(jnp.bfloat16)
    sent = sent.reshape(groups, rows // groups, 2 * width)
    incoming = [sent[0]]
    for apart in range(1, groups):
        pairs = [(low, low ^ apart) for low in range(groups)]
        incoming.append(lax.ppermute(sent[apart], "req", pairs))

    arriving = whole_table // page_rows == myself
    arrival = count_before(arriving.T).T.astype(jnp.int32)
    apart = jnp.arange(groups, dtype=jnp.int32)[:, None] ^ myself
    source = apart * per_group + arrival
    landing = jnp.where(arriving, whole_table % page_rows, -1).reshape(-1)
    slots = jnp.arange(page_rows, dtype=jnp.int32)
    source_page = jnp.sum(
        jnp.where(landing[None, :] == slots[:, None], source.reshape(-1)[None, :], 0), axis=1
    )
    source_line = (source_page[:, None] * PAGE + within[None, :]).reshape(-1)
    collect = (source_line[:, None] == lines[None, :]).astype(jnp.bfloat16)
    placed = jnp.dot(
        collect, jnp.concatenate(incoming, axis=0), preferred_element_type=jnp.float32
    ).astype(jnp.bfloat16)
    placed = placed.reshape(page_rows, PAGE, 2, width)
    return jnp.transpose(placed, (0, 2, 1, 3))


def attend_kernel(query_ref, key_ref, value_ref, line_ref, row_ref, out_ref):
    allowed = line_ref[...] == row_ref[...]
    half = out_ref.shape[1]
    scaling = 1.0 / math.sqrt(HD)
    for head in range(query_ref.shape[1] // HD):
        span = slice(head * HD, (head + 1) * HD)
        scores = lax.dot_general(
            query_ref[:, span],
            key_ref[:, span],
            (((1,), (1,)), ((), ())),
            preferred_element_type=jnp.float32,
        )
        scores = jnp.where(allowed, scores * scaling, jnp.float32(-1e30))
        weights = jnp.exp(scores - jnp.max(scores, axis=1, keepdims=True))
        totals = jnp.sum(weights, axis=1, keepdims=True)
        mixed = jnp.dot(
            weights.astype(jnp.bfloat16), value_ref[:, span], preferred_element_type=jnp.float32
        )
        mixed = (mixed / totals).astype(jnp.bfloat16)
        out_ref[0, :, span] = mixed[:half]
        out_ref[1, :, span] = mixed[half:]


def attend_columns(queries, keys, values, segments, tok_rows):
    rows, width = queries.shape
    block = 2 * tok_rows
    steps = rows // block
    return pl.pallas_call(
        attend_kernel,
        grid=(steps,),
        in_specs=[
            pl.BlockSpec((block, width), lambda i: (i, 0)),
            pl.BlockSpec((rows, width), lambda i: (0, 0)),
            pl.BlockSpec((rows, width), lambda i: (0, 0)),
            pl.BlockSpec((block, 1), lambda i: (i, 0)),
            pl.BlockSpec((1, rows), lambda i: (0, 0)),
        ],
        out_specs=pl.BlockSpec((2, tok_rows, width), lambda i: (0, i, 0)),
        out_shape=jax.ShapeDtypeStruct((2, rows // 2, width), jnp.bfloat16),
        compiler_params=pltpu.CompilerParams(vmem_limit_bytes=40 * 1024 * 1024),
        cost_estimate=pl.CostEstimate(
            flops=4 * rows * rows * width,
            bytes_accessed=8 * rows * width,
            transcendentals=rows * rows * width // HD,
        ),
    )(queries, keys, values, segments.reshape(rows, 1), segments.reshape(1, rows))


def partial_kernel(place_ref, mine_ref, other_ref, weight_ref, first_ref, rest_ref, out_ref, total):
    step = pl.program_id(0)
    total[...] = jnp.dot(mine_ref[0], weight_ref[...], preferred_element_type=jnp.float32)

    @pl.when(step < 2)
    def _():
        total[...] += jnp.dot(other_ref[...], first_ref[...], preferred_element_type=jnp.float32)

    @pl.when(step >= 2)
    def _():
        total[...] += jnp.dot(other_ref[...], rest_ref[...], preferred_element_type=jnp.float32)

    out_ref[...] = total[...].reshape(out_ref.shape).astype(jnp.bfloat16)


def partial_products(place, attended, other, out_weight, other_weight, other_rest):
    _, rows, width = attended.shape
    strip = D // 4
    column_of = lambda i, p: (i // 2 ^ p[1]) * 2 + i % 2
    return pl.pallas_call(
        partial_kernel,
        grid_spec=pltpu.PrefetchScalarGridSpec(
            num_scalar_prefetch=1,
            grid=(4,),
            in_specs=[
                pl.BlockSpec((1, rows, width), lambda i, p: (p[0], 0, 0)),
                pl.BlockSpec((rows, width), lambda i, p: (0, 0)),
                pl.BlockSpec((width, strip), lambda i, p: (0, column_of(i, p))),
                pl.BlockSpec((width, strip), lambda i, p: (0, jnp.minimum(i, 1))),
                pl.BlockSpec((width, strip), lambda i, p: (0, jnp.maximum(i - 2, 0))),
            ],
            out_specs=pl.BlockSpec(
                (PLANES, rows // PLANES, strip), lambda i, p: (0, 0, column_of(i, p))
            ),
            scratch_shapes=[pltpu.VMEM((rows, strip), jnp.float32)],
        ),
        out_shape=jax.ShapeDtypeStruct((PLANES, rows // PLANES, D), jnp.bfloat16),
        compiler_params=pltpu.CompilerParams(vmem_limit_bytes=40 * 1024 * 1024),
        cost_estimate=pl.CostEstimate(
            flops=4 * rows * width * D, bytes_accessed=2 * (rows + 2 * width) * D, transcendentals=0
        ),
    )(place, attended, other, out_weight, other_weight, other_rest)


def pack_rows(picking, block, shape):
    rows = jnp.dot(picking, block, preferred_element_type=jnp.float32)
    return rows.reshape(shape).astype(jnp.bfloat16)


def norm_kernel(*refs):
    stream_ref, parts_ref, gain_ref, picking_ref, normed_ref, residual_ref, packed_ref = refs[-7:]
    residual = stream_ref[...].astype(jnp.float32)
    for plane in range(PLANES):
        residual = residual + parts_ref[plane].astype(jnp.float32)
    residual_ref[...] = residual
    scale = lax.rsqrt(jnp.mean(residual * residual, axis=1, keepdims=True) + 1e-06)
    normed = (residual * scale * gain_ref[...]).astype(jnp.bfloat16)
    normed_ref[...] = normed
    packed_ref[:, 0] = pack_rows(
        picking_ref[...], normed, (packed_ref.shape[0],) + packed_ref.shape[2:]
    )


def norm_and_pack(after, stream_in, parts, norm_gain, picking, sources):
    tok_rows = stream_in.shape[0]
    height = picking.shape[0]
    operands = (stream_in, parts, norm_gain.reshape(1, D), picking)
    shapes = [
        jax.ShapeDtypeStruct((tok_rows, D), jnp.bfloat16),
        jax.ShapeDtypeStruct((tok_rows, D), jnp.float32),
        jax.ShapeDtypeStruct((sources, 1, height // sources, D), jnp.bfloat16),
    ]
    whole = lambda a: pl.BlockSpec(a.shape, lambda i, rank=len(a.shape): (0,) * rank)
    return pl.pallas_call(
        norm_kernel,
        grid=(1,),
        in_specs=[pl.BlockSpec(memory_space=pl.ANY)] * len(after) + [whole(a) for a in operands],
        out_specs=[whole(a) for a in shapes],
        out_shape=shapes,
        compiler_params=pltpu.CompilerParams(vmem_limit_bytes=40 * 1024 * 1024),
        cost_estimate=pl.CostEstimate(
            flops=2 * height * tok_rows * D + 10 * tok_rows * D,
            bytes_accessed=(16 * tok_rows + 2 * height) * D,
            transcendentals=tok_rows,
        ),
    )(*after, *operands)


def pack_kernel(*refs):
    picking_ref, block_ref, out_ref = refs[-3:]
    out_ref[:, 0] = pack_rows(
        picking_ref[...], block_ref[...], (out_ref.shape[0],) + out_ref.shape[2:]
    )


def pack_after(after, picking, block, sources, into=False):
    height, tok_rows = picking.shape
    parts = 2 if into else 1
    return pl.pallas_call(
        pack_kernel,
        grid=(1,),
        in_specs=[pl.BlockSpec(memory_space=pl.ANY)] * len(after)
        + [
            pl.BlockSpec((height, tok_rows), lambda i: (0, 0)),
            pl.BlockSpec((tok_rows, D), lambda i: (0, 0)),
        ],
        out_specs=pl.BlockSpec((sources, 1, height // sources, D), lambda i: (0, parts - 1, 0, 0)),
        out_shape=jax.ShapeDtypeStruct((sources, parts, height // sources, D), jnp.bfloat16),
        input_output_aliases={0: 0} if into else {},
        compiler_params=pltpu.CompilerParams(vmem_limit_bytes=40 * 1024 * 1024),
        cost_estimate=pl.CostEstimate(
            flops=2 * height * tok_rows * D, bytes_accessed=4 * height * D, transcendentals=0
        ),
    )(*after, picking, block)


def tie_kernel(*refs):
    del refs


def tie(block, *after):
    return pl.pallas_call(
        tie_kernel,
        in_specs=[pl.BlockSpec(memory_space=pl.ANY)] * (1 + len(after)),
        out_specs=pl.BlockSpec(memory_space=pl.ANY),
        out_shape=jax.ShapeDtypeStruct(block.shape, block.dtype),
        input_output_aliases={0: 0},
    )(block, *after)


def expert_kernel(*refs):
    (rows_ref, order_ref, back_ref, gate_ref, up_ref, down_ref) = refs[-10:-4]
    out_ref, sorted_rows, total, outs = refs[-4:]
    step = pl.program_id(0)
    height, depth = sorted_rows.shape
    count = height // 2

    @pl.when(step == 0)
    def _():
        rows = rows_ref[:, 0].astype(jnp.float32).reshape(height, depth).astype(jnp.bfloat16)
        sorted_rows[...] = jnp.dot(
            order_ref[...], rows, preferred_element_type=jnp.float32
        ).astype(jnp.bfloat16)

    first = pl.multiple_of((step // 2) * count, 16)
    tokens = sorted_rows[pl.ds(first, count), :]
    gate_val = jnp.dot(tokens, gate_ref[0], preferred_element_type=jnp.float32)
    up_val = jnp.dot(tokens, up_ref[0], preferred_element_type=jnp.float32)
    activated = (gate_val / (1.0 + jnp.exp(-gate_val)) * up_val).astype(jnp.bfloat16)
    half_out = jnp.dot(activated, down_ref[0], preferred_element_type=jnp.float32)

    @pl.when(step % 2 == 0)
    def _():
        total[...] = half_out

    @pl.when(step % 2 == 1)
    def _():
        outs[pl.ds(first, count), :] = (total[...] + half_out).astype(jnp.bfloat16)

    @pl.when(step == 3)
    def _():
        out_ref[:, 0] = pack_rows(back_ref[...], outs[...], (out_ref.shape[0],) + out_ref.shape[2:])


def run_experts(after, arrived, w_gate, w_up, w_down, out_parts=1):
    sources, parts, slots, depth = arrived.shape
    units = w_gate.shape[2]
    height = sources * slots
    index = np.arange(height)
    wanted = (
        index % (height // 2) // (slots // 2) * slots
        + index // (height // 2) * (slots // 2)
        + index % (slots // 2)
    )
    order = (wanted[:, None] == index[None, :]).astype(np.float32)
    fixed = lambda i: (0, 0)
    return pl.pallas_call(
        expert_kernel,
        grid=(4,),
        in_specs=[pl.BlockSpec(memory_space=pl.ANY)] * len(after)
        + [
            pl.BlockSpec((sources, 1, slots, depth), lambda i: (0, parts - 1, 0, 0)),
            pl.BlockSpec((height, height), fixed),
            pl.BlockSpec((height, height), fixed),
            pl.BlockSpec((1, depth, units), lambda i: (i, 0, 0)),
            pl.BlockSpec((1, depth, units), lambda i: (i, 0, 0)),
            pl.BlockSpec((1, units, depth), lambda i: (i, 0, 0)),
        ],
        out_specs=pl.BlockSpec((sources, 1, slots, depth), lambda i: (0, 0, 0, 0)),
        out_shape=jax.ShapeDtypeStruct((sources, out_parts, slots, depth), jnp.bfloat16),
        scratch_shapes=[
            pltpu.VMEM((height, depth), jnp.bfloat16),
            pltpu.VMEM((height // 2, depth), jnp.float32),
            pltpu.VMEM((height, depth), jnp.bfloat16),
        ],
        compiler_params=pltpu.CompilerParams(vmem_limit_bytes=56 * 1024 * 1024),
        cost_estimate=pl.CostEstimate(
            flops=12 * height * depth * units + 4 * height * height * depth,
            bytes_accessed=12 * depth * units * 2 + 4 * height * depth,
            transcendentals=2 * height * units,
        ),
    )(
        *after,
        arrived,
        jnp.asarray(order, jnp.bfloat16),
        jnp.asarray(order.T, jnp.bfloat16),
        w_gate,
        w_up,
        w_down,
    )


def on_device_whole(
    stream_in,
    queries,
    keys,
    values,
    out_weight,
    norm_gain,
    w_gate,
    w_up,
    w_down,
    combine,
    segment_ids,
    routes,
    page_table,
):
    tok_rows = stream_in.shape[0]
    groups = lax.axis_size("req")
    lanes = lax.axis_size("x")
    sources = groups * lanes
    plane_experts = 2 * sources
    height = plane_experts * MOST
    level = lax.axis_index("z")
    column = lax.axis_index("x")
    swap = [(0, 1), (1, 0)]
    pairs = [[(low, low ^ turn) for low in range(PLANES)] for turn in range(PLANES)]

    core = lax.axis_index("req") % 2
    cores = [(low, low ^ 1) for low in range(groups)]
    half = lax.dynamic_slice_in_dim(out_weight, core * (D // 2), D // 2, 1)
    other_weight = lax.ppermute(half, "x", swap)
    attended = attend_columns(queries, keys, values, segment_ids[0], tok_rows)
    leaving = lax.dynamic_index_in_dim(attended, 1 - column, 0, keepdims=False)
    other = lax.ppermute(tie(leaving, other_weight), "x", swap)
    other_weight = tie(other_weight, attended)
    other_rest = lax.ppermute(other_weight, "req", cores)

    partial = partial_products(
        jnp.stack([column, core]).astype(jnp.int32),
        attended,
        other,
        out_weight,
        other_weight,
        other_rest,
    )

    matched = routes[:, :, None] == jnp.arange(EXPERTS, dtype=jnp.int32)[None, None, :]
    named = jnp.any(matched, axis=1)
    weight_of = jnp.sum(jnp.where(matched, combine[:, :, None], 0.0), axis=1)
    place = jnp.arange(EXPERTS, dtype=jnp.int32)
    in_plane = place // (PLANES * 2 * lanes) * (2 * lanes) + place % (2 * lanes)
    slot_of = jnp.where(named, count_before(named) + (in_plane * MOST)[None, :], -1.0)
    tables = jnp.stack([slot_of.T, weight_of.T])
    tables = tables.reshape(2, groups, PLANES, 2 * lanes, tok_rows)
    tables = jnp.transpose(tables, (2, 0, 1, 3, 4)).reshape(PLANES, 2, plane_experts, tok_rows)
    lines = jnp.arange(height, dtype=jnp.float32)
    received = []
    for turn in range(PLANES):
        table = lax.dynamic_index_in_dim(tables, level ^ turn, 0, keepdims=False)
        received.append(lax.ppermute(table, "z", pairs[turn]) if turn else table)
    partial = tie(partial, *received[1:])
    pickings, mixings = [], []
    for table in received:
        hits = table[0][:, None, :] == lines[None, :, None]
        pickings.append(jnp.sum(hits.astype(jnp.float32), axis=0).astype(jnp.bfloat16))
        mixing = jnp.sum(jnp.where(hits, table[1][:, None, :], 0.0), axis=0)
        high = mixing.astype(jnp.bfloat16)
        mixings.append((high, (mixing - high.astype(jnp.float32)).astype(jnp.bfloat16)))

    gathered = lax.all_to_all(partial, "z", split_axis=0, concat_axis=0, tiled=True)
    kv_cache = move_pages(keys, values, page_table, partial)
    normed, residual, packed = norm_and_pack(
        [kv_cache] + pickings[1:], stream_in, gathered, norm_gain, pickings[0], sources
    )

    def exchange(block):
        return lax.all_to_all(block, ("req", "x"), split_axis=0, concat_axis=0, tiled=True)

    def experts(after, arrived, out_parts=1):
        return run_experts(after, arrived, w_gate, w_up, w_down, out_parts)

    def mixed(turn, returned):
        return sum(
            lax.dot_general(
                part,
                returned[:, 0].reshape(height, D),
                (((0,), (0,)), ((), ())),
                preferred_element_type=jnp.float32,
            )
            for part in mixings[turn]
        )

    def to_plane(turn, block):
        return lax.ppermute(block, "z", pairs[turn])

    blocks = [normed] + [to_plane(turn, normed) for turn in range(1, PLANES)]
    own = exchange(packed)
    packed_first = pack_after([own], pickings[1], blocks[1], sources)
    first = exchange(packed_first)
    packed_third = pack_after([first], pickings[3], blocks[3], sources)
    third = exchange(packed_third)
    outs_first = experts([packed_third], first, 2)
    outs_first = pack_after([outs_first], pickings[2], blocks[2], sources, into=True)
    second = exchange(outs_first)
    outs_third = experts([outs_first], third)
    back_third = exchange(outs_third)
    share_first = mixed(1, second).astype(jnp.bfloat16)
    outs_second = experts([outs_third, share_first], second)
    got_first = to_plane(1, share_first)
    outs_second = tie(outs_second, got_first)
    back_second = exchange(outs_second)
    share_third = mixed(3, tie(back_third, outs_second)).astype(jnp.bfloat16)
    outs_own = experts([share_third], own)
    got_third = to_plane(3, share_third)
    outs_own = tie(outs_own, got_third)
    back_own = exchange(outs_own)
    share_second = mixed(2, tie(back_second, outs_own)).astype(jnp.bfloat16)
    got_second = to_plane(2, share_second)
    total = residual + got_first.astype(jnp.float32) + got_third.astype(jnp.float32)
    total = total + mixed(0, back_own) + got_second.astype(jnp.float32)
    return (total.astype(jnp.bfloat16), kv_cache)


def solution(mesh):
    requests, members = mesh.shape["req"], mesh.shape["exp"]
    whole = 2 * EXPERTS == 4 * requests * members and members == 2 * PLANES
    if whole:
        grid = mesh.devices.reshape(requests, PLANES, members // PLANES)
        mesh = Mesh(grid, ("req", "z", "x"))
    exp = ("z", "x") if whole else "exp"
    every = ("req", "z", "x") if whole else ("req", "exp")
    return jax.shard_map(
        on_device_whole if whole else on_device_split,
        mesh=mesh,
        in_specs=(
            P(every, None),
            P("req", exp),
            P("req", exp),
            P("req", exp),
            P(exp, None),
            P(),
            P(every, None, None),
            P(every, None, None),
            P(every, None, None),
            P(every, None),
            P("req", None),
            P(every, None),
            P(),
        ),
        out_specs=(P(every, None), P("req", None, None, exp)),
        check_vma=False,
    )
```

```python
import math

import jax
import jax.numpy as jnp
import numpy as np
from jax import lax
from jax.experimental import pallas as pl
from jax.experimental.pallas import tpu as pltpu
from jax.sharding import Mesh
from jax.sharding import PartitionSpec as P

D = 2048
HD = 128
EXPERTS = 64
TOPK = 8
PAGE = 16
MOST = 20


def from_partner(block, axis, distance):
    count = lax.axis_size(axis)
    route = []
    for low in range(count):
        high = low | 1 << distance
        if high != low and high < count:
            route += [(low, high), (high, low)]
    return lax.ppermute(block, axis, route)


def attend_rows(queries, keys, values, segments):
    length = queries.shape[0]
    head_count = queries.shape[1] // HD
    query_heads = queries.reshape(length, head_count, HD)
    key_heads = keys.reshape(length, head_count, HD)
    value_heads = values.reshape(length, head_count, HD)
    scaling = 1.0 / math.sqrt(HD)
    rows_block = min(512, length)

    def attend_block(position):
        start = position * rows_block
        query_block = lax.dynamic_slice_in_dim(query_heads, start, rows_block, 0)
        segment_block = lax.dynamic_slice_in_dim(segments, start, rows_block, 0)
        scores = (
            jnp.einsum("qhd,khd->hqk", query_block, key_heads, preferred_element_type=jnp.float32)
            * scaling
        )
        allowed = (segment_block[:, None] == segments[None, :])[None, :, :]
        scores = jnp.where(allowed, scores, jnp.float32(-1e30))
        highest = jnp.max(scores, axis=2, keepdims=True)
        weights_exp = jnp.exp(scores - highest)
        totals = jnp.sum(weights_exp, axis=2)
        mixed = jnp.einsum(
            "hqk,khd->qhd",
            weights_exp.astype(jnp.bfloat16),
            value_heads,
            preferred_element_type=jnp.float32,
        )
        mixed = mixed / jnp.transpose(totals)[:, :, None]
        return mixed.astype(jnp.bfloat16)

    blocks = lax.map(attend_block, jnp.arange(length // rows_block))
    return blocks.reshape(length, head_count * HD)


def write_pages(keys, values, page_table):
    page_rows = keys.shape[0] // PAGE
    groups = lax.axis_size("req")
    per_group = page_rows // groups
    width = keys.shape[1]
    pages = jnp.stack(
        [keys.reshape(page_rows, PAGE, width), values.reshape(page_rows, PAGE, width)], axis=1
    )
    myself = lax.axis_index("req")
    whole_table = page_table.reshape(groups, page_rows)
    own_table = lax.dynamic_slice_in_dim(page_table, myself * page_rows, page_rows, 0)
    target = own_table // page_rows
    picked = (target[:, None] == jnp.arange(groups, dtype=jnp.int32)[None, :]).astype(jnp.int32)
    ranking = jnp.sum(jnp.cumsum(picked, axis=0) * picked, axis=1) - 1
    outgoing = jnp.zeros_like(pages).at[target * per_group + ranking].set(pages)
    incoming = lax.all_to_all(
        outgoing.reshape(groups, per_group, 2, PAGE, width),
        "req",
        split_axis=0,
        concat_axis=0,
        tiled=True,
    )
    arriving = whole_table // page_rows == myself
    arrival_rank = jnp.cumsum(arriving.astype(jnp.int32), axis=1) - 1
    placing = jnp.where(
        arriving, jnp.arange(groups, dtype=jnp.int32)[:, None] * per_group + arrival_rank, page_rows
    )
    slot_table = (
        jnp.zeros((page_rows + 1,), jnp.int32)
        .at[placing.reshape(-1)]
        .set((whole_table % page_rows).reshape(-1))
    )
    slot_table = slot_table[:page_rows]
    return jnp.zeros_like(pages).at[slot_table].set(incoming.reshape(page_rows, 2, PAGE, width))


def whole_experts(w_gate, w_up, w_down):
    local_halves = w_gate.shape[0]
    half_units = w_gate.shape[2]
    if local_halves == 1:
        packed = jnp.stack([w_gate[0], w_up[0], w_down[0].reshape(D, half_units)])
        partner = from_partner(packed, "exp", 0)
        leading = lax.axis_index("exp") % 2 == 0
        first = jnp.where(leading, packed, partner)
        second = jnp.where(leading, partner, packed)
        gate_full = jnp.stack([first[0], second[0]])[None]
        up_full = jnp.stack([first[1], second[1]])[None]
        down_full = jnp.stack([first[2].reshape(half_units, D), second[2].reshape(half_units, D)])[
            None
        ]
        return (gate_full, up_full, down_full, 1)
    gate_full = w_gate.reshape(local_halves // 2, 2, D, half_units)
    up_full = w_up.reshape(local_halves // 2, 2, D, half_units)
    down_full = w_down.reshape(local_halves // 2, 2, half_units, D)
    return (gate_full, up_full, down_full, 2)


def on_device_split(
    stream_in,
    queries,
    keys,
    values,
    out_weight,
    norm_gain,
    w_gate,
    w_up,
    w_down,
    combine,
    segment_ids,
    routes,
    page_table,
):
    attended = attend_rows(queries, keys, values, segment_ids[0])
    kv_cache = write_pages(keys, values, page_table)
    tok_rows = stream_in.shape[0]
    projected = lax.psum_scatter(
        jnp.dot(attended, out_weight, preferred_element_type=jnp.float32),
        "exp",
        scatter_dimension=0,
        tiled=True,
    )
    residual = stream_in.astype(jnp.float32) + projected
    scale_rows = lax.rsqrt(jnp.mean(residual * residual, axis=1, keepdims=True) + 1e-06)
    normed = (residual * scale_rows * norm_gain).astype(jnp.bfloat16)
    expert_ids = routes.reshape(-1)
    owners = (expert_ids[:, None] == jnp.arange(EXPERTS, dtype=jnp.int32)[None, :]).astype(
        jnp.int32
    )
    ranking = jnp.sum(jnp.cumsum(owners, axis=0) * owners, axis=1) - 1
    pair_rows = jnp.repeat(normed, TOPK, axis=0)
    devices = lax.axis_size(("req", "exp"))
    local_halves = w_gate.shape[0]
    slots = (MOST + 1) // 2
    holder = 2 * expert_ids + ranking % 2
    position = ranking // 2
    outgoing = jnp.zeros((devices * local_halves * slots, D), jnp.bfloat16)
    outgoing = outgoing.at[holder * slots + position].set(pair_rows)
    gate_full, up_full, down_full, copies = whole_experts(w_gate, w_up, w_down)
    local_experts = gate_full.shape[0]
    arrived = lax.all_to_all(
        outgoing.reshape(devices, local_halves, slots, D),
        ("req", "exp"),
        split_axis=0,
        concat_axis=0,
        tiled=True,
    )
    count = arrived.shape[2]
    grouped = arrived.reshape(devices, local_experts, copies, count, D)
    gate_val = jnp.einsum(
        "sercd,ejdf->serjcf", grouped, gate_full, preferred_element_type=jnp.float32
    )
    up_val = jnp.einsum("sercd,ejdf->serjcf", grouped, up_full, preferred_element_type=jnp.float32)
    activated = (jax.nn.silu(gate_val) * up_val).astype(jnp.bfloat16)
    halves_out = jnp.einsum(
        "serjcf,ejfd->serjcd", activated, down_full, preferred_element_type=jnp.float32
    ).astype(jnp.bfloat16)
    returned = lax.all_to_all(
        halves_out.reshape(devices, local_halves, 2, count, D),
        ("req", "exp"),
        split_axis=0,
        concat_axis=0,
        tiled=True,
    )
    flat_back = returned.reshape(devices * local_halves, 2, slots, D)
    combined = flat_back[holder, 0, position].astype(jnp.float32) + flat_back[
        holder, 1, position
    ].astype(jnp.float32)
    weighted = combined * combine.reshape(-1)[:, None]
    expert_sum = jnp.sum(weighted.reshape(tok_rows, TOPK, D), axis=1)
    layer_out = (residual + expert_sum).astype(jnp.bfloat16)
    return (layer_out, kv_cache)


PLANES = 4


def strictly_lower(size):
    return jnp.asarray(np.tril(np.ones((size, size), np.float32), -1), jnp.bfloat16)


def count_before(flags):
    return jnp.dot(
        strictly_lower(flags.shape[0]),
        flags.astype(jnp.bfloat16),
        preferred_element_type=jnp.float32,
    )


def move_pages(keys, values, page_table, after):
    rows, width = keys.shape
    page_rows = rows // PAGE
    groups = lax.axis_size("req")
    per_group = page_rows // groups
    myself = lax.axis_index("req")
    whole_table = page_table.reshape(groups, page_rows)
    own_table = lax.dynamic_slice_in_dim(page_table, myself * page_rows, page_rows, 0)
    target = own_table // page_rows
    picked = target[:, None] == jnp.arange(groups, dtype=jnp.int32)[None, :]
    ranking = jnp.sum(jnp.where(picked, count_before(picked), 0.0), axis=1).astype(jnp.int32)
    slot = (target ^ myself) * per_group + ranking
    within = jnp.arange(PAGE, dtype=jnp.int32)
    lines = jnp.arange(rows, dtype=jnp.int32)
    target_line = (slot[:, None] * PAGE + within[None, :]).reshape(-1, 128)
    target_line = tie(target_line, after).reshape(-1)
    spread = (target_line[None, :] == lines[:, None]).astype(jnp.bfloat16)
    both = jnp.concatenate([keys, values], axis=1)
    sent = jnp.dot(spread, both, preferred_element_type=jnp.float32).astype(jnp.bfloat16)
    sent = sent.reshape(groups, rows // groups, 2 * width)
    incoming = [sent[0]]
    for apart in range(1, groups):
        pairs = [(low, low ^ apart) for low in range(groups)]
        incoming.append(lax.ppermute(sent[apart], "req", pairs))

    arriving = whole_table // page_rows == myself
    arrival = count_before(arriving.T).T.astype(jnp.int32)
    apart = jnp.arange(groups, dtype=jnp.int32)[:, None] ^ myself
    source = apart * per_group + arrival
    landing = jnp.where(arriving, whole_table % page_rows, -1).reshape(-1)
    slots = jnp.arange(page_rows, dtype=jnp.int32)
    source_page = jnp.sum(
        jnp.where(landing[None, :] == slots[:, None], source.reshape(-1)[None, :], 0), axis=1
    )
    source_line = (source_page[:, None] * PAGE + within[None, :]).reshape(-1)
    collect = (source_line[:, None] == lines[None, :]).astype(jnp.bfloat16)
    placed = jnp.dot(
        collect, jnp.concatenate(incoming, axis=0), preferred_element_type=jnp.float32
    ).astype(jnp.bfloat16)
    placed = placed.reshape(page_rows, PAGE, 2, width)
    return jnp.transpose(placed, (0, 2, 1, 3))


def attend_kernel(query_ref, key_ref, value_ref, line_ref, row_ref, out_ref):
    allowed = line_ref[...] == row_ref[...]
    half = out_ref.shape[1]
    scaling = 1.0 / math.sqrt(HD)
    for head in range(query_ref.shape[1] // HD):
        span = slice(head * HD, (head + 1) * HD)
        scores = lax.dot_general(
            query_ref[:, span],
            key_ref[:, span],
            (((1,), (1,)), ((), ())),
            preferred_element_type=jnp.float32,
        )
        scores = jnp.where(allowed, scores * scaling, jnp.float32(-1e30))
        weights = jnp.exp(scores - jnp.max(scores, axis=1, keepdims=True))
        totals = jnp.sum(weights, axis=1, keepdims=True)
        mixed = jnp.dot(
            weights.astype(jnp.bfloat16), value_ref[:, span], preferred_element_type=jnp.float32
        )
        mixed = (mixed / totals).astype(jnp.bfloat16)
        out_ref[0, :, span] = mixed[:half]
        out_ref[1, :, span] = mixed[half:]


def attend_columns(queries, keys, values, segments, tok_rows):
    rows, width = queries.shape
    block = 2 * tok_rows
    steps = rows // block
    return pl.pallas_call(
        attend_kernel,
        grid=(steps,),
        in_specs=[
            pl.BlockSpec((block, width), lambda i: (i, 0)),
            pl.BlockSpec((rows, width), lambda i: (0, 0)),
            pl.BlockSpec((rows, width), lambda i: (0, 0)),
            pl.BlockSpec((block, 1), lambda i: (i, 0)),
            pl.BlockSpec((1, rows), lambda i: (0, 0)),
        ],
        out_specs=pl.BlockSpec((2, tok_rows, width), lambda i: (0, i, 0)),
        out_shape=jax.ShapeDtypeStruct((2, rows // 2, width), jnp.bfloat16),
        compiler_params=pltpu.CompilerParams(vmem_limit_bytes=40 * 1024 * 1024),
        cost_estimate=pl.CostEstimate(
            flops=4 * rows * rows * width,
            bytes_accessed=8 * rows * width,
            transcendentals=rows * rows * width // HD,
        ),
    )(queries, keys, values, segments.reshape(rows, 1), segments.reshape(1, rows))


def partial_kernel(place_ref, mine_ref, other_ref, weight_ref, first_ref, rest_ref, out_ref, total):
    step = pl.program_id(0)
    total[...] = jnp.dot(mine_ref[0], weight_ref[...], preferred_element_type=jnp.float32)

    @pl.when(step < 2)
    def _():
        total[...] += jnp.dot(other_ref[...], first_ref[...], preferred_element_type=jnp.float32)

    @pl.when(step >= 2)
    def _():
        total[...] += jnp.dot(other_ref[...], rest_ref[...], preferred_element_type=jnp.float32)

    out_ref[...] = total[...].reshape(out_ref.shape).astype(jnp.bfloat16)


def partial_products(place, attended, other, out_weight, other_weight, other_rest):
    _, rows, width = attended.shape
    strip = D // 4
    column_of = lambda i, p: (i // 2 ^ p[1]) * 2 + i % 2
    return pl.pallas_call(
        partial_kernel,
        grid_spec=pltpu.PrefetchScalarGridSpec(
            num_scalar_prefetch=1,
            grid=(4,),
            in_specs=[
                pl.BlockSpec((1, rows, width), lambda i, p: (p[0], 0, 0)),
                pl.BlockSpec((rows, width), lambda i, p: (0, 0)),
                pl.BlockSpec((width, strip), lambda i, p: (0, column_of(i, p))),
                pl.BlockSpec((width, strip), lambda i, p: (0, jnp.minimum(i, 1))),
                pl.BlockSpec((width, strip), lambda i, p: (0, jnp.maximum(i - 2, 0))),
            ],
            out_specs=pl.BlockSpec(
                (PLANES, rows // PLANES, strip), lambda i, p: (0, 0, column_of(i, p))
            ),
            scratch_shapes=[pltpu.VMEM((rows, strip), jnp.float32)],
        ),
        out_shape=jax.ShapeDtypeStruct((PLANES, rows // PLANES, D), jnp.bfloat16),
        compiler_params=pltpu.CompilerParams(vmem_limit_bytes=40 * 1024 * 1024),
        cost_estimate=pl.CostEstimate(
            flops=4 * rows * width * D, bytes_accessed=2 * (rows + 2 * width) * D, transcendentals=0
        ),
    )(place, attended, other, out_weight, other_weight, other_rest)


def pack_rows(picking, block, shape):
    rows = jnp.dot(picking, block, preferred_element_type=jnp.float32)
    return rows.reshape(shape).astype(jnp.bfloat16)


def norm_kernel(*refs):
    stream_ref, parts_ref, gain_ref, picking_ref, normed_ref, residual_ref, packed_ref = refs[-7:]
    residual = stream_ref[...].astype(jnp.float32)
    for plane in range(PLANES):
        residual = residual + parts_ref[plane].astype(jnp.float32)
    residual_ref[...] = residual
    scale = lax.rsqrt(jnp.mean(residual * residual, axis=1, keepdims=True) + 1e-06)
    normed = (residual * scale * gain_ref[...]).astype(jnp.bfloat16)
    normed_ref[...] = normed
    packed_ref[:, 0] = pack_rows(
        picking_ref[...], normed, (packed_ref.shape[0],) + packed_ref.shape[2:]
    )


def norm_and_pack(after, stream_in, parts, norm_gain, picking, sources):
    tok_rows = stream_in.shape[0]
    height = picking.shape[0]
    operands = (stream_in, parts, norm_gain.reshape(1, D), picking)
    shapes = [
        jax.ShapeDtypeStruct((tok_rows, D), jnp.bfloat16),
        jax.ShapeDtypeStruct((tok_rows, D), jnp.float32),
        jax.ShapeDtypeStruct((sources, 1, height // sources, D), jnp.bfloat16),
    ]
    whole = lambda a: pl.BlockSpec(a.shape, lambda i, rank=len(a.shape): (0,) * rank)
    return pl.pallas_call(
        norm_kernel,
        grid=(1,),
        in_specs=[pl.BlockSpec(memory_space=pl.ANY)] * len(after) + [whole(a) for a in operands],
        out_specs=[whole(a) for a in shapes],
        out_shape=shapes,
        compiler_params=pltpu.CompilerParams(vmem_limit_bytes=56 * 1024 * 1024),
        cost_estimate=pl.CostEstimate(
            flops=2 * height * tok_rows * D + 10 * tok_rows * D,
            bytes_accessed=(16 * tok_rows + 2 * height) * D,
            transcendentals=tok_rows,
        ),
    )(*after, *operands)


def pack_kernel(*refs):
    picking_ref, block_ref, out_ref = refs[-3:]
    out_ref[:, 0] = pack_rows(
        picking_ref[...], block_ref[...], (out_ref.shape[0],) + out_ref.shape[2:]
    )


def pack_after(after, picking, block, sources, into=False):
    height, tok_rows = picking.shape
    parts = 2 if into else 1
    return pl.pallas_call(
        pack_kernel,
        grid=(1,),
        in_specs=[pl.BlockSpec(memory_space=pl.ANY)] * len(after)
        + [
            pl.BlockSpec((height, tok_rows), lambda i: (0, 0)),
            pl.BlockSpec((tok_rows, D), lambda i: (0, 0)),
        ],
        out_specs=pl.BlockSpec((sources, 1, height // sources, D), lambda i: (0, parts - 1, 0, 0)),
        out_shape=jax.ShapeDtypeStruct((sources, parts, height // sources, D), jnp.bfloat16),
        input_output_aliases={0: 0} if into else {},
        compiler_params=pltpu.CompilerParams(vmem_limit_bytes=56 * 1024 * 1024),
        cost_estimate=pl.CostEstimate(
            flops=2 * height * tok_rows * D, bytes_accessed=4 * height * D, transcendentals=0
        ),
    )(*after, picking, block)


def tie_kernel(*refs):
    del refs


def tie(block, *after):
    return pl.pallas_call(
        tie_kernel,
        in_specs=[pl.BlockSpec(memory_space=pl.ANY)] * (1 + len(after)),
        out_specs=pl.BlockSpec(memory_space=pl.ANY),
        out_shape=jax.ShapeDtypeStruct(block.shape, block.dtype),
        input_output_aliases={0: 0},
    )(block, *after)


def expert_kernel(*refs):
    (rows_ref, order_ref, back_ref, gate_ref, up_ref, down_ref) = refs[-10:-4]
    out_ref, sorted_rows, total, outs = refs[-4:]
    step = pl.program_id(0)
    height, depth = sorted_rows.shape
    count = height // 2

    @pl.when(step == 0)
    def _():
        rows = rows_ref[:, 0].astype(jnp.float32).reshape(height, depth).astype(jnp.bfloat16)
        sorted_rows[...] = jnp.dot(
            order_ref[...], rows, preferred_element_type=jnp.float32
        ).astype(jnp.bfloat16)

    first = pl.multiple_of((step // 2) * count, 16)
    tokens = sorted_rows[pl.ds(first, count), :]
    gate_val = jnp.dot(tokens, gate_ref[0], preferred_element_type=jnp.float32)
    up_val = jnp.dot(tokens, up_ref[0], preferred_element_type=jnp.float32)
    activated = (gate_val / (1.0 + jnp.exp(-gate_val)) * up_val).astype(jnp.bfloat16)
    half_out = jnp.dot(activated, down_ref[0], preferred_element_type=jnp.float32)

    @pl.when(step % 2 == 0)
    def _():
        total[...] = half_out

    @pl.when(step % 2 == 1)
    def _():
        outs[pl.ds(first, count), :] = (total[...] + half_out).astype(jnp.bfloat16)

    @pl.when(step == 3)
    def _():
        out_ref[:, 0] = pack_rows(back_ref[...], outs[...], (out_ref.shape[0],) + out_ref.shape[2:])


def run_experts(after, arrived, w_gate, w_up, w_down, out_parts=1):
    sources, parts, slots, depth = arrived.shape
    units = w_gate.shape[2]
    height = sources * slots
    index = np.arange(height)
    wanted = (
        index % (height // 2) // (slots // 2) * slots
        + index // (height // 2) * (slots // 2)
        + index % (slots // 2)
    )
    order = (wanted[:, None] == index[None, :]).astype(np.float32)
    fixed = lambda i: (0, 0)
    return pl.pallas_call(
        expert_kernel,
        grid=(4,),
        in_specs=[pl.BlockSpec(memory_space=pl.ANY)] * len(after)
        + [
            pl.BlockSpec((sources, 1, slots, depth), lambda i: (0, parts - 1, 0, 0)),
            pl.BlockSpec((height, height), fixed),
            pl.BlockSpec((height, height), fixed),
            pl.BlockSpec((1, depth, units), lambda i: (i, 0, 0)),
            pl.BlockSpec((1, depth, units), lambda i: (i, 0, 0)),
            pl.BlockSpec((1, units, depth), lambda i: (i, 0, 0)),
        ],
        out_specs=pl.BlockSpec((sources, 1, slots, depth), lambda i: (0, 0, 0, 0)),
        out_shape=jax.ShapeDtypeStruct((sources, out_parts, slots, depth), jnp.bfloat16),
        scratch_shapes=[
            pltpu.VMEM((height, depth), jnp.bfloat16),
            pltpu.VMEM((height // 2, depth), jnp.float32),
            pltpu.VMEM((height, depth), jnp.bfloat16),
        ],
        compiler_params=pltpu.CompilerParams(vmem_limit_bytes=56 * 1024 * 1024),
        cost_estimate=pl.CostEstimate(
            flops=12 * height * depth * units + 4 * height * height * depth,
            bytes_accessed=12 * depth * units * 2 + 4 * height * depth,
            transcendentals=2 * height * units,
        ),
    )(
        *after,
        arrived,
        jnp.asarray(order, jnp.bfloat16),
        jnp.asarray(order.T, jnp.bfloat16),
        w_gate,
        w_up,
        w_down,
    )


def on_device_whole(
    stream_in,
    queries,
    keys,
    values,
    out_weight,
    norm_gain,
    w_gate,
    w_up,
    w_down,
    combine,
    segment_ids,
    routes,
    page_table,
):
    tok_rows = stream_in.shape[0]
    groups = lax.axis_size("req")
    lanes = lax.axis_size("x")
    sources = groups * lanes
    plane_experts = 2 * sources
    height = plane_experts * MOST
    level = lax.axis_index("z")
    column = lax.axis_index("x")
    swap = [(0, 1), (1, 0)]
    pairs = [[(low, low ^ turn) for low in range(PLANES)] for turn in range(PLANES)]

    core = lax.axis_index("req") % 2
    cores = [(low, low ^ 1) for low in range(groups)]
    half = lax.dynamic_slice_in_dim(out_weight, core * (D // 2), D // 2, 1)
    other_weight = lax.ppermute(half, "x", swap)
    attended = attend_columns(queries, keys, values, segment_ids[0], tok_rows)
    leaving = lax.dynamic_index_in_dim(attended, 1 - column, 0, keepdims=False)
    other = lax.ppermute(tie(leaving, other_weight), "x", swap)
    other_weight = tie(other_weight, attended)
    other_rest = lax.ppermute(other_weight, "req", cores)

    partial = partial_products(
        jnp.stack([column, core]).astype(jnp.int32),
        attended,
        other,
        out_weight,
        other_weight,
        other_rest,
    )

    matched = routes[:, :, None] == jnp.arange(EXPERTS, dtype=jnp.int32)[None, None, :]
    named = jnp.any(matched, axis=1)
    weight_of = jnp.sum(jnp.where(matched, combine[:, :, None], 0.0), axis=1)
    place = jnp.arange(EXPERTS, dtype=jnp.int32)
    in_plane = place // (PLANES * 2 * lanes) * (2 * lanes) + place % (2 * lanes)
    slot_of = jnp.where(named, count_before(named) + (in_plane * MOST)[None, :], -1.0)
    tables = jnp.stack([slot_of.T, weight_of.T])
    tables = tables.reshape(2, groups, PLANES, 2 * lanes, tok_rows)
    tables = jnp.transpose(tables, (2, 0, 1, 3, 4)).reshape(PLANES, 2, plane_experts, tok_rows)
    lines = jnp.arange(height, dtype=jnp.float32)
    received = []
    for turn in range(PLANES):
        table = lax.dynamic_index_in_dim(tables, level ^ turn, 0, keepdims=False)
        received.append(lax.ppermute(table, "z", pairs[turn]) if turn else table)
    partial = tie(partial, *received[1:])
    pickings, mixings = [], []
    for table in received:
        hits = table[0][:, None, :] == lines[None, :, None]
        pickings.append(jnp.sum(hits.astype(jnp.float32), axis=0).astype(jnp.bfloat16))
        mixing = jnp.sum(jnp.where(hits, table[1][:, None, :], 0.0), axis=0)
        high = mixing.astype(jnp.bfloat16)
        mixings.append((high, (mixing - high.astype(jnp.float32)).astype(jnp.bfloat16)))

    gathered = lax.all_to_all(partial, "z", split_axis=0, concat_axis=0, tiled=True)
    kv_cache = move_pages(keys, values, page_table, partial)
    normed, residual, packed = norm_and_pack(
        [kv_cache] + pickings[1:], stream_in, gathered, norm_gain, pickings[0], sources
    )

    def exchange(block):
        return lax.all_to_all(block, ("req", "x"), split_axis=0, concat_axis=0, tiled=True)

    def experts(after, arrived, out_parts=1):
        return run_experts(after, arrived, w_gate, w_up, w_down, out_parts)

    def mixed(turn, returned):
        return sum(
            lax.dot_general(
                part,
                returned[:, 0].reshape(height, D),
                (((0,), (0,)), ((), ())),
                preferred_element_type=jnp.float32,
            )
            for part in mixings[turn]
        )

    def to_plane(turn, block):
        return lax.ppermute(block, "z", pairs[turn])

    blocks = [normed] + [to_plane(turn, normed) for turn in range(1, PLANES)]
    own = exchange(packed)
    packed_first = pack_after([own], pickings[1], blocks[1], sources)
    first = exchange(packed_first)
    packed_third = pack_after([first], pickings[3], blocks[3], sources)
    third = exchange(packed_third)
    outs_first = experts([packed_third], first, 2)
    outs_first = pack_after([outs_first], pickings[2], blocks[2], sources, into=True)
    second = exchange(outs_first)
    outs_third = experts([outs_first], third)
    back_third = exchange(outs_third)
    share_first = mixed(1, second).astype(jnp.bfloat16)
    outs_second = experts([outs_third, share_first], second)
    got_first = to_plane(1, share_first)
    outs_second = tie(outs_second, got_first)
    back_second = exchange(outs_second)
    share_third = mixed(3, tie(back_third, outs_second)).astype(jnp.bfloat16)
    outs_own = experts([share_third], own)
    got_third = to_plane(3, share_third)
    outs_own = tie(outs_own, got_third)
    back_own = exchange(outs_own)
    share_second = mixed(2, tie(back_second, outs_own)).astype(jnp.bfloat16)
    got_second = to_plane(2, share_second)
    total = residual + got_first.astype(jnp.float32) + got_third.astype(jnp.float32)
    total = total + mixed(0, back_own) + got_second.astype(jnp.float32)
    return (total.astype(jnp.bfloat16), kv_cache)


def solution(mesh):
    requests, members = mesh.shape["req"], mesh.shape["exp"]
    whole = 2 * EXPERTS == 4 * requests * members and members == 2 * PLANES
    if whole:
        grid = mesh.devices.reshape(requests, PLANES, members // PLANES)
        mesh = Mesh(grid, ("req", "z", "x"))
    exp = ("z", "x") if whole else "exp"
    every = ("req", "z", "x") if whole else ("req", "exp")
    return jax.shard_map(
        on_device_whole if whole else on_device_split,
        mesh=mesh,
        in_specs=(
            P(every, None),
            P("req", exp),
            P("req", exp),
            P("req", exp),
            P(exp, None),
            P(),
            P(every, None, None),
            P(every, None, None),
            P(every, None, None),
            P(every, None),
            P("req", None),
            P(every, None),
            P(),
        ),
        out_specs=(P(every, None), P("req", None, None, exp)),
        check_vma=False,
    )
```
